32 devices in a mesh: row: 8 (over z, y), col: 4 (over x, core).
Axes of the slice: x: 2, y: 2, z: 4, core: 2. Of those that a mesh axis runs over, the one named last changes fastest.
Arguments:
- rhs_leaf: bfloat16 [32, 2048, 128], P(('row', 'col')), may hold values from -6 to 6
- rhs_sep: bfloat16 [2048, 128], P('col'), may hold values from -6 to 6
- leaf_sizes: int32 [32], P(('row', 'col')), may hold values from 512 to 2048, as said below
- off_blocks: int32 [32, 4], P(('row', 'col')), may hold values from 0 to 15, as said below
- linv_leaf: bfloat16 [32, 2048, 2048], P(('row', 'col')), as said below
- uinv_leaf: bfloat16 [32, 2048, 2048], P(('row', 'col')), as said below
- l_off: bfloat16 [32, 512, 2048], P(('row', 'col')), may hold values from -0.046875 to 0.046875
- u_off: bfloat16 [32, 2048, 512], P(('row', 'col')), may hold values from -0.25 to 0.25
- linv_sep: bfloat16 [2048, 2048], P('row', 'col'), as said below
- uinv_sep: bfloat16 [2048, 2048], P('row', 'col'), as said below
Outputs:
- solved_leaf: bfloat16 [32, 2048, 128], P(('row', 'col'))
- solved_sep: bfloat16 [2048, 128], P('row')
The draws below stay inside these ranges and needn't reach their ends.
Inputs may be any that keep to these rules, and one draw needn't show every extreme that they name: `leaf_sizes`: between 512 and 2048; the first leaf has exactly 2048. `off_blocks`: the 4 blocks of each leaf are different. `linv_leaf`: lower triangular, diagonal between 0.5 and 1.5. `uinv_leaf`: upper triangular, diagonal between 0.5 and 1.5. `linv_sep`: lower triangular, diagonal between 0.5 and 1.5. `uinv_sep`: upper triangular, diagonal between 0.5 and 1.5.
All inputs are finite; a program needn't handle non-finite values.
Results may differ from the reference program's by a relative error of at most 0.013.
Values may be sent and summed in bfloat16 or wider, within the bound.
No kernel may reach another device: no remote copies, remote signals or barrier semaphores. Data moves between devices by JAX's collectives and lax.ppermute only.
A program may use at most 64 MiB of HBM per device.

```python
import jax
import jax.numpy as jnp
from jax import lax

W = 2048
S = 2048
NRHS = 128
BLK = 128
KB = 4
NLEAF = 32
SB = 16


def shape_triangle(noise, diagonal_values, lower_side):
    order = noise.shape[-1]
    row_ids = jnp.arange(order)[:, None]
    col_ids = jnp.arange(order)[None, :]
    if lower_side:
        strict = col_ids < row_ids
    else:
        strict = col_ids > row_ids
    spread = order ** (-0.5)
    values = jnp.where(strict, noise * spread, 0.0)
    values = jnp.where(row_ids == col_ids, diagonal_values, values)
    return values.astype(jnp.float32)


def triangle_draw(key, dims_shape, lower_side):
    first_key, second_key = jax.random.split(key)
    noise = jax.random.normal(first_key, dims_shape, jnp.float32)
    diagonal_values = jax.random.uniform(second_key, dims_shape[:-1] + (1,), jnp.float32, 0.5, 1.5)
    return shape_triangle(noise, diagonal_values, lower_side)


def draw_leaf_sizes(key, part):
    key = jax.random.fold_in(key, 1)
    values = jax.random.randint(key, (NLEAF,), W // 4, W + 1, jnp.int32)
    return values.at[0].set(W)


def draw_off_blocks(key, part):
    key = jax.random.fold_in(key, 2)
    leaf_keys = jax.random.split(key, NLEAF)
    orders = jax.vmap(lambda one_key: jax.random.permutation(one_key, SB))(leaf_keys)
    return orders[:, :KB].astype(jnp.int32)


def draw_linv_leaf(key, part):
    key = jax.random.fold_in(key, 3)
    return triangle_draw(key, (NLEAF, W, W), True).astype(jnp.bfloat16)


def draw_uinv_leaf(key, part):
    key = jax.random.fold_in(key, 4)
    return triangle_draw(key, (NLEAF, W, W), False).astype(jnp.bfloat16)


def draw_linv_sep(key, part):
    key = jax.random.fold_in(key, 5)
    return triangle_draw(key, (S, S), True).astype(jnp.bfloat16)


def draw_uinv_sep(key, part):
    key = jax.random.fold_in(key, 6)
    return triangle_draw(key, (S, S), False).astype(jnp.bfloat16)


def block_scale(rng, shape, cuts, least, high):
    gain, own = 1.0, jax.random.fold_in(rng, 6)
    for axis_at, blocks in cuts:
        steps = jnp.exp(jax.random.uniform(jax.random.fold_in(own, axis_at), (blocks,), jnp.float32, least / len(cuts), high / len(cuts)))
        gain = gain * jnp.repeat(steps, shape[axis_at] // blocks).reshape([-1 if axis == axis_at else 1 for axis in range(len(shape))])
    return gain


def bell_draw(own_key, shape, scale, limit, shards=(), kind=jnp.bfloat16):
    factor_of = block_scale(own_key, shape, shards, -0.22, 0.18) if shards else 1.0
    values = jax.random.normal(own_key, shape, jnp.float32) * scale * factor_of
    return jnp.minimum(jnp.maximum(values, -limit), limit).astype(kind)


def setup_inputs(seed: int = 0) -> dict:
    arg_keys = jax.random.split(jax.random.key(seed), 11)
    rhs_leaf = bell_draw(arg_keys[0], (NLEAF, W, NRHS), 1.0, 6.0, ((0, 32),))
    rhs_sep = bell_draw(arg_keys[1], (S, NRHS), 1.0, 6.0, ((0, 4),))
    leaf_sizes = draw_leaf_sizes(jax.random.fold_in(arg_keys[10], 71), 0)
    off_blocks = draw_off_blocks(jax.random.fold_in(arg_keys[10], 71), 0)
    linv_leaf = draw_linv_leaf(jax.random.fold_in(arg_keys[10], 71), 0)
    uinv_leaf = draw_uinv_leaf(jax.random.fold_in(arg_keys[10], 71), 0)
    l_off = bell_draw(arg_keys[6], (NLEAF, KB * BLK, W), (W * NLEAF * KB // SB) ** -0.5, 0.046875, ((0, 32),))
    u_off = bell_draw(arg_keys[7], (NLEAF, W, KB * BLK), (KB * BLK) ** -0.5, 0.25, ((0, 32),))
    linv_sep = draw_linv_sep(jax.random.fold_in(arg_keys[10], 71), 0)
    uinv_sep = draw_uinv_sep(jax.random.fold_in(arg_keys[10], 71), 0)
    return dict(rhs_leaf=rhs_leaf, rhs_sep=rhs_sep, leaf_sizes=leaf_sizes, off_blocks=off_blocks, linv_leaf=linv_leaf, uinv_leaf=uinv_leaf, l_off=l_off, u_off=u_off, linv_sep=linv_sep, uinv_sep=uinv_sep)


def reference(rhs_leaf, rhs_sep, leaf_sizes, off_blocks, linv_leaf, uinv_leaf, l_off, u_off, linv_sep, uinv_sep):
    positions = jnp.arange(W, dtype=jnp.int32)

    def forward_leaf(carry, items):
        rhs_one, size_one, blocks_one, linv_one, loff_one = items
        keep_rows = (positions < size_one)[:, None]
        masked = jnp.where(keep_rows, rhs_one, jnp.zeros_like(rhs_one))
        forward = jnp.dot(linv_one, masked, preferred_element_type=jnp.float32)
        forward = jnp.where(keep_rows, forward, 0.0).astype(jnp.bfloat16)
        updates = jnp.dot(loff_one, forward, preferred_element_type=jnp.float32)
        carry = carry.at[blocks_one].add(updates.reshape(KB, BLK, NRHS))
        return carry, forward

    start_sum = jnp.zeros((SB, BLK, NRHS), jnp.float32)
    coupled_sum, forward_all = lax.scan(forward_leaf, start_sum, (rhs_leaf, leaf_sizes, off_blocks, linv_leaf, l_off))
    sep_rhs = (rhs_sep.astype(jnp.float32) - coupled_sum.reshape(S, NRHS)).astype(jnp.bfloat16)
    sep_forward = jnp.dot(linv_sep, sep_rhs, preferred_element_type=jnp.float32).astype(jnp.bfloat16)
    solved_sep = jnp.dot(uinv_sep, sep_forward, preferred_element_type=jnp.float32).astype(jnp.bfloat16)
    sep_blocks = solved_sep.reshape(SB, BLK, NRHS)

    def backward_leaf(items):
        forward, size_one, blocks_one, uinv_one, uoff_one = items
        keep_rows = (positions < size_one)[:, None]
        coupled = sep_blocks[blocks_one].reshape(KB * BLK, NRHS)
        residue = forward.astype(jnp.float32) - jnp.dot(uoff_one, coupled, preferred_element_type=jnp.float32)
        residue = jnp.where(keep_rows, residue, 0.0).astype(jnp.bfloat16)
        solved = jnp.dot(uinv_one, residue, preferred_element_type=jnp.float32)
        return jnp.where(keep_rows, solved, 0.0).astype(jnp.bfloat16)

    solved_leaf = lax.map(backward_leaf, (forward_all, leaf_sizes, off_blocks, uinv_leaf, u_off))
    return solved_leaf, solved_sep
```

```python
import functools

import jax
import jax.numpy as jnp
from jax import lax
from jax.sharding import PartitionSpec as P

BLK = 128
KB = 4


def pieces_to_owners(parts, axis, size):
    me = lax.axis_index(axis)

    def part(k):
        return lax.dynamic_index_in_dim(parts, lax.rem(me + k, size), 0, keepdims=False)

    total = part(0).astype(jnp.float32)
    arrived = []
    for k in range(1, size):
        arrived.append(lax.ppermute(part(k), axis, [(i, (i + k) % size) for i in range(size)]))
    for one in arrived:
        total = total + one.astype(jnp.float32)
    return total


def pieces_to_all(piece, axis, size):
    me = lax.axis_index(axis)
    arrived = [piece]
    for k in range(1, size):
        arrived.append(lax.ppermute(piece, axis, [((i + k) % size, i) for i in range(size)]))
    out = jnp.zeros((size,) + piece.shape, piece.dtype)
    for k in range(size):
        out = lax.dynamic_update_index_in_dim(out, arrived[k], lax.rem(me + k, size), 0)
    return out


def sum_of_all(term, axis, size):
    total = term.astype(jnp.float32)
    sent = term.astype(jnp.bfloat16)
    arrived = []
    for k in range(1, size):
        arrived.append(lax.ppermute(sent, axis, [(i, (i + k) % size) for i in range(size)]))
    for one in arrived:
        total = total + one.astype(jnp.float32)
    return total


def shards(
    rows_n,
    cols_n,
    rhs_leaf,
    rhs_sep,
    leaf_sizes,
    off_blocks,
    linv_leaf,
    uinv_leaf,
    l_off,
    u_off,
    linv_sep,
    uinv_sep,
):
    width, columns = rhs_leaf.shape[1:]
    share = rhs_sep.shape[0]
    sep = share * cols_n
    blocks = sep // BLK
    block_r = sep // rows_n
    piece = share // rows_n
    ratio = rows_n // cols_n
    row = lax.axis_index("row")
    col = lax.axis_index("col")

    halves = uinv_sep.reshape(block_r, ratio, block_r)
    moved = []
    for p in range(ratio):
        pick = lax.rem(row + p, ratio)
        one = lax.dynamic_index_in_dim(halves, pick, 1, keepdims=False)
        pairs = []
        for r in range(rows_n):
            for c in range(cols_n):
                to_r, to_c = ratio * c + (r + p) % ratio, r // ratio
                pairs.append((r * cols_n + c, to_r * cols_n + to_c))
        moved.append(lax.ppermute(one, ("row", "col"), pairs))
    moved = jnp.stack(moved)
    order = lax.rem(row + 2 * ratio - jnp.arange(ratio), ratio)
    uinv_turned = jnp.zeros_like(moved)
    for p in range(ratio):
        uinv_turned = lax.dynamic_update_index_in_dim(uinv_turned, moved[p], order[p], 0)
    uinv_turned = uinv_turned.reshape(share, block_r)

    size = leaf_sizes[0]
    keep = (jnp.arange(width, dtype=jnp.int32) < size)[:, None]
    masked = jnp.where(keep, rhs_leaf[0], jnp.zeros_like(rhs_leaf[0]))
    forward = jnp.dot(linv_leaf[0], masked, preferred_element_type=jnp.float32)
    forward = jnp.where(keep, forward, 0.0).astype(jnp.bfloat16)
    updates = jnp.dot(l_off[0], forward, preferred_element_type=jnp.float32).astype(jnp.bfloat16)
    updates = updates.reshape(KB, BLK, columns)
    named = off_blocks[0][None, :] == jnp.arange(blocks, dtype=jnp.int32)[:, None]
    dense = jnp.zeros((blocks, BLK, columns), jnp.bfloat16)
    for k in range(KB):
        dense = jnp.where(named[:, k][:, None, None], updates[k][None], dense)

    shared = lax.all_to_all(dense.reshape(cols_n, share, columns), "col", 0, 0)
    mine = jnp.sum(shared.astype(jnp.float32), 0).astype(jnp.bfloat16)
    mine = pieces_to_owners(mine.reshape(rows_n, piece, columns), "row", rows_n)
    rhs_piece = lax.dynamic_slice_in_dim(rhs_sep, row * piece, piece, 0)
    rhs_piece = (rhs_piece.astype(jnp.float32) - mine).astype(jnp.bfloat16)
    sep_rhs = pieces_to_all(rhs_piece, "row", rows_n).reshape(share, columns)

    terms = jnp.dot(linv_sep, sep_rhs, preferred_element_type=jnp.float32)
    sep_forward = sum_of_all(terms, "col", cols_n).astype(jnp.bfloat16)
    terms = jnp.dot(uinv_turned, sep_forward, preferred_element_type=jnp.float32)
    terms = terms.astype(jnp.bfloat16).reshape(rows_n, piece, columns)
    terms = lax.all_to_all(terms, "row", 0, 0)
    solved_piece = jnp.sum(terms.astype(jnp.float32), 0).astype(jnp.bfloat16)
    solved_share = pieces_to_all(solved_piece, "row", rows_n).reshape(share, columns)
    solved_sep = pieces_to_all(solved_share, "col", cols_n).reshape(sep, columns)
    solved_rows = lax.dynamic_slice_in_dim(solved_sep, row * block_r, block_r, 0)

    coupled = solved_sep.reshape(blocks, BLK, columns)[off_blocks[0]].reshape(KB * BLK, columns)
    residue = forward.astype(jnp.float32) - jnp.dot(
        u_off[0], coupled, preferred_element_type=jnp.float32
    )
    residue = jnp.where(keep, residue, 0.0).astype(jnp.bfloat16)
    solved = jnp.dot(uinv_leaf[0], residue, preferred_element_type=jnp.float32)
    solved_leaf = jnp.where(keep, solved, 0.0).astype(jnp.bfloat16)
    return (solved_leaf[None], solved_rows)


def solution(mesh):
    placed = (
        P(("row", "col"), None, None),
        P("col", None),
        P(("row", "col")),
        P(("row", "col"), None),
        P(("row", "col"), None, None),
        P(("row", "col"), None, None),
        P(("row", "col"), None, None),
        P(("row", "col"), None, None),
        P("row", "col"),
        P("row", "col"),
    )
    return jax.shard_map(
        functools.partial(shards, mesh.shape["row"], mesh.shape["col"]),
        mesh=mesh,
        in_specs=placed,
        out_specs=(P(("row", "col"), None, None), P("row", None)),
        check_vma=False,
    )
```

```python
import functools

import jax
import jax.numpy as jnp
from jax import lax
from jax.experimental import pallas as pl
from jax.experimental.pallas import tpu as pltpu
from jax.sharding import PartitionSpec as P

BLK = 128
KB = 4
TILE = 256


def swap(x, axis, size, bit):
    return lax.ppermute(x, axis, [(i, i ^ bit) for i in range(size)])


def add(a, b):
    return (a.astype(jnp.float32) + b.astype(jnp.float32)).astype(jnp.bfloat16)


def place_of(share, me, size):
    apart = share ^ me
    place, bit = 0, 1
    while bit < size:
        place = place * 2 + lax.rem(lax.div(apart, bit), 2)
        bit *= 2
    return place


def forward_kernel(
    cols_n, size_ref, blocks_ref, rhs_hbm, linv_hbm, loff_hbm,
    forward_ref, keep_ref, send_ref,
    rhs_v, linv_v, loff_v, total_v, sems,
):
    width = rhs_v.shape[0]
    tiles = width // TILE
    half = keep_ref.shape[0]
    per_share = 2 * half // cols_n // BLK
    size = size_ref[0]
    me = lax.axis_index("col")

    copies = [pltpu.make_async_copy(rhs_hbm.at[0], rhs_v, sems.at[0])]
    for i in range(tiles):
        rows = pl.ds(i * TILE, TILE)
        live = pl.ds(0, (i + 1) * TILE)
        copies.append(pltpu.make_async_copy(
            linv_hbm.at[0, rows, live], linv_v.at[rows, live], sems.at[1 + i]))
    loff_copy = pltpu.make_async_copy(loff_hbm.at[0], loff_v, sems.at[1 + tiles])
    copies[0].start()
    for i in range(tiles // 2):
        copies[1 + i].start()
    loff_copy.start()
    for i in range(tiles // 2, tiles):
        copies[1 + i].start()

    keep_ref[...] = jnp.zeros_like(keep_ref)
    send_ref[...] = jnp.zeros_like(send_ref)
    position = lax.broadcasted_iota(jnp.int32, (width, rhs_v.shape[1]), 0)
    copies[0].wait()
    rhs_v[...] = jnp.where(position < size, rhs_v[...], jnp.zeros_like(rhs_v))

    def update(i):
        cols = pl.ds(i * TILE, TILE)
        term = jnp.dot(loff_v[:, cols], forward_ref[cols, :], preferred_element_type=jnp.float32)
        if i == 0:
            total_v[...] = term
        else:
            total_v[...] += term

    for i in range(tiles):
        rows = pl.ds(i * TILE, TILE)
        live = pl.ds(0, (i + 1) * TILE)
        copies[1 + i].wait()
        tile = jnp.dot(linv_v[rows, live], rhs_v[live, :], preferred_element_type=jnp.float32)
        at = lax.broadcasted_iota(jnp.int32, tile.shape, 0) + i * TILE
        forward_ref[rows, :] = jnp.where(at < size, tile, 0.0).astype(jnp.bfloat16)
        if i == tiles // 2:
            loff_copy.wait()
            for j in range(i + 1):
                update(j)
        elif i > tiles // 2:
            update(i)

    for k in range(KB):
        block = blocks_ref[0, k]
        share = lax.div(block, per_share)
        start = (place_of(share, me, cols_n) * per_share + lax.rem(block, per_share)) * BLK
        part = total_v[pl.ds(k * BLK, BLK), :].astype(jnp.bfloat16)

        @pl.when(start < half)
        def _():
            keep_ref[pl.ds(pl.multiple_of(start, BLK), BLK), :] = part

        @pl.when(start >= half)
        def _():
            send_ref[pl.ds(pl.multiple_of(start - half, BLK), BLK), :] = part


def backward_kernel(
    rows_n, cols_n, size_ref, blocks_ref, own_ref, got_ref, forward_ref, uoff_ref, uinv_ref,
    leaf_hbm, rows_hbm,
    coupled_v, residue_v, solved_v, rows_v, sems,
):
    width = forward_ref.shape[0]
    tiles = width // TILE
    half = own_ref.shape[0]
    block_r = rows_v.shape[0]
    share_rows = 2 * half // cols_n
    size = size_ref[0]
    me = lax.axis_index("col")

    def solved_at(first, count):
        share = lax.div(first, share_rows)
        start = place_of(share, me, cols_n) * share_rows + lax.rem(first, share_rows)
        inside = start < half
        near = pl.multiple_of(jnp.where(inside, start, 0), BLK)
        far = pl.multiple_of(jnp.where(inside, 0, start - half), BLK)
        return jnp.where(inside, own_ref[pl.ds(near, count), :], got_ref[pl.ds(far, count), :])

    rows_v[...] = solved_at(lax.axis_index("row") * block_r, block_r)
    rows_copy = pltpu.make_async_copy(rows_v, rows_hbm, sems.at[tiles])
    rows_copy.start()
    for k in range(KB):
        coupled_v[pl.ds(k * BLK, BLK), :] = solved_at(blocks_ref[0, k] * BLK, BLK)

    copies = []
    for i in reversed(range(tiles)):
        rows = pl.ds(i * TILE, TILE)
        live = pl.ds(i * TILE, width - i * TILE)
        term = jnp.dot(uoff_ref[0, rows, :], coupled_v[...], preferred_element_type=jnp.float32)
        at = lax.broadcasted_iota(jnp.int32, term.shape, 0) + i * TILE
        residue = forward_ref[rows, :].astype(jnp.float32) - term
        residue_v[rows, :] = jnp.where(at < size, residue, 0.0).astype(jnp.bfloat16)
        tile = jnp.dot(
            uinv_ref[0, rows, live], residue_v[live, :], preferred_element_type=jnp.float32)
        solved_v[rows, :] = jnp.where(at < size, tile, 0.0).astype(jnp.bfloat16)
        copy = pltpu.make_async_copy(solved_v.at[rows], leaf_hbm.at[0, rows], sems.at[i])
        copy.start()
        copies.append(copy)
    for copy in copies:
        copy.wait()
    rows_copy.wait()


def turned_separator(uinv_sep, rows_n, cols_n, share, block_r):
    row = lax.axis_index("row")
    ratio = rows_n // cols_n
    halves = uinv_sep.reshape(block_r, ratio, block_r)
    moved = []
    for p in range(ratio):
        one = lax.dynamic_index_in_dim(halves, lax.rem(row + p, ratio), 1, keepdims=False)
        pairs = []
        for r in range(rows_n):
            for c in range(cols_n):
                to_r, to_c = ratio * c + (r + p) % ratio, r // ratio
                pairs.append((r * cols_n + c, to_r * cols_n + to_c))
        moved.append(lax.ppermute(one, ("row", "col"), pairs))
    turned = jnp.zeros((ratio, block_r, block_r), uinv_sep.dtype)
    for p in range(ratio):
        turned = lax.dynamic_update_index_in_dim(
            turned, moved[p], lax.rem(row + ratio - p, ratio), 0)
    return turned.reshape(share, block_r)


def shards(
    rows_n,
    cols_n,
    rhs_leaf,
    rhs_sep,
    leaf_sizes,
    off_blocks,
    linv_leaf,
    uinv_leaf,
    l_off,
    u_off,
    linv_sep,
    uinv_sep,
):
    width, columns = rhs_leaf.shape[1:]
    share = rhs_sep.shape[0]
    sep = share * cols_n
    block_r = sep // rows_n
    tiles = width // TILE
    bf16 = jnp.bfloat16
    smem = pl.BlockSpec(memory_space=pltpu.SMEM)
    vmem = pl.BlockSpec(memory_space=pltpu.VMEM)
    any_space = pl.BlockSpec(memory_space=pl.ANY)
    in_vmem = functools.partial(pltpu.with_memory_space_constraint, memory_space=pltpu.VMEM)
    in_hbm = functools.partial(pltpu.with_memory_space_constraint, memory_space=pltpu.HBM)

    turned = turned_separator(uinv_sep, rows_n, cols_n, share, block_r)

    forward, keep, send = pl.pallas_call(
        functools.partial(forward_kernel, cols_n),
        out_shape=[
            pltpu.VMEM((width, columns), bf16),
            pltpu.VMEM((sep // 2, columns), bf16),
            pltpu.VMEM((sep // 2, columns), bf16),
        ],
        in_specs=[smem, smem, any_space, any_space, any_space],
        out_specs=[vmem, vmem, vmem],
        scratch_shapes=[
            pltpu.VMEM((width, columns), bf16),
            pltpu.VMEM((width, width), bf16),
            pltpu.VMEM((KB * BLK, width), bf16),
            pltpu.VMEM((KB * BLK, columns), jnp.float32),
            pltpu.SemaphoreType.DMA((tiles + 2,)),
        ],
        compiler_params=pltpu.CompilerParams(vmem_limit_bytes=24 * 2**20),
        cost_estimate=pl.CostEstimate(
            flops=900_000_000, bytes_accessed=8_000_000, transcendentals=0),
        name="leaf_forward",
    )(leaf_sizes, off_blocks, in_hbm(rhs_leaf), in_hbm(linv_leaf), in_hbm(l_off))

    bit = 1
    while bit < cols_n:
        got = swap(send, "col", cols_n, bit)
        bit *= 2
        if bit < cols_n:
            part = keep.shape[0] // 2
            send = add(keep[part:], got[part:])
            keep = add(keep[:part], got[:part])
        else:
            keep = add(keep, got)
    bit = 1
    while bit < rows_n:
        keep = add(keep, swap(keep, "row", rows_n, bit))
        bit *= 2
    sep_rhs = (rhs_sep.astype(jnp.float32) - keep.astype(jnp.float32)).astype(bf16)

    terms = jnp.dot(linv_sep, sep_rhs, preferred_element_type=jnp.float32).astype(bf16)
    bit = 1
    while bit < cols_n:
        terms = add(terms, swap(terms, "col", cols_n, bit))
        bit *= 2
    terms = jnp.dot(turned, terms, preferred_element_type=jnp.float32).astype(bf16)
    bit = 1
    while bit < rows_n:
        terms = add(terms, swap(terms, "row", rows_n, bit))
        bit *= 2
    own = terms
    bit = cols_n // 2
    while bit >= 1:
        got = swap(own, "col", cols_n, bit)
        if bit > 1:
            own = jnp.concatenate([own, got], 0)
        bit //= 2

    solved_leaf, solved_rows = pl.pallas_call(
        functools.partial(backward_kernel, rows_n, cols_n),
        out_shape=[
            jax.ShapeDtypeStruct((1, width, columns), bf16),
            jax.ShapeDtypeStruct((block_r, columns), bf16),
        ],
        in_specs=[smem, smem, vmem, vmem, vmem, vmem, vmem],
        out_specs=[any_space, any_space],
        scratch_shapes=[
            pltpu.VMEM((KB * BLK, columns), bf16),
            pltpu.VMEM((width, columns), bf16),
            pltpu.VMEM((width, columns), bf16),
            pltpu.VMEM((block_r, columns), bf16),
            pltpu.SemaphoreType.DMA((tiles + 1,)),
        ],
        compiler_params=pltpu.CompilerParams(vmem_limit_bytes=24 * 2**20),
        cost_estimate=pl.CostEstimate(
            flops=900_000_000, bytes_accessed=8_000_000, transcendentals=0),
        name="leaf_backward",
    )(
        leaf_sizes, off_blocks, in_vmem(own), in_vmem(got), in_vmem(forward),
        in_vmem(u_off), in_vmem(uinv_leaf),
    )
    return (solved_leaf, solved_rows)


def solution(mesh):
    placed = (
        P(("row", "col"), None, None),
        P("col", None),
        P(("row", "col")),
        P(("row", "col"), None),
        P(("row", "col"), None, None),
        P(("row", "col"), None, None),
        P(("row", "col"), None, None),
        P(("row", "col"), None, None),
        P("row", "col"),
        P("row", "col"),
    )
    return jax.shard_map(
        functools.partial(shards, mesh.shape["row"], mesh.shape["col"]),
        mesh=mesh,
        in_specs=placed,
        out_specs=(P(("row", "col"), None, None), P("row", None)),
        check_vma=False,
    )
```

```python
import functools

import jax
import jax.numpy as jnp
from jax import lax
from jax.experimental import pallas as pl
from jax.experimental.pallas import tpu as pltpu
from jax.sharding import PartitionSpec as P

BLK = 128
KB = 4
TILE = 256


def swap(x, axis, size, bit):
    return lax.ppermute(x, axis, [(i, i ^ bit) for i in range(size)])


def add(a, b):
    return (a.astype(jnp.float32) + b.astype(jnp.float32)).astype(jnp.bfloat16)


def place_of(share, me, size):
    apart = share ^ me
    place, bit = 0, 1
    while bit < size:
        place = place * 2 + lax.rem(lax.div(apart, bit), 2)
        bit *= 2
    return place


def forward_kernel(
    cols_n, size_in, blocks_hbm, rhs_hbm, linv_hbm, loff_hbm,
    forward_ref, keep_ref, send_ref, size_ref, blocks_ref,
    rhs_v, linv_v, loff_v, sum_v, total_v, sems,
):
    width = rhs_v.shape[0]
    tiles = width // TILE
    half = keep_ref.shape[0]
    per_share = 2 * half // cols_n // BLK
    me = lax.axis_index("col")

    blocks_copy = pltpu.make_async_copy(blocks_hbm, blocks_ref, sems.at[0])
    rhs_copy = pltpu.make_async_copy(rhs_hbm.at[0], rhs_v, sems.at[1])
    panels, offs = [], []
    for j in range(tiles):
        rows = pl.ds(j * TILE, width - j * TILE)
        cols = pl.ds(j * TILE, TILE)
        panels.append(pltpu.make_async_copy(
            linv_hbm.at[0, rows, cols], linv_v.at[rows, cols], sems.at[2 + j]))
        offs.append(pltpu.make_async_copy(
            loff_hbm.at[0, :, cols], loff_v.at[:, cols], sems.at[2 + tiles + j]))
    rhs_copy.start()
    for j in range(tiles):
        panels[j].start()
        offs[j].start()
    blocks_copy.start()

    keep_ref[...] = jnp.zeros_like(keep_ref)
    send_ref[...] = jnp.zeros_like(send_ref)
    size = size_in[0]
    size_ref[0] = size
    rhs_copy.wait()
    for j in range(tiles):
        rows = pl.ds(j * TILE, width - j * TILE)
        cols = pl.ds(j * TILE, TILE)
        at = lax.broadcasted_iota(jnp.int32, (TILE, rhs_v.shape[1]), 0) + j * TILE
        rhs = jnp.where(at < size, rhs_v[cols, :], jnp.zeros_like(rhs_v[cols, :]))
        panels[j].wait()
        term = jnp.dot(linv_v[rows, cols], rhs, preferred_element_type=jnp.float32)
        if j == 0:
            sum_v[...] = term
        else:
            sum_v[rows, :] += term
        forward = jnp.where(at < size, sum_v[cols, :], 0.0).astype(jnp.bfloat16)
        forward_ref[cols, :] = forward
        offs[j].wait()
        term = jnp.dot(loff_v[:, cols], forward, preferred_element_type=jnp.float32)
        if j == 0:
            total_v[...] = term
        else:
            total_v[...] += term

    blocks_copy.wait()
    for k in range(KB):
        block = blocks_ref[0, k]
        share = lax.div(block, per_share)
        start = (place_of(share, me, cols_n) * per_share + lax.rem(block, per_share)) * BLK
        part = total_v[pl.ds(k * BLK, BLK), :].astype(jnp.bfloat16)

        @pl.when(start < half)
        def _():
            keep_ref[pl.ds(pl.multiple_of(start, BLK), BLK), :] = part

        @pl.when(start >= half)
        def _():
            send_ref[pl.ds(pl.multiple_of(start - half, BLK), BLK), :] = part


def backward_kernel(
    rows_n, cols_n, size_ref, blocks_ref, own_ref, got_ref, forward_ref, uoff_ref, uinv_ref,
    leaf_hbm, rows_hbm,
    coupled_v, residue_v, solved_v, rows_v, sems,
):
    width = forward_ref.shape[0]
    tiles = width // TILE
    half = own_ref.shape[0]
    block_r = rows_v.shape[0]
    share_rows = 2 * half // cols_n
    size = size_ref[0]
    me = lax.axis_index("col")

    def solved_at(first, count):
        share = lax.div(first, share_rows)
        start = place_of(share, me, cols_n) * share_rows + lax.rem(first, share_rows)
        inside = start < half
        near = pl.multiple_of(jnp.where(inside, start, 0), BLK)
        far = pl.multiple_of(jnp.where(inside, 0, start - half), BLK)
        return jnp.where(inside, own_ref[pl.ds(near, count), :], got_ref[pl.ds(far, count), :])

    rows_v[...] = solved_at(lax.axis_index("row") * block_r, block_r)
    rows_copy = pltpu.make_async_copy(rows_v, rows_hbm, sems.at[tiles])
    rows_copy.start()
    for k in range(KB):
        coupled_v[pl.ds(k * BLK, BLK), :] = solved_at(blocks_ref[0, k] * BLK, BLK)

    copies = []
    for i in reversed(range(tiles)):
        rows = pl.ds(i * TILE, TILE)
        live = pl.ds(i * TILE, width - i * TILE)
        term = jnp.dot(uoff_ref[0, rows, :], coupled_v[...], preferred_element_type=jnp.float32)
        at = lax.broadcasted_iota(jnp.int32, term.shape, 0) + i * TILE
        residue = forward_ref[rows, :].astype(jnp.float32) - term
        residue_v[rows, :] = jnp.where(at < size, residue, 0.0).astype(jnp.bfloat16)
        tile = jnp.dot(
            uinv_ref[0, rows, live], residue_v[live, :], preferred_element_type=jnp.float32)
        solved_v[rows, :] = jnp.where(at < size, tile, 0.0).astype(jnp.bfloat16)
        copy = pltpu.make_async_copy(solved_v.at[rows], leaf_hbm.at[0, rows], sems.at[i])
        copy.start()
        copies.append(copy)
    for copy in copies:
        copy.wait()
    rows_copy.wait()


def chosen(parts, which):
    out = parts[0]
    for h in range(1, len(parts)):
        out = jnp.where(which == h, parts[h], out)
    return out


def turned_separator(uinv_sep, rows_n, cols_n, block_r):
    row = lax.axis_index("row")
    ratio = rows_n // cols_n
    parts = [uinv_sep[:, h * block_r:(h + 1) * block_r] for h in range(ratio)]
    moved = []
    for p in range(ratio):
        pairs = []
        for r in range(rows_n):
            for c in range(cols_n):
                to_r, to_c = ratio * c + (r + p) % ratio, r // ratio
                pairs.append((r * cols_n + c, to_r * cols_n + to_c))
        moved.append(lax.ppermute(
            chosen(parts, lax.rem(row + p, ratio)), ("row", "col"), pairs))
    return jnp.concatenate(
        [chosen(moved, lax.rem(row + ratio - h, ratio)) for h in range(ratio)], 0)


def shards(
    rows_n,
    cols_n,
    rhs_leaf,
    rhs_sep,
    leaf_sizes,
    off_blocks,
    linv_leaf,
    uinv_leaf,
    l_off,
    u_off,
    linv_sep,
    uinv_sep,
):
    width, columns = rhs_leaf.shape[1:]
    share = rhs_sep.shape[0]
    sep = share * cols_n
    block_r = sep // rows_n
    tiles = width // TILE
    bf16 = jnp.bfloat16
    smem = pl.BlockSpec(memory_space=pltpu.SMEM)
    vmem = pl.BlockSpec(memory_space=pltpu.VMEM)
    any_space = pl.BlockSpec(memory_space=pl.ANY)
    in_vmem = functools.partial(pltpu.with_memory_space_constraint, memory_space=pltpu.VMEM)
    in_smem = functools.partial(pltpu.with_memory_space_constraint, memory_space=pltpu.SMEM)
    in_hbm = functools.partial(pltpu.with_memory_space_constraint, memory_space=pltpu.HBM)

    turned = turned_separator(uinv_sep, rows_n, cols_n, block_r)

    forward, keep, send, size, blocks = pl.pallas_call(
        functools.partial(forward_kernel, cols_n),
        out_shape=[
            pltpu.VMEM((width, columns), bf16),
            pltpu.VMEM((sep // 2, columns), bf16),
            pltpu.VMEM((sep // 2, columns), bf16),
            pltpu.SMEM((1,), jnp.int32),
            pltpu.SMEM((1, KB), jnp.int32),
        ],
        in_specs=[smem, any_space, any_space, any_space, any_space],
        out_specs=[vmem, vmem, vmem, smem, smem],
        scratch_shapes=[
            pltpu.VMEM((width, columns), bf16),
            pltpu.VMEM((width, width), bf16),
            pltpu.VMEM((KB * BLK, width), bf16),
            pltpu.VMEM((width, columns), jnp.float32),
            pltpu.VMEM((KB * BLK, columns), jnp.float32),
            pltpu.SemaphoreType.DMA((2 * tiles + 2,)),
        ],
        compiler_params=pltpu.CompilerParams(vmem_limit_bytes=24 * 2**20),
        cost_estimate=pl.CostEstimate(
            flops=900_000_000, bytes_accessed=8_000_000, transcendentals=0),
        name="leaf_forward",
    )(
        leaf_sizes, in_hbm(off_blocks), in_hbm(rhs_leaf), in_hbm(linv_leaf),
        in_hbm(l_off),
    )
    keep, send, turned = lax.optimization_barrier((keep, send, turned))

    bit = 1
    while bit < cols_n:
        got = swap(send, "col", cols_n, bit)
        bit *= 2
        if bit < cols_n:
            part = keep.shape[0] // 2
            send = add(keep[part:], got[part:])
            keep = add(keep[:part], got[:part])
        else:
            keep = add(keep, got)
    bit = 1
    while bit < rows_n:
        keep = add(keep, swap(keep, "row", rows_n, bit))
        bit *= 2
    sep_rhs = (rhs_sep.astype(jnp.float32) - keep.astype(jnp.float32)).astype(bf16)

    terms = jnp.dot(linv_sep, sep_rhs, preferred_element_type=jnp.float32).astype(bf16)
    bit = 1
    while bit < cols_n:
        terms = add(terms, swap(terms, "col", cols_n, bit))
        bit *= 2
    terms = jnp.dot(turned, terms, preferred_element_type=jnp.float32).astype(bf16)
    bit = 1
    while bit < rows_n:
        terms = add(terms, swap(terms, "row", rows_n, bit))
        bit *= 2
    own = terms
    bit = cols_n // 2
    while bit >= 1:
        got = swap(own, "col", cols_n, bit)
        if bit > 1:
            own = jnp.concatenate([own, got], 0)
        bit //= 2

    solved_leaf, solved_rows = pl.pallas_call(
        functools.partial(backward_kernel, rows_n, cols_n),
        out_shape=[
            jax.ShapeDtypeStruct((1, width, columns), bf16),
            jax.ShapeDtypeStruct((block_r, columns), bf16),
        ],
        in_specs=[smem, smem, vmem, vmem, vmem, vmem, vmem],
        out_specs=[any_space, any_space],
        scratch_shapes=[
            pltpu.VMEM((KB * BLK, columns), bf16),
            pltpu.VMEM((width, columns), bf16),
            pltpu.VMEM((width, columns), bf16),
            pltpu.VMEM((block_r, columns), bf16),
            pltpu.SemaphoreType.DMA((tiles + 1,)),
        ],
        compiler_params=pltpu.CompilerParams(vmem_limit_bytes=24 * 2**20),
        cost_estimate=pl.CostEstimate(
            flops=900_000_000, bytes_accessed=8_000_000, transcendentals=0),
        name="leaf_backward",
    )(
        in_smem(size), in_smem(blocks), in_vmem(own), in_vmem(got), in_vmem(forward),
        in_vmem(u_off), in_vmem(uinv_leaf),
    )
    return (solved_leaf, solved_rows)


def solution(mesh):
    placed = (
        P(("row", "col"), None, None),
        P("col", None),
        P(("row", "col")),
        P(("row", "col"), None),
        P(("row", "col"), None, None),
        P(("row", "col"), None, None),
        P(("row", "col"), None, None),
        P(("row", "col"), None, None),
        P("row", "col"),
        P("row", "col"),
    )
    return jax.shard_map(
        functools.partial(shards, mesh.shape["row"], mesh.shape["col"]),
        mesh=mesh,
        in_specs=placed,
        out_specs=(P(("row", "col"), None, None), P("row", None)),
        check_vma=False,
    )
```

```python
import functools

import jax
import jax.numpy as jnp
from jax import lax
from jax.experimental import pallas as pl
from jax.experimental.pallas import tpu as pltpu
from jax.sharding import PartitionSpec as P

BLK = 128
KB = 4
TILE = 256


def swap(x, axis, size, bit):
    return lax.ppermute(x, axis, [(i, i ^ bit) for i in range(size)])


def add(a, b):
    return (a.astype(jnp.float32) + b.astype(jnp.float32)).astype(jnp.bfloat16)


def place_of(share, me, size):
    apart = share ^ me
    place, bit = 0, 1
    while bit < size:
        place = place * 2 + lax.rem(lax.div(apart, bit), 2)
        bit *= 2
    return place


def forward_kernel(
    cols_n, size_in, blocks_hbm, rhs_hbm, linv_hbm, loff_hbm, usep_hbm,
    forward_ref, keep_ref, send_ref, size_ref, blocks_ref, *rest,
):
    piece_refs, (rhs_v, linv_v, loff_v, sum_v, total_v, sems) = rest[:-6], rest[-6:]
    width = rhs_v.shape[0]
    tiles = width // TILE
    half = keep_ref.shape[0]
    per_share = 2 * half // cols_n // BLK
    me = lax.axis_index("col")
    row = lax.axis_index("row")

    copies = [pltpu.make_async_copy(rhs_hbm.at[0], rhs_v, sems.at[0])]
    for j in range(tiles):
        rows = pl.ds(j * TILE, width - j * TILE)
        cols = pl.ds(j * TILE, TILE)
        copies.append(pltpu.make_async_copy(
            linv_hbm.at[0, rows, cols], linv_v.at[rows, cols], sems.at[1 + 2 * j]))
        copies.append(pltpu.make_async_copy(
            loff_hbm.at[0, :, cols], loff_v.at[:, cols], sems.at[2 + 2 * j]))
    late = [pltpu.make_async_copy(blocks_hbm, blocks_ref, sems.at[1 + 2 * tiles])]
    ratio = len(piece_refs)
    block_r = piece_refs[0].shape[1]
    for p in range(ratio):
        first = pl.multiple_of(lax.rem(row + p, ratio) * block_r, block_r)
        late.append(pltpu.make_async_copy(
            usep_hbm.at[:, pl.ds(first, block_r)], piece_refs[p], sems.at[2 + 2 * tiles + p]))
    ahead = 4
    for copy in copies[:ahead]:
        copy.start()

    def arrive(n):
        copies[n].wait()
        if n + ahead < len(copies):
            copies[n + ahead].start()
        elif n + ahead == len(copies):
            for copy in late:
                copy.start()

    size = size_in[0]
    size_ref[0] = size
    keep_ref[...] = jnp.zeros_like(keep_ref)
    send_ref[...] = jnp.zeros_like(send_ref)
    arrive(0)
    for j in range(tiles):
        rows = pl.ds(j * TILE, width - j * TILE)
        cols = pl.ds(j * TILE, TILE)
        at = lax.broadcasted_iota(jnp.int32, (TILE, rhs_v.shape[1]), 0) + j * TILE
        rhs = jnp.where(at < size, rhs_v[cols, :], jnp.zeros_like(rhs_v[cols, :]))
        arrive(1 + 2 * j)
        term = jnp.dot(linv_v[rows, cols], rhs, preferred_element_type=jnp.float32)
        if j == 0:
            sum_v[...] = term
        else:
            sum_v[rows, :] += term
        forward = jnp.where(at < size, sum_v[cols, :], 0.0).astype(jnp.bfloat16)
        forward_ref[cols, :] = forward
        arrive(2 + 2 * j)
        term = jnp.dot(loff_v[:, cols], forward, preferred_element_type=jnp.float32)
        if j == 0:
            total_v[...] = term
        else:
            total_v[...] += term

    for copy in late:
        copy.wait()
    for k in range(KB):
        block = blocks_ref[0, k]
        share = lax.div(block, per_share)
        start = (place_of(share, me, cols_n) * per_share + lax.rem(block, per_share)) * BLK
        part = total_v[pl.ds(k * BLK, BLK), :].astype(jnp.bfloat16)

        @pl.when(start < half)
        def _():
            keep_ref[pl.ds(pl.multiple_of(start, BLK), BLK), :] = part

        @pl.when(start >= half)
        def _():
            send_ref[pl.ds(pl.multiple_of(start - half, BLK), BLK), :] = part


def turned_kernel(term_ref, got_ref, *rest):
    moved_refs, out_ref = rest[:-1], rest[-1]
    ratio = len(moved_refs)
    block_r = moved_refs[0].shape[0]
    row = lax.axis_index("row")
    source = add(term_ref[...], got_ref[...])
    for p in range(ratio):
        first = pl.multiple_of(lax.rem(row + ratio - p, ratio) * block_r, block_r)
        out = jnp.dot(moved_refs[p][...], source, preferred_element_type=jnp.float32)
        out_ref[pl.ds(first, block_r), :] = out.astype(jnp.bfloat16)


def backward_kernel(
    rows_n, cols_n, size_ref, blocks_ref, own_ref, got_ref, forward_ref, uoff_ref, uinv_ref,
    leaf_hbm, rows_hbm,
    coupled_v, residue_v, solved_v, rows_v, sems,
):
    width = forward_ref.shape[0]
    tiles = width // TILE
    half = own_ref.shape[0]
    block_r = rows_v.shape[0]
    share_rows = 2 * half // cols_n
    size = size_ref[0]
    me = lax.axis_index("col")

    def solved_at(first, count):
        share = lax.div(first, share_rows)
        start = place_of(share, me, cols_n) * share_rows + lax.rem(first, share_rows)
        inside = start < half
        near = pl.multiple_of(jnp.where(inside, start, 0), BLK)
        far = pl.multiple_of(jnp.where(inside, 0, start - half), BLK)
        return jnp.where(inside, own_ref[pl.ds(near, count), :], got_ref[pl.ds(far, count), :])

    rows_v[...] = solved_at(lax.axis_index("row") * block_r, block_r)
    rows_copy = pltpu.make_async_copy(rows_v, rows_hbm, sems.at[tiles])
    rows_copy.start()
    for k in range(KB):
        coupled_v[pl.ds(k * BLK, BLK), :] = solved_at(blocks_ref[0, k] * BLK, BLK)

    copies = []
    for i in reversed(range(tiles)):
        rows = pl.ds(i * TILE, TILE)
        live = pl.ds(i * TILE, width - i * TILE)
        term = jnp.dot(uoff_ref[0, rows, :], coupled_v[...], preferred_element_type=jnp.float32)
        at = lax.broadcasted_iota(jnp.int32, term.shape, 0) + i * TILE
        residue = forward_ref[rows, :].astype(jnp.float32) - term
        residue_v[rows, :] = jnp.where(at < size, residue, 0.0).astype(jnp.bfloat16)
        tile = jnp.dot(
            uinv_ref[0, rows, live], residue_v[live, :], preferred_element_type=jnp.float32)
        solved_v[rows, :] = jnp.where(at < size, tile, 0.0).astype(jnp.bfloat16)
        copy = pltpu.make_async_copy(solved_v.at[rows], leaf_hbm.at[0, rows], sems.at[i])
        copy.start()
        copies.append(copy)
    for copy in copies:
        copy.wait()
    rows_copy.wait()


def moved_block(piece, p, rows_n, cols_n):
    ratio = rows_n // cols_n
    pairs = []
    for r in range(rows_n):
        for c in range(cols_n):
            to_r, to_c = ratio * c + (r + p) % ratio, r // ratio
            pairs.append((r * cols_n + c, to_r * cols_n + to_c))
    return lax.ppermute(piece, ("row", "col"), pairs)


def shards(
    rows_n,
    cols_n,
    rhs_leaf,
    rhs_sep,
    leaf_sizes,
    off_blocks,
    linv_leaf,
    uinv_leaf,
    l_off,
    u_off,
    linv_sep,
    uinv_sep,
):
    width, columns = rhs_leaf.shape[1:]
    share = rhs_sep.shape[0]
    sep = share * cols_n
    block_r = sep // rows_n
    ratio = rows_n // cols_n
    tiles = width // TILE
    bf16 = jnp.bfloat16
    smem = pl.BlockSpec(memory_space=pltpu.SMEM)
    vmem = pl.BlockSpec(memory_space=pltpu.VMEM)
    any_space = pl.BlockSpec(memory_space=pl.ANY)
    in_vmem = functools.partial(pltpu.with_memory_space_constraint, memory_space=pltpu.VMEM)
    in_smem = functools.partial(pltpu.with_memory_space_constraint, memory_space=pltpu.SMEM)
    in_hbm = functools.partial(pltpu.with_memory_space_constraint, memory_space=pltpu.HBM)

    forward, keep, send, size, blocks, *pieces = pl.pallas_call(
        functools.partial(forward_kernel, cols_n),
        out_shape=[
            pltpu.VMEM((width, columns), bf16),
            pltpu.VMEM((sep // 2, columns), bf16),
            pltpu.VMEM((sep // 2, columns), bf16),
            pltpu.SMEM((1,), jnp.int32),
            pltpu.SMEM((1, KB), jnp.int32),
        ] + [pltpu.VMEM((block_r, block_r), bf16)] * ratio,
        in_specs=[smem] + [any_space] * 5,
        out_specs=[vmem, vmem, vmem, smem, smem] + [vmem] * ratio,
        scratch_shapes=[
            pltpu.VMEM((width, columns), bf16),
            pltpu.VMEM((width, width), bf16),
            pltpu.VMEM((KB * BLK, width), bf16),
            pltpu.VMEM((width, columns), jnp.float32),
            pltpu.VMEM((KB * BLK, columns), jnp.float32),
            pltpu.SemaphoreType.DMA((2 * tiles + 2 + ratio,)),
        ],
        compiler_params=pltpu.CompilerParams(vmem_limit_bytes=59 * 2**20),
        cost_estimate=pl.CostEstimate(
            flops=900_000_000, bytes_accessed=8_000_000, transcendentals=0),
        name="leaf_forward",
    )(
        leaf_sizes, in_hbm(off_blocks), in_hbm(rhs_leaf), in_hbm(linv_leaf),
        in_hbm(l_off), in_hbm(uinv_sep),
    )
    tied = lax.optimization_barrier
    keep, send, uinv_leaf, u_off = tied((keep, send, uinv_leaf, u_off))

    bit = 1
    while bit < cols_n:
        got = swap(send, "col", cols_n, bit)
        bit *= 2
        if bit < cols_n:
            part = keep.shape[0] // 2
            send = add(keep[part:], got[part:])
            keep = add(keep[:part], got[:part])
        else:
            keep = add(keep, got)
    moved = []
    bit = 1
    while bit < rows_n:
        if len(moved) < ratio:
            keep, piece = tied((keep, pieces[len(moved)]))
            moved.append(moved_block(piece, len(moved), rows_n, cols_n))
        keep = add(keep, swap(keep, "row", rows_n, bit))
        bit *= 2
        if bit < rows_n:
            keep, *moved[:-1] = tied((keep, *moved[:-1]))
    while len(moved) < ratio:
        moved.append(moved_block(pieces[len(moved)], len(moved), rows_n, cols_n))
    keep, *moved = tied((keep, *moved))
    sep_rhs = (rhs_sep.astype(jnp.float32) - keep.astype(jnp.float32)).astype(bf16)

    terms = jnp.dot(linv_sep, sep_rhs, preferred_element_type=jnp.float32).astype(bf16)
    bit = 1
    while bit < cols_n:
        got = swap(terms, "col", cols_n, bit)
        bit *= 2
        if bit < cols_n:
            terms = add(terms, got)
    terms = pl.pallas_call(
        turned_kernel,
        out_shape=pltpu.VMEM((share, columns), bf16),
        in_specs=[vmem] * (2 + ratio),
        out_specs=vmem,
        compiler_params=pltpu.CompilerParams(vmem_limit_bytes=4 * 2**20),
        name="separator_backward",
    )(in_vmem(terms), in_vmem(got), *(in_vmem(one) for one in moved))
    bit = 1
    while bit < rows_n:
        terms = add(terms, swap(terms, "row", rows_n, bit))
        bit *= 2
    own = terms
    bit = cols_n // 2
    while bit >= 1:
        got = swap(own, "col", cols_n, bit)
        if bit > 1:
            own = jnp.concatenate([own, got], 0)
        bit //= 2

    solved_leaf, solved_rows = pl.pallas_call(
        functools.partial(backward_kernel, rows_n, cols_n),
        out_shape=[
            jax.ShapeDtypeStruct((1, width, columns), bf16),
            jax.ShapeDtypeStruct((block_r, columns), bf16),
        ],
        in_specs=[smem, smem, vmem, vmem, vmem, vmem, vmem],
        out_specs=[any_space, any_space],
        scratch_shapes=[
            pltpu.VMEM((KB * BLK, columns), bf16),
            pltpu.VMEM((width, columns), bf16),
            pltpu.VMEM((width, columns), bf16),
            pltpu.VMEM((block_r, columns), bf16),
            pltpu.SemaphoreType.DMA((tiles + 1,)),
        ],
        compiler_params=pltpu.CompilerParams(vmem_limit_bytes=24 * 2**20),
        cost_estimate=pl.CostEstimate(
            flops=900_000_000, bytes_accessed=8_000_000, transcendentals=0),
        name="leaf_backward",
    )(
        in_smem(size), in_smem(blocks), in_vmem(own), in_vmem(got), in_vmem(forward),
        in_vmem(u_off), in_vmem(uinv_leaf),
    )
    return (solved_leaf, solved_rows)


def solution(mesh):
    placed = (
        P(("row", "col"), None, None),
        P("col", None),
        P(("row", "col")),
        P(("row", "col"), None),
        P(("row", "col"), None, None),
        P(("row", "col"), None, None),
        P(("row", "col"), None, None),
        P(("row", "col"), None, None),
        P("row", "col"),
        P("row", "col"),
    )
    return jax.shard_map(
        functools.partial(shards, mesh.shape["row"], mesh.shape["col"]),
        mesh=mesh,
        in_specs=placed,
        out_specs=(P(("row", "col"), None, None), P("row", None)),
        check_vma=False,
    )
```

```python
import functools

import jax
import jax.numpy as jnp
from jax import lax
from jax.experimental import pallas as pl
from jax.experimental.pallas import tpu as pltpu
from jax.sharding import PartitionSpec as P

BLK = 128
KB = 4
TILE = 256


def swap(x, axis, size, bit):
    return lax.ppermute(x, axis, [(i, i ^ bit) for i in range(size)])


def add(a, b):
    return (a.astype(jnp.float32) + b.astype(jnp.float32)).astype(jnp.bfloat16)


def place_of(share, me, size):
    apart = share ^ me
    place, bit = 0, 1
    while bit < size:
        place = place * 2 + lax.rem(lax.div(apart, bit), 2)
        bit *= 2
    return place


def forward_kernel(
    cols_n, size_in, blocks_hbm, rhs_hbm, linv_hbm, loff_hbm,
    forward_ref, keep_ref, send_ref, size_ref, blocks_ref,
    rhs_v, linv_v, loff_v, total_v, sems,
):
    width = rhs_v.shape[0]
    tiles = width // TILE
    half = keep_ref.shape[0]
    per_share = 2 * half // cols_n // BLK
    me = lax.axis_index("col")

    copies = [pltpu.make_async_copy(rhs_hbm.at[0], rhs_v, sems.at[0])]
    for i in range(tiles):
        rows = pl.ds(i * TILE, TILE)
        live = pl.ds(0, (i + 1) * TILE)
        copies.append(pltpu.make_async_copy(
            linv_hbm.at[0, rows, live], linv_v.at[rows, live], sems.at[1 + 2 * i]))
        copies.append(pltpu.make_async_copy(
            loff_hbm.at[0, :, rows], loff_v.at[:, rows], sems.at[2 + 2 * i]))
    copies.append(pltpu.make_async_copy(blocks_hbm, blocks_ref, sems.at[1 + 2 * tiles]))
    ahead = 6
    for copy in copies[:ahead]:
        copy.start()

    def arrive(n):
        copies[n].wait()
        if n + ahead < len(copies):
            copies[n + ahead].start()

    size = size_in[0]
    size_ref[0] = size
    keep_ref[...] = jnp.zeros_like(keep_ref)
    send_ref[...] = jnp.zeros_like(send_ref)
    arrive(0)
    for i in range(tiles):
        rows = pl.ds(i * TILE, TILE)
        live = pl.ds(0, (i + 1) * TILE)
        at = lax.broadcasted_iota(jnp.int32, (TILE, rhs_v.shape[1]), 0) + i * TILE
        rhs_v[rows, :] = jnp.where(at < size, rhs_v[rows, :], jnp.zeros_like(rhs_v[rows, :]))
        arrive(1 + 2 * i)
        tile = jnp.dot(linv_v[rows, live], rhs_v[live, :], preferred_element_type=jnp.float32)
        forward = jnp.where(at < size, tile, 0.0).astype(jnp.bfloat16)
        forward_ref[rows, :] = forward
        arrive(2 + 2 * i)
        term = jnp.dot(loff_v[:, rows], forward, preferred_element_type=jnp.float32)
        if i == 0:
            total_v[...] = term
        else:
            total_v[...] += term

    copies[-1].wait()
    for k in range(KB):
        block = blocks_ref[0, k]
        share = lax.div(block, per_share)
        start = (place_of(share, me, cols_n) * per_share + lax.rem(block, per_share)) * BLK
        part = total_v[pl.ds(k * BLK, BLK), :].astype(jnp.bfloat16)

        @pl.when(start < half)
        def _():
            keep_ref[pl.ds(pl.multiple_of(start, BLK), BLK), :] = part

        @pl.when(start >= half)
        def _():
            send_ref[pl.ds(pl.multiple_of(start - half, BLK), BLK), :] = part


def turned_kernel(ratio, own_ref, got_ref, factor_ref, out_ref):
    block_r = out_ref.shape[0]
    half = own_ref.shape[0]
    low = lax.rem(lax.axis_index("row"), ratio)
    total = None
    for j in range(ratio):
        first = pl.multiple_of((low ^ j) * block_r, block_r)
        at = j * block_r
        part = own_ref[at:at + block_r, :] if at < half else got_ref[at - half:at - half + block_r, :]
        term = jnp.dot(
            factor_ref[:, pl.ds(first, block_r)], part, preferred_element_type=jnp.float32)
        total = term if total is None else total + term
    out_ref[...] = total.astype(jnp.bfloat16)


def backward_kernel(
    rows_n, cols_n, size_ref, blocks_ref, own_ref, got_ref, forward_ref, uoff_ref, uinv_ref,
    leaf_hbm, rows_hbm,
    coupled_v, residue_v, solved_v, rows_v, sems,
):
    width = forward_ref.shape[0]
    tiles = width // TILE
    half = own_ref.shape[0]
    block_r = rows_v.shape[0]
    ratio = rows_n // cols_n
    size = size_ref[0]
    me = lax.axis_index("col")
    low = lax.rem(lax.axis_index("row"), ratio)

    def solved_at(first, count):
        unit = lax.div(first, block_r)
        place = place_of(lax.div(unit, ratio), me, cols_n) * ratio + (lax.rem(unit, ratio) ^ low)
        start = place * block_r + lax.rem(first, block_r)
        inside = start < half
        near = pl.multiple_of(jnp.where(inside, start, 0), BLK)
        far = pl.multiple_of(jnp.where(inside, 0, start - half), BLK)
        return jnp.where(inside, own_ref[pl.ds(near, count), :], got_ref[pl.ds(far, count), :])

    rows_v[...] = solved_at(lax.axis_index("row") * block_r, block_r)
    rows_copy = pltpu.make_async_copy(rows_v, rows_hbm, sems.at[tiles])
    rows_copy.start()
    for k in range(KB):
        coupled_v[pl.ds(k * BLK, BLK), :] = solved_at(blocks_ref[0, k] * BLK, BLK)

    copies = []
    for i in reversed(range(tiles)):
        rows = pl.ds(i * TILE, TILE)
        live = pl.ds(i * TILE, width - i * TILE)
        term = jnp.dot(uoff_ref[0, rows, :], coupled_v[...], preferred_element_type=jnp.float32)
        at = lax.broadcasted_iota(jnp.int32, term.shape, 0) + i * TILE
        residue = forward_ref[rows, :].astype(jnp.float32) - term
        residue_v[rows, :] = jnp.where(at < size, residue, 0.0).astype(jnp.bfloat16)
        tile = jnp.dot(
            uinv_ref[0, rows, live], residue_v[live, :], preferred_element_type=jnp.float32)
        solved_v[rows, :] = jnp.where(at < size, tile, 0.0).astype(jnp.bfloat16)
        copy = pltpu.make_async_copy(solved_v.at[rows], leaf_hbm.at[0, rows], sems.at[i])
        copy.start()
        copies.append(copy)
    for copy in copies:
        copy.wait()
    rows_copy.wait()


def shards(
    rows_n,
    cols_n,
    rhs_leaf,
    rhs_sep,
    leaf_sizes,
    off_blocks,
    linv_leaf,
    uinv_leaf,
    l_off,
    u_off,
    linv_sep,
    uinv_sep,
):
    width, columns = rhs_leaf.shape[1:]
    share = rhs_sep.shape[0]
    sep = share * cols_n
    block_r = sep // rows_n
    ratio = rows_n // cols_n
    tiles = width // TILE
    bf16 = jnp.bfloat16
    smem = pl.BlockSpec(memory_space=pltpu.SMEM)
    vmem = pl.BlockSpec(memory_space=pltpu.VMEM)
    any_space = pl.BlockSpec(memory_space=pl.ANY)
    in_vmem = functools.partial(pltpu.with_memory_space_constraint, memory_space=pltpu.VMEM)
    in_smem = functools.partial(pltpu.with_memory_space_constraint, memory_space=pltpu.SMEM)
    in_hbm = functools.partial(pltpu.with_memory_space_constraint, memory_space=pltpu.HBM)

    pairs = []
    for r in range(rows_n):
        for c in range(cols_n):
            to_r, to_c = c * ratio + r % ratio, r // ratio
            pairs.append((r * cols_n + c, to_r * cols_n + to_c))
    turned = lax.ppermute(uinv_sep, ("row", "col"), pairs)

    forward, keep, send, size, blocks = pl.pallas_call(
        functools.partial(forward_kernel, cols_n),
        out_shape=[
            pltpu.VMEM((width, columns), bf16),
            pltpu.VMEM((sep // 2, columns), bf16),
            pltpu.VMEM((sep // 2, columns), bf16),
            pltpu.SMEM((1,), jnp.int32),
            pltpu.SMEM((1, KB), jnp.int32),
        ],
        in_specs=[smem] + [any_space] * 4,
        out_specs=[vmem, vmem, vmem, smem, smem],
        scratch_shapes=[
            pltpu.VMEM((width, columns), bf16),
            pltpu.VMEM((width, width), bf16),
            pltpu.VMEM((KB * BLK, width), bf16),
            pltpu.VMEM((KB * BLK, columns), jnp.float32),
            pltpu.SemaphoreType.DMA((2 * tiles + 2,)),
        ],
        compiler_params=pltpu.CompilerParams(vmem_limit_bytes=24 * 2**20),
        cost_estimate=pl.CostEstimate(
            flops=900_000_000, bytes_accessed=8_000_000, transcendentals=0),
        name="leaf_forward",
    )(
        leaf_sizes, in_hbm(off_blocks), in_hbm(rhs_leaf), in_hbm(linv_leaf),
        in_hbm(l_off),
    )
    bit = 1
    while bit < cols_n:
        got = swap(send, "col", cols_n, bit)
        bit *= 2
        if bit < cols_n:
            part = keep.shape[0] // 2
            send = add(keep[part:], got[part:])
            send, turned = lax.optimization_barrier((send, turned))
            keep = add(keep[:part], got[:part])
        else:
            keep = add(keep, got)
    bit = 1
    while bit < rows_n:
        keep = add(keep, swap(keep, "row", rows_n, bit))
        bit *= 2
    sep_rhs = (rhs_sep.astype(jnp.float32) - keep.astype(jnp.float32)).astype(bf16)

    own = jnp.dot(linv_sep, sep_rhs, preferred_element_type=jnp.float32).astype(bf16)
    bit = 1
    while bit < cols_n:
        own = add(own, swap(own, "col", cols_n, bit))
        bit *= 2
    bit = 1
    while bit < ratio:
        got = swap(own, "row", rows_n, bit)
        bit *= 2
        if bit < ratio:
            own = jnp.concatenate([own, got], 0)
    own = pl.pallas_call(
        functools.partial(turned_kernel, ratio),
        out_shape=pltpu.VMEM((block_r, columns), bf16),
        in_specs=[vmem] * 3,
        out_specs=vmem,
        compiler_params=pltpu.CompilerParams(vmem_limit_bytes=4 * 2**20),
        name="separator_backward",
    )(in_vmem(own), in_vmem(got), in_vmem(turned))
    bit = ratio
    while bit < rows_n:
        own = add(own, swap(own, "row", rows_n, bit))
        bit *= 2
    bit = 1
    while bit < ratio:
        own = jnp.concatenate([own, swap(own, "row", rows_n, bit)], 0)
        bit *= 2
    bit = cols_n // 2
    while bit >= 1:
        got = swap(own, "col", cols_n, bit)
        if bit > 1:
            own = jnp.concatenate([own, got], 0)
        bit //= 2

    solved_leaf, solved_rows = pl.pallas_call(
        functools.partial(backward_kernel, rows_n, cols_n),
        out_shape=[
            jax.ShapeDtypeStruct((1, width, columns), bf16),
            jax.ShapeDtypeStruct((block_r, columns), bf16),
        ],
        in_specs=[smem, smem, vmem, vmem, vmem, vmem, vmem],
        out_specs=[any_space, any_space],
        scratch_shapes=[
            pltpu.VMEM((KB * BLK, columns), bf16),
            pltpu.VMEM((width, columns), bf16),
            pltpu.VMEM((width, columns), bf16),
            pltpu.VMEM((block_r, columns), bf16),
            pltpu.SemaphoreType.DMA((tiles + 1,)),
        ],
        compiler_params=pltpu.CompilerParams(vmem_limit_bytes=24 * 2**20),
        cost_estimate=pl.CostEstimate(
            flops=900_000_000, bytes_accessed=8_000_000, transcendentals=0),
        name="leaf_backward",
    )(
        in_smem(size), in_smem(blocks), in_vmem(own), in_vmem(got), in_vmem(forward),
        in_vmem(u_off), in_vmem(uinv_leaf),
    )
    return (solved_leaf, solved_rows)


def solution(mesh):
    placed = (
        P(("row", "col"), None, None),
        P("col", None),
        P(("row", "col")),
        P(("row", "col"), None),
        P(("row", "col"), None, None),
        P(("row", "col"), None, None),
        P(("row", "col"), None, None),
        P(("row", "col"), None, None),
        P("row", "col"),
        P("row", "col"),
    )
    return jax.shard_map(
        functools.partial(shards, mesh.shape["row"], mesh.shape["col"]),
        mesh=mesh,
        in_specs=placed,
        out_specs=(P(("row", "col"), None, None), P("row", None)),
        check_vma=False,
    )
```

```python
import functools

import jax
import jax.numpy as jnp
from jax import lax
from jax.experimental import pallas as pl
from jax.experimental.pallas import tpu as pltpu
from jax.sharding import PartitionSpec as P

BLK = 128
KB = 4
TILE = 256


def swap(x, axis, size, bit):
    return lax.ppermute(x, axis, [(i, i ^ bit) for i in range(size)])


def add(a, b):
    return (a.astype(jnp.float32) + b.astype(jnp.float32)).astype(jnp.bfloat16)


def place_of(share, me, size):
    apart = share ^ me
    place, bit = 0, 1
    while bit < size:
        place = place * 2 + lax.rem(lax.div(apart, bit), 2)
        bit *= 2
    return place


def forward_kernel(
    cols_n, size_in, blocks_hbm, rhs_hbm, linv_hbm, loff_hbm,
    forward_ref, keep_ref, send_ref, size_ref, blocks_ref,
    rhs_v, linv_v, loff_v, total_v, sems,
):
    width = rhs_v.shape[0]
    tiles = width // TILE
    half = keep_ref.shape[0]
    per_share = 2 * half // cols_n // BLK
    me = lax.axis_index("col")

    copies = [pltpu.make_async_copy(rhs_hbm.at[0], rhs_v, sems.at[0])]
    for i in range(tiles):
        rows = pl.ds(i * TILE, TILE)
        live = pl.ds(0, (i + 1) * TILE)
        copies.append(pltpu.make_async_copy(
            linv_hbm.at[0, rows, live], linv_v.at[rows, live], sems.at[1 + 2 * i]))
        copies.append(pltpu.make_async_copy(
            loff_hbm.at[0, :, rows], loff_v.at[:, rows], sems.at[2 + 2 * i]))
    copies.append(pltpu.make_async_copy(blocks_hbm, blocks_ref, sems.at[1 + 2 * tiles]))
    ahead = 6
    for copy in copies[:ahead]:
        copy.start()

    def arrive(n):
        copies[n].wait()
        if n + ahead < len(copies):
            copies[n + ahead].start()

    size = size_in[0]
    size_ref[0] = size
    keep_ref[...] = jnp.zeros_like(keep_ref)
    send_ref[...] = jnp.zeros_like(send_ref)
    arrive(0)
    for i in range(tiles):
        rows = pl.ds(i * TILE, TILE)
        live = pl.ds(0, (i + 1) * TILE)
        at = lax.broadcasted_iota(jnp.int32, (TILE, rhs_v.shape[1]), 0) + i * TILE
        rhs_v[rows, :] = jnp.where(at < size, rhs_v[rows, :], jnp.zeros_like(rhs_v[rows, :]))
        arrive(1 + 2 * i)
        tile = jnp.dot(linv_v[rows, live], rhs_v[live, :], preferred_element_type=jnp.float32)
        forward = jnp.where(at < size, tile, 0.0).astype(jnp.bfloat16)
        forward_ref[rows, :] = forward
        arrive(2 + 2 * i)
        term = jnp.dot(loff_v[:, rows], forward, preferred_element_type=jnp.float32)
        if i == 0:
            total_v[...] = term
        else:
            total_v[...] += term

    copies[-1].wait()
    for k in range(KB):
        block = blocks_ref[0, k]
        share = lax.div(block, per_share)
        start = (place_of(share, me, cols_n) * per_share + lax.rem(block, per_share)) * BLK
        part = total_v[pl.ds(k * BLK, BLK), :].astype(jnp.bfloat16)

        @pl.when(start < half)
        def _():
            keep_ref[pl.ds(pl.multiple_of(start, BLK), BLK), :] = part

        @pl.when(start >= half)
        def _():
            send_ref[pl.ds(pl.multiple_of(start - half, BLK), BLK), :] = part


def turned_kernel(ratio, own_ref, got_ref, factor_ref, out_ref):
    block_r = out_ref.shape[0]
    half = own_ref.shape[0]
    low = lax.rem(lax.axis_index("row"), ratio)
    total = None
    for j in range(ratio):
        first = pl.multiple_of((low ^ j) * block_r, block_r)
        at = j * block_r
        part = own_ref[at:at + block_r, :] if at < half else got_ref[at - half:at - half + block_r, :]
        term = jnp.dot(
            factor_ref[:, pl.ds(first, block_r)], part, preferred_element_type=jnp.float32)
        total = term if total is None else total + term
    out_ref[...] = total.astype(jnp.bfloat16)


def backward_kernel(
    rows_n, cols_n, size_ref, blocks_ref, own_ref, got_ref, forward_ref, uoff_ref, uinv_ref,
    leaf_hbm, rows_hbm,
    coupled_v, residue_v, solved_v, rows_v, sems,
):
    width = forward_ref.shape[0]
    tiles = width // TILE
    half = own_ref.shape[0]
    block_r = rows_v.shape[0]
    ratio = rows_n // cols_n
    size = size_ref[0]
    me = lax.axis_index("col")
    low = lax.rem(lax.axis_index("row"), ratio)

    def solved_at(first, count):
        unit = lax.div(first, block_r)
        place = place_of(lax.div(unit, ratio), me, cols_n) * ratio + (lax.rem(unit, ratio) ^ low)
        start = place * block_r + lax.rem(first, block_r)
        inside = start < half
        near = pl.multiple_of(jnp.where(inside, start, 0), BLK)
        far = pl.multiple_of(jnp.where(inside, 0, start - half), BLK)
        return jnp.where(inside, own_ref[pl.ds(near, count), :], got_ref[pl.ds(far, count), :])

    rows_v[...] = solved_at(lax.axis_index("row") * block_r, block_r)
    rows_copy = pltpu.make_async_copy(rows_v, rows_hbm, sems.at[tiles])
    rows_copy.start()
    for k in range(KB):
        coupled_v[pl.ds(k * BLK, BLK), :] = solved_at(blocks_ref[0, k] * BLK, BLK)

    copies = []
    for i in reversed(range(tiles)):
        rows = pl.ds(i * TILE, TILE)
        live = pl.ds(i * TILE, width - i * TILE)
        term = jnp.dot(uoff_ref[0, rows, :], coupled_v[...], preferred_element_type=jnp.float32)
        at = lax.broadcasted_iota(jnp.int32, term.shape, 0) + i * TILE
        residue = forward_ref[rows, :].astype(jnp.float32) - term
        residue_v[rows, :] = jnp.where(at < size, residue, 0.0).astype(jnp.bfloat16)
        tile = jnp.dot(
            uinv_ref[0, rows, live], residue_v[live, :], preferred_element_type=jnp.float32)
        solved_v[rows, :] = jnp.where(at < size, tile, 0.0).astype(jnp.bfloat16)
        copy = pltpu.make_async_copy(solved_v.at[rows], leaf_hbm.at[0, rows], sems.at[i])
        copy.start()
        copies.append(copy)
    for copy in copies:
        copy.wait()
    rows_copy.wait()


def shards(
    rows_n,
    cols_n,
    rhs_leaf,
    rhs_sep,
    leaf_sizes,
    off_blocks,
    linv_leaf,
    uinv_leaf,
    l_off,
    u_off,
    linv_sep,
    uinv_sep,
):
    width, columns = rhs_leaf.shape[1:]
    share = rhs_sep.shape[0]
    sep = share * cols_n
    block_r = sep // rows_n
    ratio = rows_n // cols_n
    tiles = width // TILE
    bf16 = jnp.bfloat16
    smem = pl.BlockSpec(memory_space=pltpu.SMEM)
    vmem = pl.BlockSpec(memory_space=pltpu.VMEM)
    any_space = pl.BlockSpec(memory_space=pl.ANY)
    in_vmem = functools.partial(pltpu.with_memory_space_constraint, memory_space=pltpu.VMEM)
    in_smem = functools.partial(pltpu.with_memory_space_constraint, memory_space=pltpu.SMEM)
    in_hbm = functools.partial(pltpu.with_memory_space_constraint, memory_space=pltpu.HBM)

    pairs = []
    for r in range(rows_n):
        for c in range(r // ratio, cols_n):
            to_r, to_c = c * ratio + r % ratio, r // ratio
            pairs.append((r * cols_n + c, to_r * cols_n + to_c))
    turned = lax.ppermute(uinv_sep, ("row", "col"), pairs)

    forward, keep, send, size, blocks = pl.pallas_call(
        functools.partial(forward_kernel, cols_n),
        out_shape=[
            pltpu.VMEM((width, columns), bf16),
            pltpu.VMEM((sep // 2, columns), bf16),
            pltpu.VMEM((sep // 2, columns), bf16),
            pltpu.SMEM((1,), jnp.int32),
            pltpu.SMEM((1, KB), jnp.int32),
        ],
        in_specs=[smem] + [any_space] * 4,
        out_specs=[vmem, vmem, vmem, smem, smem],
        scratch_shapes=[
            pltpu.VMEM((width, columns), bf16),
            pltpu.VMEM((width, width), bf16),
            pltpu.VMEM((KB * BLK, width), bf16),
            pltpu.VMEM((KB * BLK, columns), jnp.float32),
            pltpu.SemaphoreType.DMA((2 * tiles + 2,)),
        ],
        compiler_params=pltpu.CompilerParams(vmem_limit_bytes=24 * 2**20),
        cost_estimate=pl.CostEstimate(
            flops=900_000_000, bytes_accessed=8_000_000, transcendentals=0),
        name="leaf_forward",
    )(
        leaf_sizes, in_hbm(off_blocks), in_hbm(rhs_leaf), in_hbm(linv_leaf),
        in_hbm(l_off),
    )
    keep, send, turned = lax.optimization_barrier((keep, send, turned))
    bit = 1
    while bit < cols_n:
        got = swap(send, "col", cols_n, bit)
        bit *= 2
        if bit < cols_n:
            part = keep.shape[0] // 2
            send = add(keep[part:], got[part:])
            keep = add(keep[:part], got[:part])
        else:
            keep = add(keep, got)
    bit = 1
    while bit < rows_n:
        keep = add(keep, swap(keep, "row", rows_n, bit))
        bit *= 2
    sep_rhs = (rhs_sep.astype(jnp.float32) - keep.astype(jnp.float32)).astype(bf16)

    own = jnp.dot(linv_sep, sep_rhs, preferred_element_type=jnp.float32).astype(bf16)
    bit = 1
    while bit < cols_n:
        own = add(own, swap(own, "col", cols_n, bit))
        bit *= 2
    bit = 1
    while bit < ratio:
        got = swap(own, "row", rows_n, bit)
        bit *= 2
        if bit < ratio:
            own = jnp.concatenate([own, got], 0)
    own = pl.pallas_call(
        functools.partial(turned_kernel, ratio),
        out_shape=pltpu.VMEM((block_r, columns), bf16),
        in_specs=[vmem] * 3,
        out_specs=vmem,
        compiler_params=pltpu.CompilerParams(vmem_limit_bytes=4 * 2**20),
        name="separator_backward",
    )(in_vmem(own), in_vmem(got), in_vmem(turned))
    bit = ratio
    while bit < rows_n:
        own = add(own, swap(own, "row", rows_n, bit))
        bit *= 2
    bit = 1
    while bit < ratio:
        own = jnp.concatenate([own, swap(own, "row", rows_n, bit)], 0)
        bit *= 2
    bit = cols_n // 2
    while bit >= 1:
        got = swap(own, "col", cols_n, bit)
        if bit > 1:
            own = jnp.concatenate([own, got], 0)
        bit //= 2

    solved_leaf, solved_rows = pl.pallas_call(
        functools.partial(backward_kernel, rows_n, cols_n),
        out_shape=[
            jax.ShapeDtypeStruct((1, width, columns), bf16),
            jax.ShapeDtypeStruct((block_r, columns), bf16),
        ],
        in_specs=[smem, smem, vmem, vmem, vmem, vmem, vmem],
        out_specs=[any_space, any_space],
        scratch_shapes=[
            pltpu.VMEM((KB * BLK, columns), bf16),
            pltpu.VMEM((width, columns), bf16),
            pltpu.VMEM((width, columns), bf16),
            pltpu.VMEM((block_r, columns), bf16),
            pltpu.SemaphoreType.DMA((tiles + 1,)),
        ],
        compiler_params=pltpu.CompilerParams(vmem_limit_bytes=24 * 2**20),
        cost_estimate=pl.CostEstimate(
            flops=900_000_000, bytes_accessed=8_000_000, transcendentals=0),
        name="leaf_backward",
    )(
        in_smem(size), in_smem(blocks), in_vmem(own), in_vmem(got), in_vmem(forward),
        in_vmem(u_off), in_vmem(uinv_leaf),
    )
    return (solved_leaf, solved_rows)


def solution(mesh):
    placed = (
        P(("row", "col"), None, None),
        P("col", None),
        P(("row", "col")),
        P(("row", "col"), None),
        P(("row", "col"), None, None),
        P(("row", "col"), None, None),
        P(("row", "col"), None, None),
        P(("row", "col"), None, None),
        P("row", "col"),
        P("row", "col"),
    )
    return jax.shard_map(
        functools.partial(shards, mesh.shape["row"], mesh.shape["col"]),
        mesh=mesh,
        in_specs=placed,
        out_specs=(P(("row", "col"), None, None), P("row", None)),
        check_vma=False,
    )
```

```python
import functools

import jax
import jax.numpy as jnp
from jax import lax
from jax.experimental import pallas as pl
from jax.experimental.pallas import tpu as pltpu
from jax.sharding import PartitionSpec as P

BLK = 128
KB = 4
TILE = 256


def swap(x, axis, size, bit):
    return lax.ppermute(x, axis, [(i, i ^ bit) for i in range(size)])


def add(a, b):
    return (a.astype(jnp.float32) + b.astype(jnp.float32)).astype(jnp.bfloat16)


def place_of(share, me, size):
    apart = share ^ me
    place, bit = 0, 1
    while bit < size:
        place = place * 2 + lax.rem(lax.div(apart, bit), 2)
        bit *= 2
    return place


def reversed_bits(index, size):
    out, bit = 0, 1
    while bit < size:
        out = out * 2 + (index // bit) % 2
        bit *= 2
    return out


def forward_kernel(
    cols_n, size_in, blocks_hbm, rhs_hbm, linv_hbm, loff_hbm,
    forward_ref, keep_ref, send_ref, size_ref, blocks_ref,
    rhs_v, linv_v, loff_v, total_v, sems,
):
    width = rhs_v.shape[0]
    tiles = width // TILE
    half = keep_ref.shape[0]
    per_share = 2 * half // cols_n // BLK
    me = lax.axis_index("col")

    copies = [pltpu.make_async_copy(rhs_hbm.at[0], rhs_v, sems.at[0])]
    for i in range(tiles):
        rows = pl.ds(i * TILE, TILE)
        live = pl.ds(0, (i + 1) * TILE)
        copies.append(pltpu.make_async_copy(
            linv_hbm.at[0, rows, live], linv_v.at[rows, live], sems.at[1 + 2 * i]))
        copies.append(pltpu.make_async_copy(
            loff_hbm.at[0, :, rows], loff_v.at[:, rows], sems.at[2 + 2 * i]))
    copies.append(pltpu.make_async_copy(blocks_hbm, blocks_ref, sems.at[1 + 2 * tiles]))
    ahead = 6
    for copy in copies[:ahead]:
        copy.start()

    def arrive(n):
        copies[n].wait()
        if n + ahead < len(copies):
            copies[n + ahead].start()

    size = size_in[0]
    size_ref[0] = size
    keep_ref[...] = jnp.zeros_like(keep_ref)
    send_ref[...] = jnp.zeros_like(send_ref)
    arrive(0)
    for i in range(tiles):
        rows = pl.ds(i * TILE, TILE)
        live = pl.ds(0, (i + 1) * TILE)
        at = lax.broadcasted_iota(jnp.int32, (TILE, rhs_v.shape[1]), 0) + i * TILE
        rhs_v[rows, :] = jnp.where(at < size, rhs_v[rows, :], jnp.zeros_like(rhs_v[rows, :]))
        arrive(1 + 2 * i)
        tile = jnp.dot(linv_v[rows, live], rhs_v[live, :], preferred_element_type=jnp.float32)
        forward = jnp.where(at < size, tile, 0.0).astype(jnp.bfloat16)
        forward_ref[rows, :] = forward
        arrive(2 + 2 * i)
        term = jnp.dot(loff_v[:, rows], forward, preferred_element_type=jnp.float32)
        if i == 0:
            total_v[...] = term
        else:
            total_v[...] += term

    copies[-1].wait()
    for k in range(KB):
        block = blocks_ref[0, k]
        share = lax.div(block, per_share)
        start = (place_of(share, me, cols_n) * per_share + lax.rem(block, per_share)) * BLK
        part = total_v[pl.ds(k * BLK, BLK), :].astype(jnp.bfloat16)

        @pl.when(start < half)
        def _():
            keep_ref[pl.ds(pl.multiple_of(start, BLK), BLK), :] = part

        @pl.when(start >= half)
        def _():
            send_ref[pl.ds(pl.multiple_of(start - half, BLK), BLK), :] = part


def turned_kernel(ratio, own_ref, got_ref, factor_ref, out_ref):
    block_r = out_ref.shape[0]
    half = own_ref.shape[0]
    low = lax.rem(lax.axis_index("row"), ratio)
    total = None
    for j in range(ratio):
        first = pl.multiple_of((low ^ j) * block_r, block_r)
        at = j * block_r
        part = own_ref[at:at + block_r, :] if at < half else got_ref[at - half:at - half + block_r, :]
        term = jnp.dot(
            factor_ref[:, pl.ds(first, block_r)], part, preferred_element_type=jnp.float32)
        total = term if total is None else total + term
    out_ref[...] = total.astype(jnp.bfloat16)


def ahead_kernel(tiles_here, size_ref, uoff_ref, forward_ref, uinv_hbm, inner_ref, outer_ref,
                 both_v, uinv_v, sems):
    width, inner = uoff_ref.shape[1:]
    size = size_ref[0]
    copies = []
    for n, i in enumerate(tiles_here):
        copies.append(pltpu.make_async_copy(
            uinv_hbm.at[0, pl.ds(i * TILE, TILE), pl.ds(i * TILE, width - i * TILE)],
            uinv_v.at[pl.ds(n * TILE, TILE), pl.ds(i * TILE, width - i * TILE)],
            sems.at[n]))
        copies[-1].start()
    for j in range(min(tiles_here), width // TILE):
        rows = pl.ds(j * TILE, TILE)
        block = uoff_ref[0, rows, :]
        at = lax.broadcasted_iota(jnp.int32, block.shape, 0) + j * TILE
        both_v[rows, 0:inner] = jnp.where(at < size, block, jnp.zeros_like(block))
        both_v[rows, inner:] = forward_ref[rows, :]
    for n, i in enumerate(tiles_here):
        rows = pl.ds(n * TILE, TILE)
        live = pl.ds(i * TILE, width - i * TILE)
        copies[n].wait()
        out = jnp.dot(uinv_v[rows, live], both_v[live, :], preferred_element_type=jnp.float32)
        inner_ref[rows, :] = out[:, :inner].astype(jnp.bfloat16)
        outer_ref[rows, :] = out[:, inner:]


def backward_kernel(rows_n, cols_n, groups, size_ref, blocks_ref, own_ref, got_ref, *rest):
    count = len(groups)
    inner_refs, outer_refs = rest[:count], rest[count:2 * count]
    leaf_hbm, rows_hbm, coupled_v, solved_v, rows_v, sems = rest[2 * count:]
    tiles = solved_v.shape[0] // TILE
    half = own_ref.shape[0]
    block_r = rows_v.shape[0]
    ratio = rows_n // cols_n
    size = size_ref[0]
    me = lax.axis_index("col")
    low = lax.rem(lax.axis_index("row"), ratio)

    def solved_at(first, length):
        unit = lax.div(first, block_r)
        where = reversed_bits(lax.div(unit, ratio), cols_n)
        place = place_of(where, me, cols_n) * ratio + (lax.rem(unit, ratio) ^ low)
        start = place * block_r + lax.rem(first, block_r)
        inside = start < half
        near = pl.multiple_of(jnp.where(inside, start, 0), BLK)
        far = pl.multiple_of(jnp.where(inside, 0, start - half), BLK)
        return jnp.where(inside, own_ref[pl.ds(near, length), :], got_ref[pl.ds(far, length), :])

    for k in range(KB):
        coupled_v[pl.ds(k * BLK, BLK), :] = solved_at(blocks_ref[0, k] * BLK, BLK)
    rows_v[...] = solved_at(lax.axis_index("row") * block_r, block_r)
    copies = [pltpu.make_async_copy(rows_v, rows_hbm, sems.at[tiles])]
    copies[0].start()
    for group, inner_ref, outer_ref in zip(groups, inner_refs, outer_refs):
        term = jnp.dot(inner_ref[...], coupled_v[...], preferred_element_type=jnp.float32)
        for n, i in enumerate(group):
            here = slice(n * TILE, (n + 1) * TILE)
            tile = outer_ref[here, :] - term[here, :]
            at = lax.broadcasted_iota(jnp.int32, tile.shape, 0) + i * TILE
            rows = pl.ds(i * TILE, TILE)
            solved_v[rows, :] = jnp.where(at < size, tile, 0.0).astype(jnp.bfloat16)
            copies.append(pltpu.make_async_copy(
                solved_v.at[rows], leaf_hbm.at[0, rows], sems.at[i]))
            copies[-1].start()
    for copy in copies:
        copy.wait()


def shards(
    rows_n,
    cols_n,
    rhs_leaf,
    rhs_sep,
    leaf_sizes,
    off_blocks,
    linv_leaf,
    uinv_leaf,
    l_off,
    u_off,
    linv_sep,
    uinv_sep,
):
    width, columns = rhs_leaf.shape[1:]
    share = rhs_sep.shape[0]
    sep = share * cols_n
    block_r = sep // rows_n
    ratio = rows_n // cols_n
    tiles = width // TILE
    bf16 = jnp.bfloat16
    smem = pl.BlockSpec(memory_space=pltpu.SMEM)
    vmem = pl.BlockSpec(memory_space=pltpu.VMEM)
    any_space = pl.BlockSpec(memory_space=pl.ANY)
    in_vmem = functools.partial(pltpu.with_memory_space_constraint, memory_space=pltpu.VMEM)
    in_smem = functools.partial(pltpu.with_memory_space_constraint, memory_space=pltpu.SMEM)
    in_hbm = functools.partial(pltpu.with_memory_space_constraint, memory_space=pltpu.HBM)

    pairs = []
    for r in range(rows_n):
        for c in range(r // ratio, cols_n):
            to_r, to_c = c * ratio + r % ratio, reversed_bits(r // ratio, cols_n)
            pairs.append((r * cols_n + c, to_r * cols_n + to_c))
    turned = lax.ppermute(uinv_sep, ("row", "col"), pairs)

    forward, keep, send, size, blocks = pl.pallas_call(
        functools.partial(forward_kernel, cols_n),
        out_shape=[
            pltpu.VMEM((width, columns), bf16),
            pltpu.VMEM((sep // 2, columns), bf16),
            pltpu.VMEM((sep // 2, columns), bf16),
            pltpu.SMEM((1,), jnp.int32),
            pltpu.SMEM((1, KB), jnp.int32),
        ],
        in_specs=[smem] + [any_space] * 4,
        out_specs=[vmem, vmem, vmem, smem, smem],
        scratch_shapes=[
            pltpu.VMEM((width, columns), bf16),
            pltpu.VMEM((width, width), bf16),
            pltpu.VMEM((KB * BLK, width), bf16),
            pltpu.VMEM((KB * BLK, columns), jnp.float32),
            pltpu.SemaphoreType.DMA((2 * tiles + 2,)),
        ],
        compiler_params=pltpu.CompilerParams(vmem_limit_bytes=24 * 2**20),
        cost_estimate=pl.CostEstimate(
            flops=900_000_000, bytes_accessed=8_000_000, transcendentals=0),
        name="leaf_forward",
    )(
        leaf_sizes, in_hbm(off_blocks), in_hbm(rhs_leaf), in_hbm(linv_leaf),
        in_hbm(l_off),
    )
    keep, send, turned = lax.optimization_barrier((keep, send, turned))
    tied = lax.optimization_barrier
    groups = [[0], [1]] + [[2 + j, tiles - 1 - j] for j in range((tiles - 2) // 2)]
    inner, outer = [], []

    def swap_beside(x, axis, count, bit):
        if len(inner) == len(groups):
            return swap(x, axis, count, bit)
        group = groups[len(inner)]
        x, factor = tied((x, uinv_leaf))
        got = swap(x, axis, count, bit)
        length = len(group) * TILE
        ahead = pl.pallas_call(
            functools.partial(ahead_kernel, group),
            out_shape=[
                pltpu.VMEM((length, u_off.shape[2]), bf16),
                pltpu.VMEM((length, columns), jnp.float32),
            ],
            in_specs=[smem, vmem, vmem, any_space],
            out_specs=[vmem, vmem],
            scratch_shapes=[
                pltpu.VMEM((width, u_off.shape[2] + columns), bf16),
                pltpu.VMEM((length, width), bf16),
                pltpu.SemaphoreType.DMA((len(group),)),
            ],
            compiler_params=pltpu.CompilerParams(vmem_limit_bytes=16 * 2**20),
            cost_estimate=pl.CostEstimate(
                flops=600_000_000, bytes_accessed=1_000_000, transcendentals=0),
            name="leaf_ahead",
        )(in_smem(size), in_vmem(u_off), in_vmem(forward), in_hbm(factor))
        got, *ahead = tied((got, *ahead))
        inner.append(ahead[0])
        outer.append(ahead[1])
        return got

    bit = 1
    while bit < cols_n:
        beside = swap if bit == 1 else swap_beside
        got = beside(send, "col", cols_n, bit)
        bit *= 2
        if bit < cols_n:
            part = keep.shape[0] // 2
            send = add(keep[part:], got[part:])
            keep = add(keep[:part], got[:part])
        else:
            keep = add(keep, got)
    bit = 1
    while bit < rows_n:
        keep = add(keep, swap_beside(keep, "row", rows_n, bit))
        bit *= 2
    sep_rhs = (rhs_sep.astype(jnp.float32) - keep.astype(jnp.float32)).astype(bf16)

    own = jnp.dot(linv_sep, sep_rhs, preferred_element_type=jnp.float32).astype(bf16)
    bit = 1
    while bit < cols_n:
        beside = swap if bit == 1 else swap_beside
        own = add(own, beside(own, "col", cols_n, bit))
        bit *= 2
    bit = 1
    while bit < ratio:
        got = swap(own, "row", rows_n, bit)
        bit *= 2
        if bit < ratio:
            own = jnp.concatenate([own, got], 0)
    own = pl.pallas_call(
        functools.partial(turned_kernel, ratio),
        out_shape=pltpu.VMEM((block_r, columns), bf16),
        in_specs=[vmem] * 3,
        out_specs=vmem,
        compiler_params=pltpu.CompilerParams(vmem_limit_bytes=4 * 2**20),
        name="separator_backward",
    )(in_vmem(own), in_vmem(got), in_vmem(turned))
    bit = ratio
    while bit < rows_n:
        own = add(own, swap(own, "row", rows_n, bit))
        bit *= 2
    bit = 1
    while bit < ratio:
        own = jnp.concatenate([own, swap(own, "row", rows_n, bit)], 0)
        bit *= 2
    bit = cols_n // 2
    while bit >= 1:
        got = swap(own, "col", cols_n, bit)
        if bit > 1:
            own = jnp.concatenate([own, got], 0)
        bit //= 2

    solved_leaf, solved_rows = pl.pallas_call(
        functools.partial(backward_kernel, rows_n, cols_n, groups),
        out_shape=[
            jax.ShapeDtypeStruct((1, width, columns), bf16),
            jax.ShapeDtypeStruct((block_r, columns), bf16),
        ],
        in_specs=[smem, smem] + [vmem] * (2 + 2 * len(groups)),
        out_specs=[any_space, any_space],
        scratch_shapes=[
            pltpu.VMEM((KB * BLK, columns), bf16),
            pltpu.VMEM((width, columns), bf16),
            pltpu.VMEM((block_r, columns), bf16),
            pltpu.SemaphoreType.DMA((tiles + 1,)),
        ],
        compiler_params=pltpu.CompilerParams(vmem_limit_bytes=16 * 2**20),
        cost_estimate=pl.CostEstimate(
            flops=270_000_000, bytes_accessed=4_000_000, transcendentals=0),
        name="leaf_backward",
    )(
        in_smem(size), in_smem(blocks), in_vmem(own), in_vmem(got),
        *map(in_vmem, inner), *map(in_vmem, outer),
    )
    return (solved_leaf, solved_rows)


def solution(mesh):
    placed = (
        P(("row", "col"), None, None),
        P("col", None),
        P(("row", "col")),
        P(("row", "col"), None),
        P(("row", "col"), None, None),
        P(("row", "col"), None, None),
        P(("row", "col"), None, None),
        P(("row", "col"), None, None),
        P("row", "col"),
        P("row", "col"),
    )
    return jax.shard_map(
        functools.partial(shards, mesh.shape["row"], mesh.shape["col"]),
        mesh=mesh,
        in_specs=placed,
        out_specs=(P(("row", "col"), None, None), P("row", None)),
        check_vma=False,
    )
```

```python
import functools

import jax
import jax.numpy as jnp
from jax import lax
from jax.experimental import pallas as pl
from jax.experimental.pallas import tpu as pltpu
from jax.sharding import PartitionSpec as P

BLK = 128
KB = 4
TILE = 256


def swap(x, axis, size, bit):
    return lax.ppermute(x, axis, [(i, i ^ bit) for i in range(size)])


def add(a, b):
    return (a.astype(jnp.float32) + b.astype(jnp.float32)).astype(jnp.bfloat16)


def place_of(share, me, size):
    apart = share ^ me
    place, bit = 0, 1
    while bit < size:
        place = place * 2 + lax.rem(lax.div(apart, bit), 2)
        bit *= 2
    return place


def forward_kernel(
    cols_n, size_in, blocks_hbm, rhs_hbm, linv_hbm, loff_hbm,
    forward_ref, keep_ref, send_ref, size_ref, blocks_ref,
    rhs_v, linv_v, loff_v, total_v, sems,
):
    width = rhs_v.shape[0]
    tiles = width // TILE
    half = keep_ref.shape[0]
    per_share = 2 * half // cols_n // BLK
    me = lax.axis_index("col")

    step = 2 * TILE
    copies = [pltpu.make_async_copy(rhs_hbm.at[0], rhs_v, sems.at[0])]
    for i in range(tiles):
        rows = pl.ds(i * TILE, TILE)
        live = pl.ds(0, (i + 1) * TILE)
        copies.append(pltpu.make_async_copy(
            linv_hbm.at[0, rows, live], linv_v.at[rows, live], sems.at[len(copies)]))
        if i % 2:
            cols = pl.ds((i - 1) * TILE, step)
            copies.append(pltpu.make_async_copy(
                loff_hbm.at[0, :, cols], loff_v.at[:, cols], sems.at[len(copies)]))
    copies.append(pltpu.make_async_copy(blocks_hbm, blocks_ref, sems.at[len(copies)]))
    ahead = 7
    for copy in copies[:ahead]:
        copy.start()

    def arrive(n):
        copies[n].wait()
        if n + ahead < len(copies):
            copies[n + ahead].start()

    def update(s):
        cols = pl.ds(s * step, step)
        return jnp.dot(loff_v[:, cols], forward_ref[cols, :], preferred_element_type=jnp.float32)

    size = size_in[0]
    size_ref[0] = size
    keep_ref[...] = jnp.zeros_like(keep_ref)
    send_ref[...] = jnp.zeros_like(send_ref)
    arrive(0)
    at = lax.broadcasted_iota(jnp.int32, rhs_v.shape, 0)
    rhs_v[...] = jnp.where(at < size, rhs_v[...], jnp.zeros_like(rhs_v))
    for s in range(tiles // 2):
        if s >= 1:
            arrive(3 * s)
        arrive(3 * s + 1)
        arrive(3 * s + 2)
        if s == 1:
            total_v[...] = update(0)
        elif s > 1:
            total_v[...] += update(s - 1)
        for i in (2 * s, 2 * s + 1):
            rows = pl.ds(i * TILE, TILE)
            live = pl.ds(0, (i + 1) * TILE)
            tile = jnp.dot(linv_v[rows, live], rhs_v[live, :], preferred_element_type=jnp.float32)
            at = lax.broadcasted_iota(jnp.int32, tile.shape, 0) + i * TILE
            forward_ref[rows, :] = jnp.where(at < size, tile, 0.0).astype(jnp.bfloat16)
    arrive(3 * (tiles // 2))
    total_v[...] += update(tiles // 2 - 1)

    copies[-1].wait()
    for k in range(KB):
        block = blocks_ref[0, k]
        share = lax.div(block, per_share)
        start = (place_of(share, me, cols_n) * per_share + lax.rem(block, per_share)) * BLK
        part = total_v[pl.ds(k * BLK, BLK), :].astype(jnp.bfloat16)

        @pl.when(start < half)
        def _():
            keep_ref[pl.ds(pl.multiple_of(start, BLK), BLK), :] = part

        @pl.when(start >= half)
        def _():
            send_ref[pl.ds(pl.multiple_of(start - half, BLK), BLK), :] = part


def separator_kernel(ratio, own_ref, got_ref, factor_ref, out_ref):
    block_r = out_ref.shape[0]
    half = own_ref.shape[0]
    low = lax.rem(lax.axis_index("row"), ratio)
    total = None
    for j in range(ratio):
        first = pl.multiple_of((low ^ j) * block_r, block_r)
        at = j * block_r
        part = own_ref[at:at + block_r, :] if at < half else got_ref[at - half:at - half + block_r, :]
        term = jnp.dot(
            factor_ref[:, pl.ds(first, block_r)], part, preferred_element_type=jnp.float32)
        total = term if total is None else total + term
    out_ref[...] = total.astype(jnp.bfloat16)


def ahead_kernel(tiles_here, size_ref, uoff_ref, forward_ref, uinv_hbm, inner_ref, outer_ref,
                 both_v, uinv_v, sems):
    width, inner = uoff_ref.shape[1:]
    size = size_ref[0]
    copies = []
    for n, i in enumerate(tiles_here):
        copies.append(pltpu.make_async_copy(
            uinv_hbm.at[0, pl.ds(i * TILE, TILE), pl.ds(i * TILE, width - i * TILE)],
            uinv_v.at[pl.ds(n * TILE, TILE), pl.ds(i * TILE, width - i * TILE)],
            sems.at[n]))
        copies[-1].start()
    for j in range(min(tiles_here), width // TILE):
        rows = pl.ds(j * TILE, TILE)
        block = uoff_ref[0, rows, :]
        at = lax.broadcasted_iota(jnp.int32, block.shape, 0) + j * TILE
        both_v[rows, 0:inner] = jnp.where(at < size, block, jnp.zeros_like(block))
        both_v[rows, inner:] = forward_ref[rows, :]
    for n, i in enumerate(tiles_here):
        rows = pl.ds(n * TILE, TILE)
        live = pl.ds(i * TILE, width - i * TILE)
        copies[n].wait()
        out = jnp.dot(uinv_v[rows, live], both_v[live, :], preferred_element_type=jnp.float32)
        inner_ref[rows, :] = out[:, :inner].astype(jnp.bfloat16)
        outer_ref[rows, :] = out[:, inner:]


def backward_kernel(rows_n, groups, size_ref, blocks_ref, own_ref, got_ref, *rest):
    count = len(groups)
    inner_refs, outer_refs = rest[:count], rest[count:2 * count]
    leaf_hbm, rows_hbm, coupled_v, solved_v, sems = rest[2 * count:]
    tiles = solved_v.shape[0] // TILE
    half = own_ref.shape[0]
    block_r = rows_hbm.shape[0]
    size = size_ref[0]
    row = lax.axis_index("row")

    def solved_at(first):
        start = place_of(lax.div(first, block_r), row, rows_n) * block_r + lax.rem(first, block_r)
        inside = start < half
        near = pl.multiple_of(jnp.where(inside, start, 0), BLK)
        far = pl.multiple_of(jnp.where(inside, 0, start - half), BLK)
        return jnp.where(inside, own_ref[pl.ds(near, BLK), :], got_ref[pl.ds(far, BLK), :])

    for k in range(KB):
        coupled_v[pl.ds(k * BLK, BLK), :] = solved_at(blocks_ref[0, k] * BLK)
    copies = [pltpu.make_async_copy(own_ref.at[pl.ds(0, block_r)], rows_hbm, sems.at[tiles])]
    copies[0].start()
    for group, inner_ref, outer_ref in zip(groups, inner_refs, outer_refs):
        term = jnp.dot(inner_ref[...], coupled_v[...], preferred_element_type=jnp.float32)
        for n, i in enumerate(group):
            here = slice(n * TILE, (n + 1) * TILE)
            tile = outer_ref[here, :] - term[here, :]
            at = lax.broadcasted_iota(jnp.int32, tile.shape, 0) + i * TILE
            rows = pl.ds(i * TILE, TILE)
            solved_v[rows, :] = jnp.where(at < size, tile, 0.0).astype(jnp.bfloat16)
            copies.append(pltpu.make_async_copy(
                solved_v.at[rows], leaf_hbm.at[0, rows], sems.at[i]))
            copies[-1].start()
    for copy in copies:
        copy.wait()


def shards(
    rows_n,
    cols_n,
    rhs_leaf,
    rhs_sep,
    leaf_sizes,
    off_blocks,
    linv_leaf,
    uinv_leaf,
    l_off,
    u_off,
    linv_sep,
    uinv_sep,
):
    width, columns = rhs_leaf.shape[1:]
    share = rhs_sep.shape[0]
    sep = share * cols_n
    block_r = sep // rows_n
    ratio = rows_n // cols_n
    tiles = width // TILE
    bf16 = jnp.bfloat16
    smem = pl.BlockSpec(memory_space=pltpu.SMEM)
    vmem = pl.BlockSpec(memory_space=pltpu.VMEM)
    any_space = pl.BlockSpec(memory_space=pl.ANY)
    in_vmem = functools.partial(pltpu.with_memory_space_constraint, memory_space=pltpu.VMEM)
    in_smem = functools.partial(pltpu.with_memory_space_constraint, memory_space=pltpu.SMEM)
    in_hbm = functools.partial(pltpu.with_memory_space_constraint, memory_space=pltpu.HBM)

    forward, keep, send, size, blocks = pl.pallas_call(
        functools.partial(forward_kernel, cols_n),
        out_shape=[
            pltpu.VMEM((width, columns), bf16),
            pltpu.VMEM((sep // 2, columns), bf16),
            pltpu.VMEM((sep // 2, columns), bf16),
            pltpu.SMEM((1,), jnp.int32),
            pltpu.SMEM((1, KB), jnp.int32),
        ],
        in_specs=[smem] + [any_space] * 4,
        out_specs=[vmem, vmem, vmem, smem, smem],
        scratch_shapes=[
            pltpu.VMEM((width, columns), bf16),
            pltpu.VMEM((width, width), bf16),
            pltpu.VMEM((KB * BLK, width), bf16),
            pltpu.VMEM((KB * BLK, columns), jnp.float32),
            pltpu.SemaphoreType.DMA((2 * tiles + 2,)),
        ],
        compiler_params=pltpu.CompilerParams(vmem_limit_bytes=24 * 2**20),
        cost_estimate=pl.CostEstimate(
            flops=900_000_000, bytes_accessed=8_000_000, transcendentals=0),
        name="leaf_forward",
    )(
        leaf_sizes, in_hbm(off_blocks), in_hbm(rhs_leaf), in_hbm(linv_leaf),
        in_hbm(l_off),
    )
    tied = lax.optimization_barrier
    groups = [[0], [1]] + [[2 + j, tiles - 1 - j] for j in range((tiles - 2) // 2)]
    inner, outer = [], []

    def swap_beside(x, axis, count, bit):
        if len(inner) == len(groups):
            return swap(x, axis, count, bit)
        group = groups[len(inner)]
        x, factor = tied((x, uinv_leaf))
        got = swap(x, axis, count, bit)
        length = len(group) * TILE
        ahead = pl.pallas_call(
            functools.partial(ahead_kernel, group),
            out_shape=[
                pltpu.VMEM((length, u_off.shape[2]), bf16),
                pltpu.VMEM((length, columns), jnp.float32),
            ],
            in_specs=[smem, vmem, vmem, any_space],
            out_specs=[vmem, vmem],
            scratch_shapes=[
                pltpu.VMEM((width, u_off.shape[2] + columns), bf16),
                pltpu.VMEM((length, width), bf16),
                pltpu.SemaphoreType.DMA((len(group),)),
            ],
            compiler_params=pltpu.CompilerParams(vmem_limit_bytes=16 * 2**20),
            cost_estimate=pl.CostEstimate(
                flops=600_000_000, bytes_accessed=1_000_000, transcendentals=0),
            name="leaf_ahead",
        )(in_smem(size), in_vmem(u_off), in_vmem(forward), in_hbm(factor))
        got, *ahead = tied((got, *ahead))
        inner.append(ahead[0])
        outer.append(ahead[1])
        return got

    bit = 1
    while bit < cols_n:
        beside = swap if bit == 1 else swap_beside
        got = beside(send, "col", cols_n, bit)
        bit *= 2
        if bit < cols_n:
            part = keep.shape[0] // 2
            send = add(keep[part:], got[part:])
            keep = add(keep[:part], got[:part])
        else:
            keep = add(keep, got)
    bit = 1
    while bit < rows_n:
        keep = add(keep, swap_beside(keep, "row", rows_n, bit))
        bit *= 2
    sep_rhs = (rhs_sep.astype(jnp.float32) - keep.astype(jnp.float32)).astype(bf16)

    own = jnp.dot(linv_sep, sep_rhs, preferred_element_type=jnp.float32).astype(bf16)
    bit = 1
    while bit < cols_n:
        beside = swap if bit == 1 else swap_beside
        own = add(own, beside(own, "col", cols_n, bit))
        bit *= 2
    pairs = []
    for r in range(rows_n):
        for c in range(cols_n):
            pairs.append((r * cols_n + c, (c * ratio + r % ratio) * cols_n + r // ratio))
    own = lax.ppermute(own, ("row", "col"), pairs)
    bit = 1
    while bit < ratio:
        got = swap(own, "row", rows_n, bit)
        bit *= 2
        if bit < ratio:
            own = jnp.concatenate([own, got], 0)
    own = pl.pallas_call(
        functools.partial(separator_kernel, ratio),
        out_shape=pltpu.VMEM((block_r, columns), bf16),
        in_specs=[vmem] * 3,
        out_specs=vmem,
        compiler_params=pltpu.CompilerParams(vmem_limit_bytes=4 * 2**20),
        name="separator_backward",
    )(in_vmem(own), in_vmem(got), in_vmem(uinv_sep))
    bit = 1
    while bit < cols_n:
        own = add(own, swap(own, "col", cols_n, bit))
        bit *= 2
    bit = rows_n // 2
    while bit >= 1:
        got = swap(own, "row", rows_n, bit)
        if bit > 1:
            own = jnp.concatenate([own, got], 0)
        bit //= 2

    solved_leaf, solved_rows = pl.pallas_call(
        functools.partial(backward_kernel, rows_n, groups),
        out_shape=[
            jax.ShapeDtypeStruct((1, width, columns), bf16),
            jax.ShapeDtypeStruct((block_r, columns), bf16),
        ],
        in_specs=[smem, smem] + [vmem] * (2 + 2 * len(groups)),
        out_specs=[any_space, any_space],
        scratch_shapes=[
            pltpu.VMEM((KB * BLK, columns), bf16),
            pltpu.VMEM((width, columns), bf16),
            pltpu.SemaphoreType.DMA((tiles + 1,)),
        ],
        compiler_params=pltpu.CompilerParams(vmem_limit_bytes=16 * 2**20),
        cost_estimate=pl.CostEstimate(
            flops=270_000_000, bytes_accessed=4_000_000, transcendentals=0),
        name="leaf_backward",
    )(
        in_smem(size), in_smem(blocks), in_vmem(own), in_vmem(got),
        *map(in_vmem, inner), *map(in_vmem, outer),
    )
    return (solved_leaf, solved_rows)


def solution(mesh):
    placed = (
        P(("row", "col"), None, None),
        P("col", None),
        P(("row", "col")),
        P(("row", "col"), None),
        P(("row", "col"), None, None),
        P(("row", "col"), None, None),
        P(("row", "col"), None, None),
        P(("row", "col"), None, None),
        P("row", "col"),
        P("row", "col"),
    )
    return jax.shard_map(
        functools.partial(shards, mesh.shape["row"], mesh.shape["col"]),
        mesh=mesh,
        in_specs=placed,
        out_specs=(P(("row", "col"), None, None), P("row", None)),
        check_vma=False,
    )
```

```python
import functools

import jax
import jax.numpy as jnp
from jax import lax
from jax.experimental import pallas as pl
from jax.experimental.pallas import tpu as pltpu
from jax.sharding import PartitionSpec as P

BLK = 128
KB = 4
TILE = 256


def swap(x, axis, size, bit):
    return lax.ppermute(x, axis, [(i, i ^ bit) for i in range(size)])


def add(a, b):
    return (a.astype(jnp.float32) + b.astype(jnp.float32)).astype(jnp.bfloat16)


def place_of(share, me, size):
    apart = share ^ me
    place, bit = 0, 1
    while bit < size:
        place = place * 2 + lax.rem(lax.div(apart, bit), 2)
        bit *= 2
    return place


def forward_kernel(
    cols_n, ratio, size_in, blocks_hbm, rhs_hbm, linv_hbm, loff_hbm, usep_hbm,
    forward_ref, keep_ref, send_ref, size_ref, blocks_ref, *rest,
):
    piece_refs, (rhs_v, linv_v, loff_v, total_v, sems) = rest[:-5], rest[-5:]
    width = rhs_v.shape[0]
    tiles = width // TILE
    half = keep_ref.shape[0]
    per_share = 2 * half // cols_n // BLK
    me = lax.axis_index("col")

    step = 2 * TILE
    copies = [pltpu.make_async_copy(rhs_hbm.at[0], rhs_v, sems.at[0])]
    for i in range(tiles):
        rows = pl.ds(i * TILE, TILE)
        live = pl.ds(0, (i + 1) * TILE)
        copies.append(pltpu.make_async_copy(
            linv_hbm.at[0, rows, live], linv_v.at[rows, live], sems.at[len(copies)]))
        if i % 2:
            cols = pl.ds((i - 1) * TILE, step)
            copies.append(pltpu.make_async_copy(
                loff_hbm.at[0, :, cols], loff_v.at[:, cols], sems.at[len(copies)]))
    copies.append(pltpu.make_async_copy(blocks_hbm, blocks_ref, sems.at[len(copies)]))
    late = len(copies)
    parts = cols_n // ratio
    unit, block_r = piece_refs[0].shape
    for p, piece_ref in enumerate(piece_refs):
        first = pl.multiple_of((lax.rem(me, parts) ^ (p % parts)) * unit, unit)
        across = pl.multiple_of((lax.div(me, parts) ^ (p // parts)) * block_r, block_r)
        copies.append(pltpu.make_async_copy(
            usep_hbm.at[pl.ds(first, unit), pl.ds(across, block_r)], piece_ref,
            sems.at[len(copies)]))
    ahead = 7
    for copy in copies[:ahead]:
        copy.start()

    def arrive(n):
        copies[n].wait()
        if n + ahead < len(copies):
            copies[n + ahead].start()

    def update(s):
        cols = pl.ds(s * step, step)
        return jnp.dot(loff_v[:, cols], forward_ref[cols, :], preferred_element_type=jnp.float32)

    size = size_in[0]
    size_ref[0] = size
    keep_ref[...] = jnp.zeros_like(keep_ref)
    send_ref[...] = jnp.zeros_like(send_ref)
    arrive(0)
    at = lax.broadcasted_iota(jnp.int32, rhs_v.shape, 0)
    rhs_v[...] = jnp.where(at < size, rhs_v[...], jnp.zeros_like(rhs_v))
    for s in range(tiles // 2):
        if s >= 1:
            arrive(3 * s)
        arrive(3 * s + 1)
        arrive(3 * s + 2)
        if s == 1:
            total_v[...] = update(0)
        elif s > 1:
            total_v[...] += update(s - 1)
        for i in (2 * s, 2 * s + 1):
            rows = pl.ds(i * TILE, TILE)
            live = pl.ds(0, (i + 1) * TILE)
            tile = jnp.dot(linv_v[rows, live], rhs_v[live, :], preferred_element_type=jnp.float32)
            at = lax.broadcasted_iota(jnp.int32, tile.shape, 0) + i * TILE
            forward_ref[rows, :] = jnp.where(at < size, tile, 0.0).astype(jnp.bfloat16)
    arrive(3 * (tiles // 2))
    total_v[...] += update(tiles // 2 - 1)

    for n in range(late - 1, len(copies)):
        arrive(n)
    for k in range(KB):
        block = blocks_ref[0, k]
        share = lax.div(block, per_share)
        start = (place_of(share, me, cols_n) * per_share + lax.rem(block, per_share)) * BLK
        part = total_v[pl.ds(k * BLK, BLK), :].astype(jnp.bfloat16)

        @pl.when(start < half)
        def _():
            keep_ref[pl.ds(pl.multiple_of(start, BLK), BLK), :] = part

        @pl.when(start >= half)
        def _():
            send_ref[pl.ds(pl.multiple_of(start - half, BLK), BLK), :] = part


def separator_kernel(cols_n, ratio, own_ref, got_ref, *rest):
    moved_refs, out_ref = rest[:-1], rest[-1]
    block_r = moved_refs[0].shape[1]
    half = own_ref.shape[0]
    parts = cols_n // ratio
    row, col = lax.axis_index("row"), lax.axis_index("col")
    total = None
    for p, moved_ref in enumerate(moved_refs):
        source = (lax.rem(row, ratio) ^ (p // parts)) * parts + (lax.rem(col, parts) ^ (p % parts))
        start = place_of(source, lax.div(row, ratio), cols_n) * block_r
        inside = start < half
        near = pl.multiple_of(jnp.where(inside, start, 0), block_r)
        far = pl.multiple_of(jnp.where(inside, 0, start - half), block_r)
        part = jnp.where(
            inside, own_ref[pl.ds(near, block_r), :], got_ref[pl.ds(far, block_r), :])
        term = jnp.dot(moved_ref[...], part, preferred_element_type=jnp.float32)
        total = term if total is None else total + term
    out_ref[...] = total.astype(jnp.bfloat16)


def ahead_kernel(tiles_here, size_ref, uoff_ref, forward_ref, uinv_hbm, inner_ref, outer_ref,
                 both_v, uinv_v, sems):
    width, inner = uoff_ref.shape[1:]
    size = size_ref[0]
    copies = []
    for n, i in enumerate(tiles_here):
        copies.append(pltpu.make_async_copy(
            uinv_hbm.at[0, pl.ds(i * TILE, TILE), pl.ds(i * TILE, width - i * TILE)],
            uinv_v.at[pl.ds(n * TILE, TILE), pl.ds(i * TILE, width - i * TILE)],
            sems.at[n]))
        copies[-1].start()
    for j in range(min(tiles_here), width // TILE):
        rows = pl.ds(j * TILE, TILE)
        block = uoff_ref[0, rows, :]
        at = lax.broadcasted_iota(jnp.int32, block.shape, 0) + j * TILE
        both_v[rows, 0:inner] = jnp.where(at < size, block, jnp.zeros_like(block))
        both_v[rows, inner:] = forward_ref[rows, :]
    for n, i in enumerate(tiles_here):
        rows = pl.ds(n * TILE, TILE)
        live = pl.ds(i * TILE, width - i * TILE)
        copies[n].wait()
        out = jnp.dot(uinv_v[rows, live], both_v[live, :], preferred_element_type=jnp.float32)
        inner_ref[rows, :] = out[:, :inner].astype(jnp.bfloat16)
        outer_ref[rows, :] = out[:, inner:]


def backward_kernel(cols_n, ratio, groups, size_ref, blocks_ref, own_ref, got_ref, *rest):
    count = len(groups)
    inner_refs, outer_refs = rest[:count], rest[count:2 * count]
    leaf_hbm, rows_hbm, coupled_v, solved_v, rows_v, sems = rest[2 * count:]
    tiles = solved_v.shape[0] // TILE
    half = own_ref.shape[0]
    block_r = rows_hbm.shape[0]
    unit = 2 * half // cols_n // cols_n
    size = size_ref[0]
    row, col = lax.axis_index("row"), lax.axis_index("col")

    def bring(out_v, at, first, length):
        part = min(unit, length)
        for n in range(0, length, part):
            index = lax.div(first + n, unit)
            place = place_of(lax.div(index, cols_n), lax.div(row, ratio), cols_n)
            place += cols_n * place_of(lax.rem(index, cols_n), col, cols_n)
            start = place * unit + lax.rem(first + n, unit)
            inside = start < half
            near = pl.multiple_of(jnp.where(inside, start, 0), part)
            far = pl.multiple_of(jnp.where(inside, 0, start - half), part)
            out_v[pl.ds(at + n, part), :] = jnp.where(
                inside, own_ref[pl.ds(near, part), :], got_ref[pl.ds(far, part), :])

    for k in range(KB):
        bring(coupled_v, k * BLK, blocks_ref[0, k] * BLK, BLK)
    bring(rows_v, 0, row * block_r, block_r)
    copies = [pltpu.make_async_copy(rows_v, rows_hbm, sems.at[tiles])]
    copies[0].start()
    for group, inner_ref, outer_ref in zip(groups, inner_refs, outer_refs):
        term = jnp.dot(inner_ref[...], coupled_v[...], preferred_element_type=jnp.float32)
        for n, i in enumerate(group):
            here = slice(n * TILE, (n + 1) * TILE)
            tile = outer_ref[here, :] - term[here, :]
            at = lax.broadcasted_iota(jnp.int32, tile.shape, 0) + i * TILE
            rows = pl.ds(i * TILE, TILE)
            solved_v[rows, :] = jnp.where(at < size, tile, 0.0).astype(jnp.bfloat16)
            copies.append(pltpu.make_async_copy(
                solved_v.at[rows], leaf_hbm.at[0, rows], sems.at[i]))
            copies[-1].start()
    for copy in copies:
        copy.wait()


def shards(
    rows_n,
    cols_n,
    rhs_leaf,
    rhs_sep,
    leaf_sizes,
    off_blocks,
    linv_leaf,
    uinv_leaf,
    l_off,
    u_off,
    linv_sep,
    uinv_sep,
):
    width, columns = rhs_leaf.shape[1:]
    share = rhs_sep.shape[0]
    sep = share * cols_n
    block_r = sep // rows_n
    ratio = rows_n // cols_n
    tiles = width // TILE
    bf16 = jnp.bfloat16
    smem = pl.BlockSpec(memory_space=pltpu.SMEM)
    vmem = pl.BlockSpec(memory_space=pltpu.VMEM)
    any_space = pl.BlockSpec(memory_space=pl.ANY)
    in_vmem = functools.partial(pltpu.with_memory_space_constraint, memory_space=pltpu.VMEM)
    in_smem = functools.partial(pltpu.with_memory_space_constraint, memory_space=pltpu.SMEM)
    in_hbm = functools.partial(pltpu.with_memory_space_constraint, memory_space=pltpu.HBM)

    unit = share // cols_n
    forward, keep, send, size, blocks, *pieces = pl.pallas_call(
        functools.partial(forward_kernel, cols_n, ratio),
        out_shape=[
            pltpu.VMEM((width, columns), bf16),
            pltpu.VMEM((sep // 2, columns), bf16),
            pltpu.VMEM((sep // 2, columns), bf16),
            pltpu.SMEM((1,), jnp.int32),
            pltpu.SMEM((1, KB), jnp.int32),
        ] + [pltpu.VMEM((unit, block_r), bf16)] * cols_n,
        in_specs=[smem] + [any_space] * 5,
        out_specs=[vmem, vmem, vmem, smem, smem] + [vmem] * cols_n,
        scratch_shapes=[
            pltpu.VMEM((width, columns), bf16),
            pltpu.VMEM((width, width), bf16),
            pltpu.VMEM((KB * BLK, width), bf16),
            pltpu.VMEM((KB * BLK, columns), jnp.float32),
            pltpu.SemaphoreType.DMA((2 * tiles + cols_n,)),
        ],
        compiler_params=pltpu.CompilerParams(vmem_limit_bytes=24 * 2**20),
        cost_estimate=pl.CostEstimate(
            flops=900_000_000, bytes_accessed=8_000_000, transcendentals=0),
        name="leaf_forward",
    )(
        leaf_sizes, in_hbm(off_blocks), in_hbm(rhs_leaf), in_hbm(linv_leaf),
        in_hbm(l_off), in_hbm(uinv_sep),
    )
    tied = lax.optimization_barrier
    groups = [[0], [1]] + [[2 + j, tiles - 1 - j] for j in range((tiles - 2) // 2)]
    inner, outer, moved = [], [], []

    def move(p):
        parts = cols_n // ratio
        pairs = []
        for r in range(rows_n):
            for c in range(cols_n):
                low = (c // parts) ^ (p // parts)
                to_c = (r % ratio) * parts + ((c % parts) ^ (p % parts))
                pairs.append((r * cols_n + c, (r - r % ratio + low) * cols_n + to_c))
        return lax.ppermute(pieces[p], ("row", "col"), pairs)

    def swap_and_move(x, axis, count, bit, pieces_now):
        x, *moved[:] = tied((x, *moved))
        for _ in range(min(pieces_now, cols_n - len(moved))):
            x, pieces[len(moved)] = tied((x, pieces[len(moved)]))
            moved.append(move(len(moved)))
        return swap(x, axis, count, bit)

    def swap_beside(x, axis, count, bit):
        if len(inner) == len(groups):
            return swap(x, axis, count, bit)
        group = groups[len(inner)]
        x, factor = tied((x, uinv_leaf))
        got = swap(x, axis, count, bit)
        length = len(group) * TILE
        ahead = pl.pallas_call(
            functools.partial(ahead_kernel, group),
            out_shape=[
                pltpu.VMEM((length, u_off.shape[2]), bf16),
                pltpu.VMEM((length, columns), jnp.float32),
            ],
            in_specs=[smem, vmem, vmem, any_space],
            out_specs=[vmem, vmem],
            scratch_shapes=[
                pltpu.VMEM((width, u_off.shape[2] + columns), bf16),
                pltpu.VMEM((length, width), bf16),
                pltpu.SemaphoreType.DMA((len(group),)),
            ],
            compiler_params=pltpu.CompilerParams(vmem_limit_bytes=16 * 2**20),
            cost_estimate=pl.CostEstimate(
                flops=600_000_000, bytes_accessed=1_000_000, transcendentals=0),
            name="leaf_ahead",
        )(in_smem(size), in_vmem(u_off), in_vmem(forward), in_hbm(factor))
        got, *ahead = tied((got, *ahead))
        inner.append(ahead[0])
        outer.append(ahead[1])
        return got

    waits = rows_n.bit_length() + cols_n.bit_length() - 3
    pieces_now = -(-cols_n // waits)
    bit = 1
    while bit < cols_n:
        if bit == 1:
            got = swap(send, "col", cols_n, bit)
        else:
            got = swap_and_move(send, "col", cols_n, bit, pieces_now)
        bit *= 2
        if bit < cols_n:
            part = keep.shape[0] // 2
            send = add(keep[part:], got[part:])
            keep = add(keep[:part], got[:part])
        else:
            keep = add(keep, got)
    bit = 1
    while bit < rows_n:
        keep = add(keep, swap_and_move(keep, "row", rows_n, bit, pieces_now))
        bit *= 2
    keep, *moved[:] = tied((keep, *moved))
    sep_rhs = (rhs_sep.astype(jnp.float32) - keep.astype(jnp.float32)).astype(bf16)

    own = jnp.dot(linv_sep, sep_rhs, preferred_element_type=jnp.float32).astype(bf16)
    bit = 1
    while bit < cols_n:
        own = add(own, swap(own, "col", cols_n, bit))
        bit *= 2
    bit = rows_n // 2
    while bit >= ratio:
        got = swap_beside(own, "row", rows_n, bit)
        if bit > ratio:
            own = jnp.concatenate([own, got], 0)
        bit //= 2
    own = pl.pallas_call(
        functools.partial(separator_kernel, cols_n, ratio),
        out_shape=pltpu.VMEM((unit, columns), bf16),
        in_specs=[vmem] * (2 + cols_n),
        out_specs=vmem,
        compiler_params=pltpu.CompilerParams(vmem_limit_bytes=8 * 2**20),
        name="separator_backward",
    )(in_vmem(own), in_vmem(got), *map(in_vmem, moved))
    bit = 1
    while bit < ratio:
        own = add(own, swap(own, "row", rows_n, bit))
        bit *= 2
    bit = rows_n // 2
    while bit >= ratio:
        own = jnp.concatenate([own, swap_beside(own, "row", rows_n, bit)], 0)
        bit //= 2
    bit = cols_n // 2
    while bit >= 1:
        got = swap(own, "col", cols_n, bit) if bit == 1 else swap_beside(own, "col", cols_n, bit)
        if bit > 1:
            own = jnp.concatenate([own, got], 0)
        bit //= 2

    solved_leaf, solved_rows = pl.pallas_call(
        functools.partial(backward_kernel, cols_n, ratio, groups),
        out_shape=[
            jax.ShapeDtypeStruct((1, width, columns), bf16),
            jax.ShapeDtypeStruct((block_r, columns), bf16),
        ],
        in_specs=[smem, smem] + [vmem] * (2 + 2 * len(groups)),
        out_specs=[any_space, any_space],
        scratch_shapes=[
            pltpu.VMEM((KB * BLK, columns), bf16),
            pltpu.VMEM((width, columns), bf16),
            pltpu.VMEM((block_r, columns), bf16),
            pltpu.SemaphoreType.DMA((tiles + 1,)),
        ],
        compiler_params=pltpu.CompilerParams(vmem_limit_bytes=16 * 2**20),
        cost_estimate=pl.CostEstimate(
            flops=270_000_000, bytes_accessed=4_000_000, transcendentals=0),
        name="leaf_backward",
    )(
        in_smem(size), in_smem(blocks), in_vmem(own), in_vmem(got),
        *map(in_vmem, inner), *map(in_vmem, outer),
    )
    return (solved_leaf, solved_rows)


def solution(mesh):
    placed = (
        P(("row", "col"), None, None),
        P("col", None),
        P(("row", "col")),
        P(("row", "col"), None),
        P(("row", "col"), None, None),
        P(("row", "col"), None, None),
        P(("row", "col"), None, None),
        P(("row", "col"), None, None),
        P("row", "col"),
        P("row", "col"),
    )
    return jax.shard_map(
        functools.partial(shards, mesh.shape["row"], mesh.shape["col"]),
        mesh=mesh,
        in_specs=placed,
        out_specs=(P(("row", "col"), None, None), P("row", None)),
        check_vma=False,
    )
```

```python
import functools

import jax
import jax.numpy as jnp
from jax import lax
from jax.experimental import pallas as pl
from jax.experimental.pallas import tpu as pltpu
from jax.sharding import PartitionSpec as P

BLK = 128
KB = 4
TILE = 256


def swap(x, axis, size, bit):
    return lax.ppermute(x, axis, [(i, i ^ bit) for i in range(size)])


def add(a, b):
    return (a.astype(jnp.float32) + b.astype(jnp.float32)).astype(jnp.bfloat16)


def place_of(share, me, size):
    apart = share ^ me
    place, bit = 0, 1
    while bit < size:
        place = place * 2 + lax.rem(lax.div(apart, bit), 2)
        bit *= 2
    return place


def forward_kernel(
    cols_n, size_in, blocks_hbm, rhs_hbm, linv_hbm, loff_hbm, usep_hbm,
    forward_ref, keep_ref, send_ref, size_ref, blocks_ref, *rest,
):
    piece_refs, (rhs_v, linv_v, loff_v, total_v, sems) = rest[:-5], rest[-5:]
    width = rhs_v.shape[0]
    tiles = width // TILE
    half = keep_ref.shape[0]
    per_share = 2 * half // cols_n // BLK
    me = lax.axis_index("col")

    step = 2 * TILE
    copies = [pltpu.make_async_copy(rhs_hbm.at[0], rhs_v, sems.at[0])]
    for i in range(tiles):
        rows = pl.ds(i * TILE, TILE)
        live = pl.ds(0, (i + 1) * TILE)
        copies.append(pltpu.make_async_copy(
            linv_hbm.at[0, rows, live], linv_v.at[rows, live], sems.at[len(copies)]))
        if i % 2:
            cols = pl.ds((i - 1) * TILE, step)
            copies.append(pltpu.make_async_copy(
                loff_hbm.at[0, :, cols], loff_v.at[:, cols], sems.at[len(copies)]))
    copies.append(pltpu.make_async_copy(blocks_hbm, blocks_ref, sems.at[len(copies)]))
    late = len(copies)
    block_r = piece_refs[0].shape[1]
    for p, piece_ref in enumerate(piece_refs):
        across = pl.multiple_of((lax.div(me, cols_n // 2) ^ p) * block_r, block_r)
        copies.append(pltpu.make_async_copy(
            usep_hbm.at[:, pl.ds(across, block_r)], piece_ref, sems.at[len(copies)]))
    ahead = 7
    for copy in copies[:ahead]:
        copy.start()

    def arrive(n):
        copies[n].wait()
        if n + ahead < len(copies):
            copies[n + ahead].start()

    def update(s):
        cols = pl.ds(s * step, step)
        return jnp.dot(loff_v[:, cols], forward_ref[cols, :], preferred_element_type=jnp.float32)

    size = size_in[0]
    size_ref[0] = size
    keep_ref[...] = jnp.zeros_like(keep_ref)
    send_ref[...] = jnp.zeros_like(send_ref)
    arrive(0)
    at = lax.broadcasted_iota(jnp.int32, rhs_v.shape, 0)
    rhs_v[...] = jnp.where(at < size, rhs_v[...], jnp.zeros_like(rhs_v))
    for s in range(tiles // 2):
        if s >= 1:
            arrive(3 * s)
        arrive(3 * s + 1)
        arrive(3 * s + 2)
        if s == 1:
            total_v[...] = update(0)
        elif s > 1:
            total_v[...] += update(s - 1)
        for i in (2 * s, 2 * s + 1):
            rows = pl.ds(i * TILE, TILE)
            live = pl.ds(0, (i + 1) * TILE)
            tile = jnp.dot(linv_v[rows, live], rhs_v[live, :], preferred_element_type=jnp.float32)
            at = lax.broadcasted_iota(jnp.int32, tile.shape, 0) + i * TILE
            forward_ref[rows, :] = jnp.where(at < size, tile, 0.0).astype(jnp.bfloat16)
    arrive(3 * (tiles // 2))
    total_v[...] += update(tiles // 2 - 1)

    for n in range(late - 1, len(copies)):
        arrive(n)
    for k in range(KB):
        block = blocks_ref[0, k]
        share = lax.div(block, per_share)
        start = (place_of(share, me, cols_n) * per_share + lax.rem(block, per_share)) * BLK
        part = total_v[pl.ds(k * BLK, BLK), :].astype(jnp.bfloat16)

        @pl.when(start < half)
        def _():
            keep_ref[pl.ds(pl.multiple_of(start, BLK), BLK), :] = part

        @pl.when(start >= half)
        def _():
            send_ref[pl.ds(pl.multiple_of(start - half, BLK), BLK), :] = part


def separator_kernel(rows_n, own_ref, got_ref, near_ref, far_ref, out_ref):
    row = lax.axis_index("row")
    top, low = lax.div(row, rows_n // 2), lax.rem(row, 2)
    straight = top == low
    first = jnp.where(straight, own_ref[...], got_ref[...])
    second = jnp.where(straight, got_ref[...], own_ref[...])
    total = jnp.dot(near_ref[...], first, preferred_element_type=jnp.float32)
    total += jnp.dot(far_ref[...], second, preferred_element_type=jnp.float32)
    out_ref[...] = total.astype(jnp.bfloat16)


def ahead_kernel(tiles_here, size_ref, uoff_ref, forward_ref, uinv_hbm, inner_ref, outer_ref,
                 both_v, uinv_v, sems):
    width, inner = uoff_ref.shape[1:]
    size = size_ref[0]
    copies = []
    for n, i in enumerate(tiles_here):
        copies.append(pltpu.make_async_copy(
            uinv_hbm.at[0, pl.ds(i * TILE, TILE), pl.ds(i * TILE, width - i * TILE)],
            uinv_v.at[pl.ds(n * TILE, TILE), pl.ds(i * TILE, width - i * TILE)],
            sems.at[n]))
        copies[-1].start()
    for j in range(min(tiles_here), width // TILE):
        rows = pl.ds(j * TILE, TILE)
        block = uoff_ref[0, rows, :]
        at = lax.broadcasted_iota(jnp.int32, block.shape, 0) + j * TILE
        both_v[rows, 0:inner] = jnp.where(at < size, block, jnp.zeros_like(block))
        both_v[rows, inner:] = forward_ref[rows, :]
    for n, i in enumerate(tiles_here):
        rows = pl.ds(n * TILE, TILE)
        live = pl.ds(i * TILE, width - i * TILE)
        copies[n].wait()
        out = jnp.dot(uinv_v[rows, live], both_v[live, :], preferred_element_type=jnp.float32)
        inner_ref[rows, :] = out[:, :inner].astype(jnp.bfloat16)
        outer_ref[rows, :] = out[:, inner:]


def backward_kernel(cols_n, groups, size_ref, blocks_ref, own_ref, got_ref, *rest):
    count = len(groups)
    inner_refs, outer_refs = rest[:count], rest[count:2 * count]
    leaf_hbm, rows_hbm, coupled_v, solved_v, rows_v, sems = rest[2 * count:]
    tiles = solved_v.shape[0] // TILE
    half = own_ref.shape[0]
    block_r = rows_hbm.shape[0]
    rows_n = 2 * half // block_r
    size = size_ref[0]
    row, col = lax.axis_index("row"), lax.axis_index("col")

    def solved_at(first, length):
        index = lax.div(first, block_r)
        top, rest = lax.div(index, rows_n // 2), lax.rem(index, rows_n // 2)
        where = lax.rem(rest, 2) * (cols_n // 2) + lax.div(rest, 2)
        place = (top ^ lax.div(row, rows_n // 2)) + 2 * place_of(where, col, cols_n)
        start = place * block_r + lax.rem(first, block_r)
        inside = start < half
        near = pl.multiple_of(jnp.where(inside, start, 0), BLK)
        far = pl.multiple_of(jnp.where(inside, 0, start - half), BLK)
        return jnp.where(inside, own_ref[pl.ds(near, length), :], got_ref[pl.ds(far, length), :])

    for k in range(KB):
        coupled_v[pl.ds(k * BLK, BLK), :] = solved_at(blocks_ref[0, k] * BLK, BLK)
    rows_v[...] = solved_at(row * block_r, block_r)
    copies = [pltpu.make_async_copy(rows_v, rows_hbm, sems.at[tiles])]
    copies[0].start()
    for group, inner_ref, outer_ref in zip(groups, inner_refs, outer_refs):
        term = jnp.dot(inner_ref[...], coupled_v[...], preferred_element_type=jnp.float32)
        for n, i in enumerate(group):
            here = slice(n * TILE, (n + 1) * TILE)
            tile = outer_ref[here, :] - term[here, :]
            at = lax.broadcasted_iota(jnp.int32, tile.shape, 0) + i * TILE
            rows = pl.ds(i * TILE, TILE)
            solved_v[rows, :] = jnp.where(at < size, tile, 0.0).astype(jnp.bfloat16)
            copies.append(pltpu.make_async_copy(
                solved_v.at[rows], leaf_hbm.at[0, rows], sems.at[i]))
            copies[-1].start()
    for copy in copies:
        copy.wait()


def shards(
    rows_n,
    cols_n,
    rhs_leaf,
    rhs_sep,
    leaf_sizes,
    off_blocks,
    linv_leaf,
    uinv_leaf,
    l_off,
    u_off,
    linv_sep,
    uinv_sep,
):
    width, columns = rhs_leaf.shape[1:]
    share = rhs_sep.shape[0]
    sep = share * cols_n
    block_r = sep // rows_n
    assert rows_n == 2 * cols_n
    tiles = width // TILE
    bf16 = jnp.bfloat16
    smem = pl.BlockSpec(memory_space=pltpu.SMEM)
    vmem = pl.BlockSpec(memory_space=pltpu.VMEM)
    any_space = pl.BlockSpec(memory_space=pl.ANY)
    in_vmem = functools.partial(pltpu.with_memory_space_constraint, memory_space=pltpu.VMEM)
    in_smem = functools.partial(pltpu.with_memory_space_constraint, memory_space=pltpu.SMEM)
    in_hbm = functools.partial(pltpu.with_memory_space_constraint, memory_space=pltpu.HBM)

    forward, keep, send, size, blocks, *pieces = pl.pallas_call(
        functools.partial(forward_kernel, cols_n),
        out_shape=[
            pltpu.VMEM((width, columns), bf16),
            pltpu.VMEM((sep // 2, columns), bf16),
            pltpu.VMEM((sep // 2, columns), bf16),
            pltpu.SMEM((1,), jnp.int32),
            pltpu.SMEM((1, KB), jnp.int32),
        ] + [pltpu.VMEM((block_r, block_r), bf16)] * 2,
        in_specs=[smem] + [any_space] * 5,
        out_specs=[vmem, vmem, vmem, smem, smem, vmem, vmem],
        scratch_shapes=[
            pltpu.VMEM((width, columns), bf16),
            pltpu.VMEM((width, width), bf16),
            pltpu.VMEM((KB * BLK, width), bf16),
            pltpu.VMEM((KB * BLK, columns), jnp.float32),
            pltpu.SemaphoreType.DMA((2 * tiles + 2,)),
        ],
        compiler_params=pltpu.CompilerParams(vmem_limit_bytes=24 * 2**20),
        cost_estimate=pl.CostEstimate(
            flops=900_000_000, bytes_accessed=8_000_000, transcendentals=0),
        name="leaf_forward",
    )(
        leaf_sizes, in_hbm(off_blocks), in_hbm(rhs_leaf), in_hbm(linv_leaf),
        in_hbm(l_off), in_hbm(uinv_sep),
    )
    tied = lax.optimization_barrier
    groups = [[0], [1]] + [[2 + j, tiles - 1 - j] for j in range((tiles - 2) // 2)]
    inner, outer, moved = [], [], []

    def move(p):
        wide = cols_n // 2
        pairs = []
        for r in range(rows_n):
            for c in range(cols_n):
                top, zl, y = r // 2 // wide, r // 2 % wide, r % 2
                to_r = (top * wide + c % wide) * 2 + ((c // wide) ^ p)
                pairs.append((r * cols_n + c, to_r * cols_n + y * wide + zl))
        return lax.ppermute(pieces[p], ("row", "col"), pairs)

    def swap_and_move(x, axis, count, bit):
        x, pieces[len(moved)] = tied((x, pieces[len(moved)]))
        moved.append(move(len(moved)))
        return swap(x, axis, count, bit)

    def swap_beside(x, axis, count, bit):
        if len(inner) == len(groups):
            return swap(x, axis, count, bit)
        group = groups[len(inner)]
        x, factor = tied((x, uinv_leaf))
        got = swap(x, axis, count, bit)
        length = len(group) * TILE
        ahead = pl.pallas_call(
            functools.partial(ahead_kernel, group),
            out_shape=[
                pltpu.VMEM((length, u_off.shape[2]), bf16),
                pltpu.VMEM((length, columns), jnp.float32),
            ],
            in_specs=[smem, vmem, vmem, any_space],
            out_specs=[vmem, vmem],
            scratch_shapes=[
                pltpu.VMEM((width, u_off.shape[2] + columns), bf16),
                pltpu.VMEM((length, width), bf16),
                pltpu.SemaphoreType.DMA((len(group),)),
            ],
            compiler_params=pltpu.CompilerParams(vmem_limit_bytes=16 * 2**20),
            cost_estimate=pl.CostEstimate(
                flops=600_000_000, bytes_accessed=1_000_000, transcendentals=0),
            name="leaf_ahead",
        )(in_smem(size), in_vmem(u_off), in_vmem(forward), in_hbm(factor))
        got, *ahead = tied((got, *ahead))
        inner.append(ahead[0])
        outer.append(ahead[1])
        return got

    def swap_busy(x, axis, count, bit):
        busy = swap_and_move if len(moved) < 2 else swap_beside
        return busy(x, axis, count, bit)

    bit = 1
    while bit < cols_n:
        got = (swap if bit == 1 else swap_busy)(send, "col", cols_n, bit)
        bit *= 2
        if bit < cols_n:
            part = keep.shape[0] // 2
            send = add(keep[part:], got[part:])
            keep = add(keep[:part], got[:part])
        else:
            keep = add(keep, got)
    bit = 1
    while bit < rows_n:
        if bit == rows_n // 4:
            keep, moved[0] = tied((keep, moved[0]))
        elif bit == rows_n // 2:
            keep, moved[1] = tied((keep, moved[1]))
        keep = add(keep, swap_busy(keep, "row", rows_n, bit))
        bit *= 2
    sep_rhs = (rhs_sep.astype(jnp.float32) - keep.astype(jnp.float32)).astype(bf16)

    own = jnp.dot(linv_sep, sep_rhs, preferred_element_type=jnp.float32).astype(bf16)
    bit = 1
    while bit < cols_n:
        own = add(own, swap(own, "col", cols_n, bit))
        bit *= 2
    got = swap_beside(own, "row", rows_n, rows_n // 2)
    own = pl.pallas_call(
        functools.partial(separator_kernel, rows_n),
        out_shape=pltpu.VMEM((block_r, columns), bf16),
        in_specs=[vmem] * 4,
        out_specs=vmem,
        compiler_params=pltpu.CompilerParams(vmem_limit_bytes=8 * 2**20),
        name="separator_backward",
    )(in_vmem(own), in_vmem(got), *map(in_vmem, moved))
    bit = 1
    while bit < rows_n // 2:
        own = add(own, swap(own, "row", rows_n, bit))
        bit *= 2
    own = jnp.concatenate([own, swap_beside(own, "row", rows_n, rows_n // 2)], 0)
    bit = cols_n // 2
    while bit >= 1:
        got = (swap if bit == 1 else swap_beside)(own, "col", cols_n, bit)
        if bit > 1:
            own = jnp.concatenate([own, got], 0)
        bit //= 2

    solved_leaf, solved_rows = pl.pallas_call(
        functools.partial(backward_kernel, cols_n, groups),
        out_shape=[
            jax.ShapeDtypeStruct((1, width, columns), bf16),
            jax.ShapeDtypeStruct((block_r, columns), bf16),
        ],
        in_specs=[smem, smem] + [vmem] * (2 + 2 * len(groups)),
        out_specs=[any_space, any_space],
        scratch_shapes=[
            pltpu.VMEM((KB * BLK, columns), bf16),
            pltpu.VMEM((width, columns), bf16),
            pltpu.VMEM((block_r, columns), bf16),
            pltpu.SemaphoreType.DMA((tiles + 1,)),
        ],
        compiler_params=pltpu.CompilerParams(vmem_limit_bytes=16 * 2**20),
        cost_estimate=pl.CostEstimate(
            flops=270_000_000, bytes_accessed=4_000_000, transcendentals=0),
        name="leaf_backward",
    )(
        in_smem(size), in_smem(blocks), in_vmem(own), in_vmem(got),
        *map(in_vmem, inner), *map(in_vmem, outer),
    )
    return (solved_leaf, solved_rows)


def solution(mesh):
    placed = (
        P(("row", "col"), None, None),
        P("col", None),
        P(("row", "col")),
        P(("row", "col"), None),
        P(("row", "col"), None, None),
        P(("row", "col"), None, None),
        P(("row", "col"), None, None),
        P(("row", "col"), None, None),
        P("row", "col"),
        P("row", "col"),
    )
    return jax.shard_map(
        functools.partial(shards, mesh.shape["row"], mesh.shape["col"]),
        mesh=mesh,
        in_specs=placed,
        out_specs=(P(("row", "col"), None, None), P("row", None)),
        check_vma=False,
    )
```

```python
import functools

import jax
import jax.numpy as jnp
from jax import lax
from jax.experimental import pallas as pl
from jax.experimental.pallas import tpu as pltpu
from jax.sharding import PartitionSpec as P

BLK = 128
KB = 4
TILE = 256


def swap(x, axis, size, bit):
    return lax.ppermute(x, axis, [(i, i ^ bit) for i in range(size)])


def add(a, b):
    return (a.astype(jnp.float32) + b.astype(jnp.float32)).astype(jnp.bfloat16)


def place_of(share, me, size):
    apart = share ^ me
    place, bit = 0, 1
    while bit < size:
        place = place * 2 + lax.rem(lax.div(apart, bit), 2)
        bit *= 2
    return place


def forward_kernel(
    cols_n, size_in, blocks_hbm, rhs_hbm, linv_hbm, loff_hbm, usep_hbm,
    forward_ref, keep_ref, send_ref, size_ref, blocks_ref, *rest,
):
    piece_refs, (rhs_v, linv_v, loff_v, total_v, sems) = rest[:-5], rest[-5:]
    width = rhs_v.shape[0]
    tiles = width // TILE
    half = keep_ref.shape[0]
    per_share = 2 * half // cols_n // BLK
    me = lax.axis_index("col")

    step = 2 * TILE
    copies = [pltpu.make_async_copy(rhs_hbm.at[0], rhs_v, sems.at[0])]
    for i in range(tiles):
        rows = pl.ds(i * TILE, TILE)
        live = pl.ds(0, (i + 1) * TILE)
        copies.append(pltpu.make_async_copy(
            linv_hbm.at[0, rows, live], linv_v.at[rows, live], sems.at[len(copies)]))
        if i % 2:
            cols = pl.ds((i - 1) * TILE, step)
            copies.append(pltpu.make_async_copy(
                loff_hbm.at[0, :, cols], loff_v.at[:, cols], sems.at[len(copies)]))
    copies.append(pltpu.make_async_copy(blocks_hbm, blocks_ref, sems.at[len(copies)]))
    late = len(copies)
    block_r = piece_refs[0].shape[1]
    for p, piece_ref in enumerate(piece_refs):
        across = pl.multiple_of((lax.div(me, cols_n // 2) ^ p) * block_r, block_r)
        copies.append(pltpu.make_async_copy(
            usep_hbm.at[:, pl.ds(across, block_r)], piece_ref, sems.at[len(copies)]))
    ahead = 7
    for copy in copies[:ahead]:
        copy.start()

    def arrive(n):
        copies[n].wait()
        if n + ahead < len(copies):
            copies[n + ahead].start()

    def update(s):
        cols = pl.ds(s * step, step)
        return jnp.dot(loff_v[:, cols], forward_ref[cols, :], preferred_element_type=jnp.float32)

    size = size_in[0]
    size_ref[0] = size
    keep_ref[...] = jnp.zeros_like(keep_ref)
    send_ref[...] = jnp.zeros_like(send_ref)
    arrive(0)
    at = lax.broadcasted_iota(jnp.int32, rhs_v.shape, 0)
    rhs_v[...] = jnp.where(at < size, rhs_v[...], jnp.zeros_like(rhs_v))
    for s in range(tiles // 2):
        if s >= 1:
            arrive(3 * s)
        arrive(3 * s + 1)
        arrive(3 * s + 2)
        if s == 1:
            total_v[...] = update(0)
        elif s > 1:
            total_v[...] += update(s - 1)
        for i in (2 * s, 2 * s + 1):
            rows = pl.ds(i * TILE, TILE)
            live = pl.ds(0, (i + 1) * TILE)
            tile = jnp.dot(linv_v[rows, live], rhs_v[live, :], preferred_element_type=jnp.float32)
            at = lax.broadcasted_iota(jnp.int32, tile.shape, 0) + i * TILE
            forward_ref[rows, :] = jnp.where(at < size, tile, 0.0).astype(jnp.bfloat16)
    arrive(3 * (tiles // 2))
    total_v[...] += update(tiles // 2 - 1)

    for n in range(late - 1, len(copies)):
        arrive(n)
    for k in range(KB):
        block = blocks_ref[0, k]
        share = lax.div(block, per_share)
        start = (place_of(share, me, cols_n) * per_share + lax.rem(block, per_share)) * BLK
        part = total_v[pl.ds(k * BLK, BLK), :].astype(jnp.bfloat16)

        @pl.when(start < half)
        def _():
            keep_ref[pl.ds(pl.multiple_of(start, BLK), BLK), :] = part

        @pl.when(start >= half)
        def _():
            send_ref[pl.ds(pl.multiple_of(start - half, BLK), BLK), :] = part


def separator_kernel(rows_n, own_ref, got_ref, near_ref, far_ref, out_ref):
    row = lax.axis_index("row")
    top, low = lax.div(row, rows_n // 2), lax.rem(row, 2)
    straight = top == low
    first = jnp.where(straight, own_ref[...], got_ref[...])
    second = jnp.where(straight, got_ref[...], own_ref[...])
    total = jnp.dot(near_ref[...], first, preferred_element_type=jnp.float32)
    total += jnp.dot(far_ref[...], second, preferred_element_type=jnp.float32)
    out_ref[...] = total.astype(jnp.bfloat16)


def ahead_kernel(tiles_here, size_ref, uoff_ref, forward_ref, uinv_hbm, inner_ref, outer_ref,
                 both_v, uinv_v, sems):
    width, inner = uoff_ref.shape[1:]
    size = size_ref[0]
    copies = []
    for n, i in enumerate(tiles_here):
        copies.append(pltpu.make_async_copy(
            uinv_hbm.at[0, pl.ds(i * TILE, TILE), pl.ds(i * TILE, width - i * TILE)],
            uinv_v.at[pl.ds(n * TILE, TILE), pl.ds(i * TILE, width - i * TILE)],
            sems.at[n]))
        copies[-1].start()
    for j in range(min(tiles_here), width // TILE):
        rows = pl.ds(j * TILE, TILE)
        block = uoff_ref[0, rows, :]
        at = lax.broadcasted_iota(jnp.int32, block.shape, 0) + j * TILE
        both_v[rows, 0:inner] = jnp.where(at < size, block, jnp.zeros_like(block))
        both_v[rows, inner:] = forward_ref[rows, :]
    for n, i in enumerate(tiles_here):
        rows = pl.ds(n * TILE, TILE)
        live = pl.ds(i * TILE, width - i * TILE)
        copies[n].wait()
        out = jnp.dot(uinv_v[rows, live], both_v[live, :], preferred_element_type=jnp.float32)
        inner_ref[rows, :] = out[:, :inner].astype(jnp.bfloat16)
        outer_ref[rows, :] = out[:, inner:]


def backward_kernel(cols_n, groups, size_ref, blocks_ref, own_ref, got_ref, *rest):
    count = len(groups)
    inner_refs, outer_refs = rest[:count], rest[count:2 * count]
    leaf_hbm, rows_hbm, coupled_v, solved_v, rows_v, sems = rest[2 * count:]
    tiles = solved_v.shape[0] // TILE
    half = own_ref.shape[0]
    block_r = rows_hbm.shape[0]
    rows_n = 2 * half // block_r
    size = size_ref[0]
    row, col = lax.axis_index("row"), lax.axis_index("col")

    def solved_at(first, length):
        index = lax.div(first, block_r)
        top, rest = lax.div(index, rows_n // 2), lax.rem(index, rows_n // 2)
        where = lax.rem(rest, 2) * (cols_n // 2) + lax.div(rest, 2)
        place = (top ^ lax.div(row, rows_n // 2)) + 2 * place_of(where, col, cols_n)
        start = place * block_r + lax.rem(first, block_r)
        inside = start < half
        near = pl.multiple_of(jnp.where(inside, start, 0), BLK)
        far = pl.multiple_of(jnp.where(inside, 0, start - half), BLK)
        return jnp.where(inside, own_ref[pl.ds(near, length), :], got_ref[pl.ds(far, length), :])

    for k in range(KB):
        coupled_v[pl.ds(k * BLK, BLK), :] = solved_at(blocks_ref[0, k] * BLK, BLK)
    rows_v[...] = solved_at(row * block_r, block_r)
    copies = [pltpu.make_async_copy(rows_v, rows_hbm, sems.at[tiles])]
    copies[0].start()
    for group, inner_ref, outer_ref in zip(groups, inner_refs, outer_refs):
        term = jnp.dot(inner_ref[...], coupled_v[...], preferred_element_type=jnp.float32)
        for n, i in enumerate(group):
            here = slice(n * TILE, (n + 1) * TILE)
            tile = outer_ref[here, :] - term[here, :]
            at = lax.broadcasted_iota(jnp.int32, tile.shape, 0) + i * TILE
            rows = pl.ds(i * TILE, TILE)
            solved_v[rows, :] = jnp.where(at < size, tile, 0.0).astype(jnp.bfloat16)
            copies.append(pltpu.make_async_copy(
                solved_v.at[rows], leaf_hbm.at[0, rows], sems.at[i]))
            copies[-1].start()
    for copy in copies:
        copy.wait()


def shards(
    rows_n,
    cols_n,
    rhs_leaf,
    rhs_sep,
    leaf_sizes,
    off_blocks,
    linv_leaf,
    uinv_leaf,
    l_off,
    u_off,
    linv_sep,
    uinv_sep,
):
    width, columns = rhs_leaf.shape[1:]
    share = rhs_sep.shape[0]
    sep = share * cols_n
    block_r = sep // rows_n
    assert rows_n == 2 * cols_n
    tiles = width // TILE
    bf16 = jnp.bfloat16
    smem = pl.BlockSpec(memory_space=pltpu.SMEM)
    vmem = pl.BlockSpec(memory_space=pltpu.VMEM)
    any_space = pl.BlockSpec(memory_space=pl.ANY)
    in_vmem = functools.partial(pltpu.with_memory_space_constraint, memory_space=pltpu.VMEM)
    in_smem = functools.partial(pltpu.with_memory_space_constraint, memory_space=pltpu.SMEM)
    in_hbm = functools.partial(pltpu.with_memory_space_constraint, memory_space=pltpu.HBM)

    forward, keep, send, size, blocks, *pieces = pl.pallas_call(
        functools.partial(forward_kernel, cols_n),
        out_shape=[
            pltpu.VMEM((width, columns), bf16),
            pltpu.VMEM((sep // 2, columns), bf16),
            pltpu.VMEM((sep // 2, columns), bf16),
            pltpu.SMEM((1,), jnp.int32),
            pltpu.SMEM((1, KB), jnp.int32),
        ] + [pltpu.VMEM((block_r, block_r), bf16)] * 2,
        in_specs=[smem] + [any_space] * 5,
        out_specs=[vmem, vmem, vmem, smem, smem, vmem, vmem],
        scratch_shapes=[
            pltpu.VMEM((width, columns), bf16),
            pltpu.VMEM((width, width), bf16),
            pltpu.VMEM((KB * BLK, width), bf16),
            pltpu.VMEM((KB * BLK, columns), jnp.float32),
            pltpu.SemaphoreType.DMA((2 * tiles + 2,)),
        ],
        compiler_params=pltpu.CompilerParams(vmem_limit_bytes=24 * 2**20),
        cost_estimate=pl.CostEstimate(
            flops=900_000_000, bytes_accessed=8_000_000, transcendentals=0),
        name="leaf_forward",
    )(
        leaf_sizes, in_hbm(off_blocks), in_hbm(rhs_leaf), in_hbm(linv_leaf),
        in_hbm(l_off), in_hbm(uinv_sep),
    )
    tied = lax.optimization_barrier
    groups = [[0], [1]] + [[2 + j, tiles - 1 - j] for j in range((tiles - 2) // 2)]
    inner, outer = [], []

    def move(p):
        wide = cols_n // 2
        pairs = []
        for r in range(rows_n):
            for c in range(cols_n):
                top, zl, y = r // 2 // wide, r // 2 % wide, r % 2
                to_r = (top * wide + c % wide) * 2 + ((c // wide) ^ p)
                pairs.append((r * cols_n + c, to_r * cols_n + y * wide + zl))
        return lax.ppermute(pieces[p], ("row", "col"), pairs)

    def swap_beside(x, axis, count, bit):
        if len(inner) == len(groups):
            return swap(x, axis, count, bit)
        group = groups[len(inner)]
        x, factor = tied((x, uinv_leaf))
        got = swap(x, axis, count, bit)
        length = len(group) * TILE
        ahead = pl.pallas_call(
            functools.partial(ahead_kernel, group),
            out_shape=[
                pltpu.VMEM((length, u_off.shape[2]), bf16),
                pltpu.VMEM((length, columns), jnp.float32),
            ],
            in_specs=[smem, vmem, vmem, any_space],
            out_specs=[vmem, vmem],
            scratch_shapes=[
                pltpu.VMEM((width, u_off.shape[2] + columns), bf16),
                pltpu.VMEM((length, width), bf16),
                pltpu.SemaphoreType.DMA((len(group),)),
            ],
            compiler_params=pltpu.CompilerParams(vmem_limit_bytes=16 * 2**20),
            cost_estimate=pl.CostEstimate(
                flops=600_000_000, bytes_accessed=1_000_000, transcendentals=0),
            name="leaf_ahead",
        )(in_smem(size), in_vmem(u_off), in_vmem(forward), in_hbm(factor))
        got, *ahead = tied((got, *ahead))
        inner.append(ahead[0])
        outer.append(ahead[1])
        return got

    bit = 1
    while bit < cols_n:
        got = (swap if bit == 1 else swap_beside)(send, "col", cols_n, bit)
        bit *= 2
        if bit < cols_n:
            part = keep.shape[0] // 2
            send = add(keep[part:], got[part:])
            keep = add(keep[:part], got[:part])
        else:
            keep = add(keep, got)
    bit = 1
    while bit < rows_n // 2:
        keep = add(keep, swap_beside(keep, "row", rows_n, bit))
        bit *= 2
    keep, *pieces = tied((keep, *pieces))
    got = swap(keep, "row", rows_n, rows_n // 2)
    got, *moved = tied((got, move(0), move(1)))
    keep = add(keep, got)
    sep_rhs = (rhs_sep.astype(jnp.float32) - keep.astype(jnp.float32)).astype(bf16)

    own = jnp.dot(linv_sep, sep_rhs, preferred_element_type=jnp.float32).astype(bf16)
    bit = 1
    while bit < cols_n:
        own = add(own, swap(own, "col", cols_n, bit))
        bit *= 2
    got = swap_beside(own, "row", rows_n, rows_n // 2)
    own = pl.pallas_call(
        functools.partial(separator_kernel, rows_n),
        out_shape=pltpu.VMEM((block_r, columns), bf16),
        in_specs=[vmem] * 4,
        out_specs=vmem,
        compiler_params=pltpu.CompilerParams(vmem_limit_bytes=8 * 2**20),
        name="separator_backward",
    )(in_vmem(own), in_vmem(got), *map(in_vmem, moved))
    bit = 1
    while bit < rows_n // 2:
        own = add(own, swap(own, "row", rows_n, bit))
        bit *= 2
    own = jnp.concatenate([own, swap_beside(own, "row", rows_n, rows_n // 2)], 0)
    bit = cols_n // 2
    while bit >= 1:
        got = (swap if bit == 1 else swap_beside)(own, "col", cols_n, bit)
        if bit > 1:
            own = jnp.concatenate([own, got], 0)
        bit //= 2

    solved_leaf, solved_rows = pl.pallas_call(
        functools.partial(backward_kernel, cols_n, groups),
        out_shape=[
            jax.ShapeDtypeStruct((1, width, columns), bf16),
            jax.ShapeDtypeStruct((block_r, columns), bf16),
        ],
        in_specs=[smem, smem] + [vmem] * (2 + 2 * len(groups)),
        out_specs=[any_space, any_space],
        scratch_shapes=[
            pltpu.VMEM((KB * BLK, columns), bf16),
            pltpu.VMEM((width, columns), bf16),
            pltpu.VMEM((block_r, columns), bf16),
            pltpu.SemaphoreType.DMA((tiles + 1,)),
        ],
        compiler_params=pltpu.CompilerParams(vmem_limit_bytes=16 * 2**20),
        cost_estimate=pl.CostEstimate(
            flops=270_000_000, bytes_accessed=4_000_000, transcendentals=0),
        name="leaf_backward",
    )(
        in_smem(size), in_smem(blocks), in_vmem(own), in_vmem(got),
        *map(in_vmem, inner), *map(in_vmem, outer),
    )
    return (solved_leaf, solved_rows)


def solution(mesh):
    placed = (
        P(("row", "col"), None, None),
        P("col", None),
        P(("row", "col")),
        P(("row", "col"), None),
        P(("row", "col"), None, None),
        P(("row", "col"), None, None),
        P(("row", "col"), None, None),
        P(("row", "col"), None, None),
        P("row", "col"),
        P("row", "col"),
    )
    return jax.shard_map(
        functools.partial(shards, mesh.shape["row"], mesh.shape["col"]),
        mesh=mesh,
        in_specs=placed,
        out_specs=(P(("row", "col"), None, None), P("row", None)),
        check_vma=False,
    )
```

```python
import functools

import jax
import jax.numpy as jnp
from jax import lax
from jax.experimental import pallas as pl
from jax.experimental.pallas import tpu as pltpu
from jax.sharding import PartitionSpec as P

BLK = 128
KB = 4
TILE = 256


def swap(x, axis, size, bit):
    return lax.ppermute(x, axis, [(i, i ^ bit) for i in range(size)])


def add(a, b):
    return (a.astype(jnp.float32) + b.astype(jnp.float32)).astype(jnp.bfloat16)


def place_of(share, me, size):
    apart = share ^ me
    place, bit = 0, 1
    while bit < size:
        place = place * 2 + lax.rem(lax.div(apart, bit), 2)
        bit *= 2
    return place


def forward_kernel(
    cols_n, size_in, blocks_hbm, rhs_hbm, linv_hbm, loff_hbm, usep_hbm,
    forward_ref, keep_ref, send_ref, size_ref, blocks_ref, *rest,
):
    piece_refs, (rhs_v, linv_v, loff_v, total_v, sems) = rest[:-5], rest[-5:]
    width = rhs_v.shape[0]
    tiles = width // TILE
    half = keep_ref.shape[0]
    per_share = 2 * half // cols_n // BLK
    me = lax.axis_index("col")

    step = 2 * TILE
    copies = [pltpu.make_async_copy(rhs_hbm.at[0], rhs_v, sems.at[0])]
    for i in range(tiles):
        rows = pl.ds(i * TILE, TILE)
        live = pl.ds(0, (i + 1) * TILE)
        copies.append(pltpu.make_async_copy(
            linv_hbm.at[0, rows, live], linv_v.at[rows, live], sems.at[len(copies)]))
        if i % 2:
            cols = pl.ds((i - 1) * TILE, step)
            copies.append(pltpu.make_async_copy(
                loff_hbm.at[0, :, cols], loff_v.at[:, cols], sems.at[len(copies)]))
    copies.append(pltpu.make_async_copy(blocks_hbm, blocks_ref, sems.at[len(copies)]))
    late = len(copies)
    block_r = piece_refs[0].shape[1]
    for p, piece_ref in enumerate(piece_refs):
        across = pl.multiple_of((lax.div(me, cols_n // 2) ^ p) * block_r, block_r)
        copies.append(pltpu.make_async_copy(
            usep_hbm.at[:, pl.ds(across, block_r)], piece_ref, sems.at[len(copies)]))
    ahead = 7
    for copy in copies[:ahead]:
        copy.start()

    def arrive(n):
        copies[n].wait()
        if n + ahead < len(copies):
            copies[n + ahead].start()

    def update(s):
        cols = pl.ds(s * step, step)
        return jnp.dot(loff_v[:, cols], forward_ref[cols, :], preferred_element_type=jnp.float32)

    size = size_in[0]
    size_ref[0] = size
    keep_ref[...] = jnp.zeros_like(keep_ref)
    send_ref[...] = jnp.zeros_like(send_ref)
    arrive(0)
    at = lax.broadcasted_iota(jnp.int32, rhs_v.shape, 0)
    rhs_v[...] = jnp.where(at < size, rhs_v[...], jnp.zeros_like(rhs_v))
    for s in range(tiles // 2):
        if s >= 1:
            arrive(3 * s)
        arrive(3 * s + 1)
        arrive(3 * s + 2)
        if s == 1:
            total_v[...] = update(0)
        elif s > 1:
            total_v[...] += update(s - 1)
        for i in (2 * s, 2 * s + 1):
            rows = pl.ds(i * TILE, TILE)
            live = pl.ds(0, (i + 1) * TILE)
            tile = jnp.dot(linv_v[rows, live], rhs_v[live, :], preferred_element_type=jnp.float32)
            at = lax.broadcasted_iota(jnp.int32, tile.shape, 0) + i * TILE
            forward_ref[rows, :] = jnp.where(at < size, tile, 0.0).astype(jnp.bfloat16)
    arrive(3 * (tiles // 2))
    total_v[...] += update(tiles // 2 - 1)

    for n in range(late - 1, len(copies)):
        arrive(n)
    for k in range(KB):
        block = blocks_ref[0, k]
        share = lax.div(block, per_share)
        start = (place_of(share, me, cols_n) * per_share + lax.rem(block, per_share)) * BLK
        part = total_v[pl.ds(k * BLK, BLK), :].astype(jnp.bfloat16)

        @pl.when(start < half)
        def _():
            keep_ref[pl.ds(pl.multiple_of(start, BLK), BLK), :] = part

        @pl.when(start >= half)
        def _():
            send_ref[pl.ds(pl.multiple_of(start - half, BLK), BLK), :] = part


def separator_kernel(rows_n, own_ref, got_ref, near_ref, far_ref, out_ref):
    row = lax.axis_index("row")
    top, low = lax.div(row, rows_n // 2), lax.rem(row, 2)
    straight = top == low
    first = jnp.where(straight, own_ref[...], got_ref[...])
    second = jnp.where(straight, got_ref[...], own_ref[...])
    total = jnp.dot(near_ref[...], first, preferred_element_type=jnp.float32)
    total += jnp.dot(far_ref[...], second, preferred_element_type=jnp.float32)
    out_ref[...] = total.astype(jnp.bfloat16)


def ahead_kernel(tiles_here, size_ref, uoff_ref, forward_ref, uinv_hbm, inner_ref, outer_ref,
                 both_v, uinv_v, sems):
    width, inner = uoff_ref.shape[1:]
    size = size_ref[0]
    copies = []
    for n, i in enumerate(tiles_here):
        copies.append(pltpu.make_async_copy(
            uinv_hbm.at[0, pl.ds(i * TILE, TILE), pl.ds(i * TILE, width - i * TILE)],
            uinv_v.at[pl.ds(n * TILE, TILE), pl.ds(i * TILE, width - i * TILE)],
            sems.at[n]))
        copies[-1].start()
    for j in range(min(tiles_here), width // TILE):
        rows = pl.ds(j * TILE, TILE)
        block = uoff_ref[0, rows, :]
        at = lax.broadcasted_iota(jnp.int32, block.shape, 0) + j * TILE
        both_v[rows, 0:inner] = jnp.where(at < size, block, jnp.zeros_like(block))
        both_v[rows, inner:] = forward_ref[rows, :]
    for n, i in enumerate(tiles_here):
        rows = pl.ds(n * TILE, TILE)
        live = pl.ds(i * TILE, width - i * TILE)
        copies[n].wait()
        out = jnp.dot(uinv_v[rows, live], both_v[live, :], preferred_element_type=jnp.float32)
        inner_ref[rows, :] = out[:, :inner].astype(jnp.bfloat16)
        outer_ref[rows, :] = out[:, inner:]


def backward_kernel(cols_n, groups, size_ref, blocks_ref, own_ref, got_ref, *rest):
    count = len(groups)
    inner_refs, outer_refs = rest[:count], rest[count:2 * count]
    leaf_hbm, rows_hbm, coupled_v, solved_v, rows_v, sems = rest[2 * count:]
    tiles = solved_v.shape[0] // TILE
    half = own_ref.shape[0]
    block_r = rows_hbm.shape[0]
    rows_n = 2 * half // block_r
    size = size_ref[0]
    row, col = lax.axis_index("row"), lax.axis_index("col")

    def solved_at(first, length):
        index = lax.div(first, block_r)
        top, rest = lax.div(index, rows_n // 2), lax.rem(index, rows_n // 2)
        where = lax.rem(rest, 2) * (cols_n // 2) + lax.div(rest, 2)
        place = (top ^ lax.div(row, rows_n // 2)) + 2 * place_of(where, col, cols_n)
        start = place * block_r + lax.rem(first, block_r)
        inside = start < half
        near = pl.multiple_of(jnp.where(inside, start, 0), BLK)
        far = pl.multiple_of(jnp.where(inside, 0, start - half), BLK)
        return jnp.where(inside, own_ref[pl.ds(near, length), :], got_ref[pl.ds(far, length), :])

    for k in range(KB):
        coupled_v[pl.ds(k * BLK, BLK), :] = solved_at(blocks_ref[0, k] * BLK, BLK)
    rows_v[...] = solved_at(row * block_r, block_r)
    copies = [pltpu.make_async_copy(rows_v, rows_hbm, sems.at[tiles])]
    copies[0].start()
    for group, inner_ref, outer_ref in zip(groups, inner_refs, outer_refs):
        term = jnp.dot(inner_ref[...], coupled_v[...], preferred_element_type=jnp.float32)
        for n, i in enumerate(group):
            here = slice(n * TILE, (n + 1) * TILE)
            tile = outer_ref[here, :] - term[here, :]
            at = lax.broadcasted_iota(jnp.int32, tile.shape, 0) + i * TILE
            rows = pl.ds(i * TILE, TILE)
            solved_v[rows, :] = jnp.where(at < size, tile, 0.0).astype(jnp.bfloat16)
            copies.append(pltpu.make_async_copy(
                solved_v.at[rows], leaf_hbm.at[0, rows], sems.at[i]))
            copies[-1].start()
    for copy in copies:
        copy.wait()


def shards(
    rows_n,
    cols_n,
    rhs_leaf,
    rhs_sep,
    leaf_sizes,
    off_blocks,
    linv_leaf,
    uinv_leaf,
    l_off,
    u_off,
    linv_sep,
    uinv_sep,
):
    width, columns = rhs_leaf.shape[1:]
    share = rhs_sep.shape[0]
    sep = share * cols_n
    block_r = sep // rows_n
    assert rows_n == 2 * cols_n
    tiles = width // TILE
    bf16 = jnp.bfloat16
    smem = pl.BlockSpec(memory_space=pltpu.SMEM)
    vmem = pl.BlockSpec(memory_space=pltpu.VMEM)
    any_space = pl.BlockSpec(memory_space=pl.ANY)
    in_vmem = functools.partial(pltpu.with_memory_space_constraint, memory_space=pltpu.VMEM)
    in_smem = functools.partial(pltpu.with_memory_space_constraint, memory_space=pltpu.SMEM)
    in_hbm = functools.partial(pltpu.with_memory_space_constraint, memory_space=pltpu.HBM)

    forward, keep, send, size, blocks, *pieces = pl.pallas_call(
        functools.partial(forward_kernel, cols_n),
        out_shape=[
            pltpu.VMEM((width, columns), bf16),
            pltpu.VMEM((sep // 2, columns), bf16),
            pltpu.VMEM((sep // 2, columns), bf16),
            pltpu.SMEM((1,), jnp.int32),
            pltpu.SMEM((1, KB), jnp.int32),
        ] + [pltpu.VMEM((block_r, block_r), bf16)] * 2,
        in_specs=[smem] + [any_space] * 5,
        out_specs=[vmem, vmem, vmem, smem, smem, vmem, vmem],
        scratch_shapes=[
            pltpu.VMEM((width, columns), bf16),
            pltpu.VMEM((width, width), bf16),
            pltpu.VMEM((KB * BLK, width), bf16),
            pltpu.VMEM((KB * BLK, columns), jnp.float32),
            pltpu.SemaphoreType.DMA((2 * tiles + 2,)),
        ],
        compiler_params=pltpu.CompilerParams(vmem_limit_bytes=24 * 2**20),
        cost_estimate=pl.CostEstimate(
            flops=900_000_000, bytes_accessed=8_000_000, transcendentals=0),
        name="leaf_forward",
    )(
        leaf_sizes, in_hbm(off_blocks), in_hbm(rhs_leaf), in_hbm(linv_leaf),
        in_hbm(l_off), in_hbm(uinv_sep),
    )
    tied = lax.optimization_barrier
    groups = [[0], [1]] + [[2 + j, tiles - 1 - j] for j in range((tiles - 2) // 2)]
    inner, outer = [], []

    def move(p):
        wide = cols_n // 2
        pairs = []
        for r in range(rows_n):
            for c in range(cols_n):
                top, zl, y = r // 2 // wide, r // 2 % wide, r % 2
                to_r = (top * wide + c % wide) * 2 + ((c // wide) ^ p)
                pairs.append((r * cols_n + c, to_r * cols_n + y * wide + zl))
        return lax.ppermute(pieces[p], ("row", "col"), pairs)

    def swap_beside(x, axis, count, bit):
        if len(inner) == len(groups):
            return swap(x, axis, count, bit)
        group = groups[len(inner)]
        x, factor = tied((x, uinv_leaf))
        got = swap(x, axis, count, bit)
        length = len(group) * TILE
        ahead = pl.pallas_call(
            functools.partial(ahead_kernel, group),
            out_shape=[
                pltpu.VMEM((length, u_off.shape[2]), bf16),
                pltpu.VMEM((length, columns), jnp.float32),
            ],
            in_specs=[smem, vmem, vmem, any_space],
            out_specs=[vmem, vmem],
            scratch_shapes=[
                pltpu.VMEM((width, u_off.shape[2] + columns), bf16),
                pltpu.VMEM((length, width), bf16),
                pltpu.SemaphoreType.DMA((len(group),)),
            ],
            compiler_params=pltpu.CompilerParams(vmem_limit_bytes=16 * 2**20),
            cost_estimate=pl.CostEstimate(
                flops=600_000_000, bytes_accessed=1_000_000, transcendentals=0),
            name="leaf_ahead",
        )(in_smem(size), in_vmem(u_off), in_vmem(forward), in_hbm(factor))
        got, *ahead = tied((got, *ahead))
        inner.append(ahead[0])
        outer.append(ahead[1])
        return got

    bit = 1
    while bit < cols_n:
        got = (swap if bit == 1 else swap_beside)(send, "col", cols_n, bit)
        bit *= 2
        if bit < cols_n:
            part = keep.shape[0] // 2
            send = add(keep[part:], got[part:])
            keep = add(keep[:part], got[:part])
        else:
            keep = add(keep, got)
    bit = 1
    while bit < rows_n // 2:
        keep = add(keep, swap_beside(keep, "row", rows_n, bit))
        bit *= 2
    keep, *pieces = tied((keep, *pieces))
    moved = [move(0), move(1)]
    keep = add(keep, swap(keep, "row", rows_n, rows_n // 2))
    sep_rhs = (rhs_sep.astype(jnp.float32) - keep.astype(jnp.float32)).astype(bf16)

    own = jnp.dot(linv_sep, sep_rhs, preferred_element_type=jnp.float32).astype(bf16)
    own, *moved = tied((own, *moved))
    bit = 1
    while bit < cols_n:
        own = add(own, swap(own, "col", cols_n, bit))
        bit *= 2
    got = swap_beside(own, "row", rows_n, rows_n // 2)
    own = pl.pallas_call(
        functools.partial(separator_kernel, rows_n),
        out_shape=pltpu.VMEM((block_r, columns), bf16),
        in_specs=[vmem] * 4,
        out_specs=vmem,
        compiler_params=pltpu.CompilerParams(vmem_limit_bytes=8 * 2**20),
        name="separator_backward",
    )(in_vmem(own), in_vmem(got), *map(in_vmem, moved))
    bit = 1
    while bit < rows_n // 2:
        own = add(own, swap(own, "row", rows_n, bit))
        bit *= 2
    own = jnp.concatenate([own, swap_beside(own, "row", rows_n, rows_n // 2)], 0)
    bit = cols_n // 2
    while bit >= 1:
        got = (swap if bit == 1 else swap_beside)(own, "col", cols_n, bit)
        if bit > 1:
            own = jnp.concatenate([own, got], 0)
        bit //= 2

    solved_leaf, solved_rows = pl.pallas_call(
        functools.partial(backward_kernel, cols_n, groups),
        out_shape=[
            jax.ShapeDtypeStruct((1, width, columns), bf16),
            jax.ShapeDtypeStruct((block_r, columns), bf16),
        ],
        in_specs=[smem, smem] + [vmem] * (2 + 2 * len(groups)),
        out_specs=[any_space, any_space],
        scratch_shapes=[
            pltpu.VMEM((KB * BLK, columns), bf16),
            pltpu.VMEM((width, columns), bf16),
            pltpu.VMEM((block_r, columns), bf16),
            pltpu.SemaphoreType.DMA((tiles + 1,)),
        ],
        compiler_params=pltpu.CompilerParams(vmem_limit_bytes=16 * 2**20),
        cost_estimate=pl.CostEstimate(
            flops=270_000_000, bytes_accessed=4_000_000, transcendentals=0),
        name="leaf_backward",
    )(
        in_smem(size), in_smem(blocks), in_vmem(own), in_vmem(got),
        *map(in_vmem, inner), *map(in_vmem, outer),
    )
    return (solved_leaf, solved_rows)


def solution(mesh):
    placed = (
        P(("row", "col"), None, None),
        P("col", None),
        P(("row", "col")),
        P(("row", "col"), None),
        P(("row", "col"), None, None),
        P(("row", "col"), None, None),
        P(("row", "col"), None, None),
        P(("row", "col"), None, None),
        P("row", "col"),
        P("row", "col"),
    )
    return jax.shard_map(
        functools.partial(shards, mesh.shape["row"], mesh.shape["col"]),
        mesh=mesh,
        in_specs=placed,
        out_specs=(P(("row", "col"), None, None), P("row", None)),
        check_vma=False,
    )
```

```python
import functools

import jax
import jax.numpy as jnp
from jax import lax
from jax.experimental import pallas as pl
from jax.experimental.pallas import tpu as pltpu
from jax.sharding import PartitionSpec as P

BLK = 128
KB = 4
TILE = 256


def swap(x, axis, size, bit):
    return lax.ppermute(x, axis, [(i, i ^ bit) for i in range(size)])


def add(a, b):
    return (a.astype(jnp.float32) + b.astype(jnp.float32)).astype(jnp.bfloat16)


def place_of(share, me, size):
    apart = share ^ me
    place, bit = 0, 1
    while bit < size:
        place = place * 2 + lax.rem(lax.div(apart, bit), 2)
        bit *= 2
    return place


def forward_kernel(
    cols_n, size_in, blocks_hbm, rhs_hbm, linv_hbm, loff_hbm, usep_hbm,
    forward_ref, keep_ref, send_ref, size_ref, blocks_ref, *rest,
):
    piece_refs, (rhs_v, linv_v, loff_v, total_v, sems) = rest[:-5], rest[-5:]
    width = rhs_v.shape[0]
    tiles = width // TILE
    half = keep_ref.shape[0]
    per_share = 2 * half // cols_n // BLK
    me = lax.axis_index("col")

    step = 2 * TILE
    copies = [pltpu.make_async_copy(rhs_hbm.at[0], rhs_v, sems.at[0])]
    for i in range(tiles):
        rows = pl.ds(i * TILE, TILE)
        live = pl.ds(0, (i + 1) * TILE)
        copies.append(pltpu.make_async_copy(
            linv_hbm.at[0, rows, live], linv_v.at[rows, live], sems.at[len(copies)]))
        if i % 2:
            cols = pl.ds((i - 1) * TILE, step)
            copies.append(pltpu.make_async_copy(
                loff_hbm.at[0, :, cols], loff_v.at[:, cols], sems.at[len(copies)]))
    copies.append(pltpu.make_async_copy(blocks_hbm, blocks_ref, sems.at[len(copies)]))
    late = len(copies)
    block_r = piece_refs[0].shape[1]
    for p, piece_ref in enumerate(piece_refs):
        across = pl.multiple_of((lax.div(me, cols_n // 2) ^ p) * block_r, block_r)
        copies.append(pltpu.make_async_copy(
            usep_hbm.at[:, pl.ds(across, block_r)], piece_ref, sems.at[len(copies)]))
    ahead = 7
    for copy in copies[:ahead]:
        copy.start()

    def arrive(n):
        copies[n].wait()
        if n + ahead < len(copies):
            copies[n + ahead].start()

    def update(s):
        cols = pl.ds(s * step, step)
        return jnp.dot(loff_v[:, cols], forward_ref[cols, :], preferred_element_type=jnp.float32)

    size = size_in[0]
    size_ref[0] = size
    keep_ref[...] = jnp.zeros_like(keep_ref)
    send_ref[...] = jnp.zeros_like(send_ref)
    arrive(0)
    at = lax.broadcasted_iota(jnp.int32, rhs_v.shape, 0)
    rhs_v[...] = jnp.where(at < size, rhs_v[...], jnp.zeros_like(rhs_v))
    for s in range(tiles // 2):
        if s >= 1:
            arrive(3 * s)
        arrive(3 * s + 1)
        arrive(3 * s + 2)
        if s == 1:
            total_v[...] = update(0)
        elif s > 1:
            total_v[...] += update(s - 1)
        for i in (2 * s, 2 * s + 1):
            rows = pl.ds(i * TILE, TILE)
            live = pl.ds(0, (i + 1) * TILE)
            tile = jnp.dot(linv_v[rows, live], rhs_v[live, :], preferred_element_type=jnp.float32)
            at = lax.broadcasted_iota(jnp.int32, tile.shape, 0) + i * TILE
            forward_ref[rows, :] = jnp.where(at < size, tile, 0.0).astype(jnp.bfloat16)
    arrive(3 * (tiles // 2))
    total_v[...] += update(tiles // 2 - 1)

    for n in range(late - 1, len(copies)):
        arrive(n)
    for k in range(KB):
        block = blocks_ref[0, k]
        share = lax.div(block, per_share)
        start = (place_of(share, me, cols_n) * per_share + lax.rem(block, per_share)) * BLK
        part = total_v[pl.ds(k * BLK, BLK), :].astype(jnp.bfloat16)

        @pl.when(start < half)
        def _():
            keep_ref[pl.ds(pl.multiple_of(start, BLK), BLK), :] = part

        @pl.when(start >= half)
        def _():
            send_ref[pl.ds(pl.multiple_of(start - half, BLK), BLK), :] = part


def separator_kernel(rows_n, own_ref, got_ref, near_ref, far_ref, out_ref):
    row = lax.axis_index("row")
    top, low = lax.div(row, rows_n // 2), lax.rem(row, 2)
    straight = top == low
    first = jnp.where(straight, own_ref[...], got_ref[...])
    second = jnp.where(straight, got_ref[...], own_ref[...])
    total = jnp.dot(near_ref[...], first, preferred_element_type=jnp.float32)
    total += jnp.dot(far_ref[...], second, preferred_element_type=jnp.float32)
    out_ref[...] = total.astype(jnp.bfloat16)


def ahead_kernel(tiles_here, size_ref, uoff_ref, forward_ref, uinv_hbm, inner_ref, outer_ref,
                 both_v, uinv_v, sems):
    width, inner = uoff_ref.shape[1:]
    size = size_ref[0]
    copies = []
    for n, i in enumerate(tiles_here):
        copies.append(pltpu.make_async_copy(
            uinv_hbm.at[0, pl.ds(i * TILE, TILE), pl.ds(i * TILE, width - i * TILE)],
            uinv_v.at[pl.ds(n * TILE, TILE), pl.ds(i * TILE, width - i * TILE)],
            sems.at[n]))
        copies[-1].start()
    for j in range(min(tiles_here), width // TILE):
        rows = pl.ds(j * TILE, TILE)
        block = uoff_ref[0, rows, :]
        at = lax.broadcasted_iota(jnp.int32, block.shape, 0) + j * TILE
        both_v[rows, 0:inner] = jnp.where(at < size, block, jnp.zeros_like(block))
        both_v[rows, inner:] = forward_ref[rows, :]
    for n, i in enumerate(tiles_here):
        rows = pl.ds(n * TILE, TILE)
        live = pl.ds(i * TILE, width - i * TILE)
        copies[n].wait()
        out = jnp.dot(uinv_v[rows, live], both_v[live, :], preferred_element_type=jnp.float32)
        inner_ref[rows, :] = out[:, :inner].astype(jnp.bfloat16)
        outer_ref[rows, :] = out[:, inner:]


def backward_kernel(cols_n, groups, size_ref, blocks_ref, own_ref, got_ref, *rest):
    count = len(groups)
    inner_refs, outer_refs = rest[:count], rest[count:2 * count]
    leaf_hbm, rows_hbm, coupled_v, solved_v, rows_v, sems = rest[2 * count:]
    tiles = solved_v.shape[0] // TILE
    half = own_ref.shape[0]
    block_r = rows_hbm.shape[0]
    rows_n = 2 * half // block_r
    size = size_ref[0]
    row, col = lax.axis_index("row"), lax.axis_index("col")

    def solved_at(first, length):
        index = lax.div(first, block_r)
        top, rest = lax.div(index, rows_n // 2), lax.rem(index, rows_n // 2)
        where = lax.rem(rest, 2) * (cols_n // 2) + lax.div(rest, 2)
        place = (top ^ lax.div(row, rows_n // 2)) + 2 * place_of(where, col, cols_n)
        start = place * block_r + lax.rem(first, block_r)
        inside = start < half
        near = pl.multiple_of(jnp.where(inside, start, 0), BLK)
        far = pl.multiple_of(jnp.where(inside, 0, start - half), BLK)
        return jnp.where(inside, own_ref[pl.ds(near, length), :], got_ref[pl.ds(far, length), :])

    for k in range(KB):
        coupled_v[pl.ds(k * BLK, BLK), :] = solved_at(blocks_ref[0, k] * BLK, BLK)
    rows_v[...] = solved_at(row * block_r, block_r)
    copies = [pltpu.make_async_copy(rows_v, rows_hbm, sems.at[tiles])]
    copies[0].start()
    for group, inner_ref, outer_ref in zip(groups, inner_refs, outer_refs):
        term = jnp.dot(inner_ref[...], coupled_v[...], preferred_element_type=jnp.float32)
        for n, i in enumerate(group):
            here = slice(n * TILE, (n + 1) * TILE)
            tile = outer_ref[here, :] - term[here, :]
            at = lax.broadcasted_iota(jnp.int32, tile.shape, 0) + i * TILE
            rows = pl.ds(i * TILE, TILE)
            solved_v[rows, :] = jnp.where(at < size, tile, 0.0).astype(jnp.bfloat16)
            copies.append(pltpu.make_async_copy(
                solved_v.at[rows], leaf_hbm.at[0, rows], sems.at[i]))
            copies[-1].start()
    for copy in copies:
        copy.wait()


def shards(
    rows_n,
    cols_n,
    rhs_leaf,
    rhs_sep,
    leaf_sizes,
    off_blocks,
    linv_leaf,
    uinv_leaf,
    l_off,
    u_off,
    linv_sep,
    uinv_sep,
):
    width, columns = rhs_leaf.shape[1:]
    share = rhs_sep.shape[0]
    sep = share * cols_n
    block_r = sep // rows_n
    assert rows_n == 2 * cols_n
    tiles = width // TILE
    bf16 = jnp.bfloat16
    smem = pl.BlockSpec(memory_space=pltpu.SMEM)
    vmem = pl.BlockSpec(memory_space=pltpu.VMEM)
    any_space = pl.BlockSpec(memory_space=pl.ANY)
    in_vmem = functools.partial(pltpu.with_memory_space_constraint, memory_space=pltpu.VMEM)
    in_smem = functools.partial(pltpu.with_memory_space_constraint, memory_space=pltpu.SMEM)
    in_hbm = functools.partial(pltpu.with_memory_space_constraint, memory_space=pltpu.HBM)

    forward, keep, send, size, blocks, *pieces = pl.pallas_call(
        functools.partial(forward_kernel, cols_n),
        out_shape=[
            pltpu.VMEM((width, columns), bf16),
            pltpu.VMEM((sep // 2, columns), bf16),
            pltpu.VMEM((sep // 2, columns), bf16),
            pltpu.SMEM((1,), jnp.int32),
            pltpu.SMEM((1, KB), jnp.int32),
        ] + [pltpu.VMEM((block_r, block_r), bf16)] * 2,
        in_specs=[smem] + [any_space] * 5,
        out_specs=[vmem, vmem, vmem, smem, smem, vmem, vmem],
        scratch_shapes=[
            pltpu.VMEM((width, columns), bf16),
            pltpu.VMEM((width, width), bf16),
            pltpu.VMEM((KB * BLK, width), bf16),
            pltpu.VMEM((KB * BLK, columns), jnp.float32),
            pltpu.SemaphoreType.DMA((2 * tiles + 2,)),
        ],
        compiler_params=pltpu.CompilerParams(vmem_limit_bytes=24 * 2**20),
        cost_estimate=pl.CostEstimate(
            flops=900_000_000, bytes_accessed=8_000_000, transcendentals=0),
        name="leaf_forward",
    )(
        leaf_sizes, in_hbm(off_blocks), in_hbm(rhs_leaf), in_hbm(linv_leaf),
        in_hbm(l_off), in_hbm(uinv_sep),
    )
    tied = lax.optimization_barrier
    groups = [[0], [1]] + [[2 + j, tiles - 1 - j] for j in range((tiles - 2) // 2)]
    inner, outer, moved = [], [], []

    def move(p):
        wide = cols_n // 2
        pairs = []
        for r in range(rows_n):
            for c in range(cols_n):
                top, zl, y = r // 2 // wide, r // 2 % wide, r % 2
                to_r = (top * wide + c % wide) * 2 + ((c // wide) ^ p)
                pairs.append((r * cols_n + c, to_r * cols_n + y * wide + zl))
        return lax.ppermute(pieces[p], ("row", "col"), pairs)

    def swap_and_move(x, axis, count, bit):
        x, piece = tied((x, pieces[len(moved)]))
        pieces[len(moved)] = piece
        moved.append(move(len(moved)))
        return swap(x, axis, count, bit)

    def swap_beside(x, axis, count, bit):
        if len(inner) == len(groups):
            return swap(x, axis, count, bit)
        group = groups[len(inner)]
        x, factor = tied((x, uinv_leaf))
        if moved and len(inner) < 2:
            factor, moved[-1] = tied((factor, moved[-1]))
        got = swap(x, axis, count, bit)
        length = len(group) * TILE
        ahead = pl.pallas_call(
            functools.partial(ahead_kernel, group),
            out_shape=[
                pltpu.VMEM((length, u_off.shape[2]), bf16),
                pltpu.VMEM((length, columns), jnp.float32),
            ],
            in_specs=[smem, vmem, vmem, any_space],
            out_specs=[vmem, vmem],
            scratch_shapes=[
                pltpu.VMEM((width, u_off.shape[2] + columns), bf16),
                pltpu.VMEM((length, width), bf16),
                pltpu.SemaphoreType.DMA((len(group),)),
            ],
            compiler_params=pltpu.CompilerParams(vmem_limit_bytes=16 * 2**20),
            cost_estimate=pl.CostEstimate(
                flops=600_000_000, bytes_accessed=1_000_000, transcendentals=0),
            name="leaf_ahead",
        )(in_smem(size), in_vmem(u_off), in_vmem(forward), in_hbm(factor))
        got, *ahead = tied((got, *ahead))
        inner.append(ahead[0])
        outer.append(ahead[1])
        return got

    def swap_busy(x, axis, count, bit):
        turn = len(moved) == len(inner) and len(moved) < 2
        return (swap_and_move if turn else swap_beside)(x, axis, count, bit)

    bit = 1
    while bit < cols_n:
        got = (swap if bit == 1 else swap_busy)(send, "col", cols_n, bit)
        bit *= 2
        if bit < cols_n:
            part = keep.shape[0] // 2
            send = add(keep[part:], got[part:])
            keep = add(keep[:part], got[:part])
        else:
            keep = add(keep, got)
    bit = 1
    while bit < rows_n:
        keep = add(keep, swap_busy(keep, "row", rows_n, bit))
        bit *= 2
    sep_rhs = (rhs_sep.astype(jnp.float32) - keep.astype(jnp.float32)).astype(bf16)

    own = jnp.dot(linv_sep, sep_rhs, preferred_element_type=jnp.float32).astype(bf16)
    bit = 1
    while bit < cols_n:
        own = add(own, swap(own, "col", cols_n, bit))
        bit *= 2
    got = swap_beside(own, "row", rows_n, rows_n // 2)
    own = pl.pallas_call(
        functools.partial(separator_kernel, rows_n),
        out_shape=pltpu.VMEM((block_r, columns), bf16),
        in_specs=[vmem] * 4,
        out_specs=vmem,
        compiler_params=pltpu.CompilerParams(vmem_limit_bytes=8 * 2**20),
        name="separator_backward",
    )(in_vmem(own), in_vmem(got), *map(in_vmem, moved))
    bit = 1
    while bit < rows_n // 2:
        own = add(own, swap(own, "row", rows_n, bit))
        bit *= 2
    own = jnp.concatenate([own, swap_beside(own, "row", rows_n, rows_n // 2)], 0)
    bit = cols_n // 2
    while bit >= 1:
        got = (swap if bit == 1 else swap_beside)(own, "col", cols_n, bit)
        if bit > 1:
            own = jnp.concatenate([own, got], 0)
        bit //= 2

    solved_leaf, solved_rows = pl.pallas_call(
        functools.partial(backward_kernel, cols_n, groups),
        out_shape=[
            jax.ShapeDtypeStruct((1, width, columns), bf16),
            jax.ShapeDtypeStruct((block_r, columns), bf16),
        ],
        in_specs=[smem, smem] + [vmem] * (2 + 2 * len(groups)),
        out_specs=[any_space, any_space],
        scratch_shapes=[
            pltpu.VMEM((KB * BLK, columns), bf16),
            pltpu.VMEM((width, columns), bf16),
            pltpu.VMEM((block_r, columns), bf16),
            pltpu.SemaphoreType.DMA((tiles + 1,)),
        ],
        compiler_params=pltpu.CompilerParams(vmem_limit_bytes=16 * 2**20),
        cost_estimate=pl.CostEstimate(
            flops=270_000_000, bytes_accessed=4_000_000, transcendentals=0),
        name="leaf_backward",
    )(
        in_smem(size), in_smem(blocks), in_vmem(own), in_vmem(got),
        *map(in_vmem, inner), *map(in_vmem, outer),
    )
    return (solved_leaf, solved_rows)


def solution(mesh):
    placed = (
        P(("row", "col"), None, None),
        P("col", None),
        P(("row", "col")),
        P(("row", "col"), None),
        P(("row", "col"), None, None),
        P(("row", "col"), None, None),
        P(("row", "col"), None, None),
        P(("row", "col"), None, None),
        P("row", "col"),
        P("row", "col"),
    )
    return jax.shard_map(
        functools.partial(shards, mesh.shape["row"], mesh.shape["col"]),
        mesh=mesh,
        in_specs=placed,
        out_specs=(P(("row", "col"), None, None), P("row", None)),
        check_vma=False,
    )
```

```python
import functools

import jax
import jax.numpy as jnp
from jax import lax
from jax.experimental import pallas as pl
from jax.experimental.pallas import tpu as pltpu
from jax.sharding import PartitionSpec as P

BLK = 128
KB = 4
TILE = 256


def swap(x, axis, size, bit):
    return lax.ppermute(x, axis, [(i, i ^ bit) for i in range(size)])


def swap_both(x, rows_n, cols_n, row_bit, col_bit):
    pairs = []
    for r in range(rows_n):
        for c in range(cols_n):
            pairs.append((r * cols_n + c, (r ^ row_bit) * cols_n + (c ^ col_bit)))
    return lax.ppermute(x, ("row", "col"), pairs)


def add(a, b):
    return (a.astype(jnp.float32) + b.astype(jnp.float32)).astype(jnp.bfloat16)


def place_of(share, me, size):
    apart = share ^ me
    place, bit = 0, 1
    while bit < size:
        place = place * 2 + lax.rem(lax.div(apart, bit), 2)
        bit *= 2
    return place


def forward_kernel(
    cols_n, size_in, blocks_hbm, rhs_hbm, linv_hbm, loff_hbm, usep_hbm,
    forward_ref, keep_ref, send_ref, size_ref, blocks_ref, *rest,
):
    piece_refs, (rhs_v, linv_v, loff_v, total_v, sems) = rest[:-5], rest[-5:]
    width = rhs_v.shape[0]
    tiles = width // TILE
    half = keep_ref.shape[0]
    per_share = 2 * half // cols_n // BLK
    me = lax.axis_index("col")

    step = 2 * TILE
    copies = [pltpu.make_async_copy(rhs_hbm.at[0], rhs_v, sems.at[0])]
    for i in range(tiles):
        rows = pl.ds(i * TILE, TILE)
        live = pl.ds(0, (i + 1) * TILE)
        copies.append(pltpu.make_async_copy(
            linv_hbm.at[0, rows, live], linv_v.at[rows, live], sems.at[len(copies)]))
        if i % 2:
            cols = pl.ds((i - 1) * TILE, step)
            copies.append(pltpu.make_async_copy(
                loff_hbm.at[0, :, cols], loff_v.at[:, cols], sems.at[len(copies)]))
    copies.append(pltpu.make_async_copy(blocks_hbm, blocks_ref, sems.at[len(copies)]))
    late = len(copies)
    block_r = piece_refs[0].shape[1]
    for p, piece_ref in enumerate(piece_refs):
        across = pl.multiple_of((lax.div(me, cols_n // 2) ^ p) * block_r, block_r)
        copies.append(pltpu.make_async_copy(
            usep_hbm.at[:, pl.ds(across, block_r)], piece_ref, sems.at[len(copies)]))
    ahead = 7
    for copy in copies[:ahead]:
        copy.start()

    def arrive(n):
        copies[n].wait()
        if n + ahead < len(copies):
            copies[n + ahead].start()

    def update(s):
        cols = pl.ds(s * step, step)
        return jnp.dot(loff_v[:, cols], forward_ref[cols, :], preferred_element_type=jnp.float32)

    size = size_in[0]
    size_ref[0] = size
    keep_ref[...] = jnp.zeros_like(keep_ref)
    send_ref[...] = jnp.zeros_like(send_ref)
    arrive(0)
    at = lax.broadcasted_iota(jnp.int32, rhs_v.shape, 0)
    rhs_v[...] = jnp.where(at < size, rhs_v[...], jnp.zeros_like(rhs_v))
    for s in range(tiles // 2):
        if s >= 1:
            arrive(3 * s)
        arrive(3 * s + 1)
        arrive(3 * s + 2)
        if s == 1:
            total_v[...] = update(0)
        elif s > 1:
            total_v[...] += update(s - 1)
        for i in (2 * s, 2 * s + 1):
            rows = pl.ds(i * TILE, TILE)
            live = pl.ds(0, (i + 1) * TILE)
            tile = jnp.dot(linv_v[rows, live], rhs_v[live, :], preferred_element_type=jnp.float32)
            at = lax.broadcasted_iota(jnp.int32, tile.shape, 0) + i * TILE
            forward_ref[rows, :] = jnp.where(at < size, tile, 0.0).astype(jnp.bfloat16)
    arrive(3 * (tiles // 2))
    total_v[...] += update(tiles // 2 - 1)

    for n in range(late - 1, len(copies)):
        arrive(n)
    for k in range(KB):
        block = blocks_ref[0, k]
        share = lax.div(block, per_share)
        start = (place_of(share, me, cols_n) * per_share + lax.rem(block, per_share)) * BLK
        part = total_v[pl.ds(k * BLK, BLK), :].astype(jnp.bfloat16)

        @pl.when(start < half)
        def _():
            keep_ref[pl.ds(pl.multiple_of(start, BLK), BLK), :] = part

        @pl.when(start >= half)
        def _():
            send_ref[pl.ds(pl.multiple_of(start - half, BLK), BLK), :] = part


def separator_kernel(rows_n, own_ref, got_ref, near_ref, far_ref, out_ref):
    row = lax.axis_index("row")
    top, low = lax.div(row, rows_n // 2), lax.rem(row, 2)
    straight = top == low
    first = jnp.where(straight, own_ref[...], got_ref[...])
    second = jnp.where(straight, got_ref[...], own_ref[...])
    total = jnp.dot(near_ref[...], first, preferred_element_type=jnp.float32)
    total += jnp.dot(far_ref[...], second, preferred_element_type=jnp.float32)
    out_ref[...] = total.astype(jnp.bfloat16)


def ahead_kernel(tiles_here, size_ref, uoff_ref, forward_ref, uinv_hbm, inner_ref, outer_ref,
                 both_v, uinv_v, sems):
    width, inner = uoff_ref.shape[1:]
    size = size_ref[0]
    copies = []
    for n, i in enumerate(tiles_here):
        copies.append(pltpu.make_async_copy(
            uinv_hbm.at[0, pl.ds(i * TILE, TILE), pl.ds(i * TILE, width - i * TILE)],
            uinv_v.at[pl.ds(n * TILE, TILE), pl.ds(i * TILE, width - i * TILE)],
            sems.at[n]))
        copies[-1].start()
    for j in range(min(tiles_here), width // TILE):
        rows = pl.ds(j * TILE, TILE)
        block = uoff_ref[0, rows, :]
        at = lax.broadcasted_iota(jnp.int32, block.shape, 0) + j * TILE
        both_v[rows, 0:inner] = jnp.where(at < size, block, jnp.zeros_like(block))
        both_v[rows, inner:] = forward_ref[rows, :]
    for n, i in enumerate(tiles_here):
        rows = pl.ds(n * TILE, TILE)
        live = pl.ds(i * TILE, width - i * TILE)
        copies[n].wait()
        out = jnp.dot(uinv_v[rows, live], both_v[live, :], preferred_element_type=jnp.float32)
        inner_ref[rows, :] = out[:, :inner].astype(jnp.bfloat16)
        outer_ref[rows, :] = out[:, inner:]


def backward_kernel(cols_n, groups, size_ref, blocks_ref, own_ref, got_ref, *rest):
    count = len(groups)
    inner_refs, outer_refs = rest[:count], rest[count:2 * count]
    leaf_hbm, rows_hbm, coupled_v, solved_v, rows_v, sems = rest[2 * count:]
    tiles = solved_v.shape[0] // TILE
    half = own_ref.shape[0]
    block_r = rows_hbm.shape[0]
    rows_n = 2 * half // block_r
    size = size_ref[0]
    row, col = lax.axis_index("row"), lax.axis_index("col")

    def solved_at(first, length):
        index = lax.div(first, block_r)
        top, rest = lax.div(index, rows_n // 2), lax.rem(index, rows_n // 2)
        where = lax.rem(rest, 2) * (cols_n // 2) + lax.div(rest, 2)
        place = (top ^ lax.div(row, rows_n // 2)) + 2 * place_of(where, col, cols_n)
        start = place * block_r + lax.rem(first, block_r)
        inside = start < half
        near = pl.multiple_of(jnp.where(inside, start, 0), BLK)
        far = pl.multiple_of(jnp.where(inside, 0, start - half), BLK)
        return jnp.where(inside, own_ref[pl.ds(near, length), :], got_ref[pl.ds(far, length), :])

    for k in range(KB):
        coupled_v[pl.ds(k * BLK, BLK), :] = solved_at(blocks_ref[0, k] * BLK, BLK)
    rows_v[...] = solved_at(row * block_r, block_r)
    copies = [pltpu.make_async_copy(rows_v, rows_hbm, sems.at[tiles])]
    copies[0].start()
    for group, inner_ref, outer_ref in zip(groups, inner_refs, outer_refs):
        term = jnp.dot(inner_ref[...], coupled_v[...], preferred_element_type=jnp.float32)
        for n, i in enumerate(group):
            here = slice(n * TILE, (n + 1) * TILE)
            tile = outer_ref[here, :] - term[here, :]
            at = lax.broadcasted_iota(jnp.int32, tile.shape, 0) + i * TILE
            rows = pl.ds(i * TILE, TILE)
            solved_v[rows, :] = jnp.where(at < size, tile, 0.0).astype(jnp.bfloat16)
            copies.append(pltpu.make_async_copy(
                solved_v.at[rows], leaf_hbm.at[0, rows], sems.at[i]))
            copies[-1].start()
    for copy in copies:
        copy.wait()


def shards(
    rows_n,
    cols_n,
    rhs_leaf,
    rhs_sep,
    leaf_sizes,
    off_blocks,
    linv_leaf,
    uinv_leaf,
    l_off,
    u_off,
    linv_sep,
    uinv_sep,
):
    width, columns = rhs_leaf.shape[1:]
    share = rhs_sep.shape[0]
    sep = share * cols_n
    block_r = sep // rows_n
    assert rows_n == 2 * cols_n and rows_n >= 8
    tiles = width // TILE
    bf16 = jnp.bfloat16
    smem = pl.BlockSpec(memory_space=pltpu.SMEM)
    vmem = pl.BlockSpec(memory_space=pltpu.VMEM)
    any_space = pl.BlockSpec(memory_space=pl.ANY)
    in_vmem = functools.partial(pltpu.with_memory_space_constraint, memory_space=pltpu.VMEM)
    in_smem = functools.partial(pltpu.with_memory_space_constraint, memory_space=pltpu.SMEM)
    in_hbm = functools.partial(pltpu.with_memory_space_constraint, memory_space=pltpu.HBM)

    forward, keep, send, size, blocks, *pieces = pl.pallas_call(
        functools.partial(forward_kernel, cols_n),
        out_shape=[
            pltpu.VMEM((width, columns), bf16),
            pltpu.VMEM((sep // 2, columns), bf16),
            pltpu.VMEM((sep // 2, columns), bf16),
            pltpu.SMEM((1,), jnp.int32),
            pltpu.SMEM((1, KB), jnp.int32),
        ] + [pltpu.VMEM((block_r, block_r), bf16)] * 2,
        in_specs=[smem] + [any_space] * 5,
        out_specs=[vmem, vmem, vmem, smem, smem, vmem, vmem],
        scratch_shapes=[
            pltpu.VMEM((width, columns), bf16),
            pltpu.VMEM((width, width), bf16),
            pltpu.VMEM((KB * BLK, width), bf16),
            pltpu.VMEM((KB * BLK, columns), jnp.float32),
            pltpu.SemaphoreType.DMA((2 * tiles + 2,)),
        ],
        compiler_params=pltpu.CompilerParams(vmem_limit_bytes=24 * 2**20),
        cost_estimate=pl.CostEstimate(
            flops=900_000_000, bytes_accessed=8_000_000, transcendentals=0),
        name="leaf_forward",
    )(
        leaf_sizes, in_hbm(off_blocks), in_hbm(rhs_leaf), in_hbm(linv_leaf),
        in_hbm(l_off), in_hbm(uinv_sep),
    )
    tied = lax.optimization_barrier
    groups = [[0], [1]] + [[2 + j, tiles - 1 - j] for j in range((tiles - 2) // 2)]
    inner, outer, moved = [], [], []

    def move(p):
        wide = cols_n // 2
        pairs = []
        for r in range(rows_n):
            for c in range(cols_n):
                top, zl, y = r // 2 // wide, r // 2 % wide, r % 2
                to_r = (top * wide + c % wide) * 2 + ((c // wide) ^ p)
                pairs.append((r * cols_n + c, to_r * cols_n + y * wide + zl))
        return lax.ppermute(pieces[p], ("row", "col"), pairs)

    def swap_and_move(x, axis, count, bit):
        x, piece = tied((x, pieces[len(moved)]))
        pieces[len(moved)] = piece
        moved.append(move(len(moved)))
        return swap(x, axis, count, bit)

    def swap_beside(x, axis, count, bit):
        return beside(x, lambda part: [swap(part, axis, count, bit)])[0]

    def beside(x, exchange):
        if len(inner) == len(groups):
            return exchange(x)
        group = groups[len(inner)]
        x, factor = tied((x, uinv_leaf))
        if moved and len(inner) < 2:
            factor, moved[-1] = tied((factor, moved[-1]))
        got = exchange(x)
        length = len(group) * TILE
        ahead = pl.pallas_call(
            functools.partial(ahead_kernel, group),
            out_shape=[
                pltpu.VMEM((length, u_off.shape[2]), bf16),
                pltpu.VMEM((length, columns), jnp.float32),
            ],
            in_specs=[smem, vmem, vmem, any_space],
            out_specs=[vmem, vmem],
            scratch_shapes=[
                pltpu.VMEM((width, u_off.shape[2] + columns), bf16),
                pltpu.VMEM((length, width), bf16),
                pltpu.SemaphoreType.DMA((len(group),)),
            ],
            compiler_params=pltpu.CompilerParams(vmem_limit_bytes=16 * 2**20),
            cost_estimate=pl.CostEstimate(
                flops=600_000_000, bytes_accessed=1_000_000, transcendentals=0),
            name="leaf_ahead",
        )(in_smem(size), in_vmem(u_off), in_vmem(forward), in_hbm(factor))
        *got, first, second = tied((*got, *ahead))
        inner.append(first)
        outer.append(second)
        return got

    def swap_busy(x, axis, count, bit):
        turn = len(moved) == len(inner) and len(moved) < 2
        return (swap_and_move if turn else swap_beside)(x, axis, count, bit)

    bit = 1
    while bit < cols_n:
        got = (swap if bit == 1 else swap_busy)(send, "col", cols_n, bit)
        bit *= 2
        if bit < cols_n:
            part = keep.shape[0] // 2
            send = add(keep[part:], got[part:])
            keep = add(keep[:part], got[:part])
        else:
            keep = add(keep, got)
    bit = 1
    while bit < rows_n:
        keep = add(keep, swap_busy(keep, "row", rows_n, bit))
        bit *= 2
    sep_rhs = (rhs_sep.astype(jnp.float32) - keep.astype(jnp.float32)).astype(bf16)

    own = jnp.dot(linv_sep, sep_rhs, preferred_element_type=jnp.float32).astype(bf16)
    bit = 1
    while bit < cols_n // 2:
        own = add(own, swap(own, "col", cols_n, bit))
        bit *= 2
    near, far, both = beside(own, lambda part: [
        swap_both(part, rows_n, cols_n, 0, cols_n // 2),
        swap_both(part, rows_n, cols_n, rows_n // 2, 0),
        swap_both(part, rows_n, cols_n, rows_n // 2, cols_n // 2),
    ])
    own, got = add(own, near), add(far, both)
    own = pl.pallas_call(
        functools.partial(separator_kernel, rows_n),
        out_shape=pltpu.VMEM((block_r, columns), bf16),
        in_specs=[vmem] * 4,
        out_specs=vmem,
        compiler_params=pltpu.CompilerParams(vmem_limit_bytes=8 * 2**20),
        name="separator_backward",
    )(in_vmem(own), in_vmem(got), *map(in_vmem, moved))
    near, far, both = [swap(own, "row", rows_n, bits) for bits in (1, 2, 3)]
    own = (own.astype(jnp.float32) + near.astype(jnp.float32)) + (
        far.astype(jnp.float32) + both.astype(jnp.float32))
    own = own.astype(bf16)
    bit = 4
    while bit < rows_n // 2:
        own = add(own, swap(own, "row", rows_n, bit))
        bit *= 2
    own = jnp.concatenate([own, swap_beside(own, "row", rows_n, rows_n // 2)], 0)
    bit = cols_n // 2
    while bit >= 1:
        got = (swap if bit == 1 else swap_beside)(own, "col", cols_n, bit)
        if bit > 1:
            own = jnp.concatenate([own, got], 0)
        bit //= 2

    solved_leaf, solved_rows = pl.pallas_call(
        functools.partial(backward_kernel, cols_n, groups),
        out_shape=[
            jax.ShapeDtypeStruct((1, width, columns), bf16),
            jax.ShapeDtypeStruct((block_r, columns), bf16),
        ],
        in_specs=[smem, smem] + [vmem] * (2 + 2 * len(groups)),
        out_specs=[any_space, any_space],
        scratch_shapes=[
            pltpu.VMEM((KB * BLK, columns), bf16),
            pltpu.VMEM((width, columns), bf16),
            pltpu.VMEM((block_r, columns), bf16),
            pltpu.SemaphoreType.DMA((tiles + 1,)),
        ],
        compiler_params=pltpu.CompilerParams(vmem_limit_bytes=16 * 2**20),
        cost_estimate=pl.CostEstimate(
            flops=270_000_000, bytes_accessed=4_000_000, transcendentals=0),
        name="leaf_backward",
    )(
        in_smem(size), in_smem(blocks), in_vmem(own), in_vmem(got),
        *map(in_vmem, inner), *map(in_vmem, outer),
    )
    return (solved_leaf, solved_rows)


def solution(mesh):
    placed = (
        P(("row", "col"), None, None),
        P("col", None),
        P(("row", "col")),
        P(("row", "col"), None),
        P(("row", "col"), None, None),
        P(("row", "col"), None, None),
        P(("row", "col"), None, None),
        P(("row", "col"), None, None),
        P("row", "col"),
        P("row", "col"),
    )
    return jax.shard_map(
        functools.partial(shards, mesh.shape["row"], mesh.shape["col"]),
        mesh=mesh,
        in_specs=placed,
        out_specs=(P(("row", "col"), None, None), P("row", None)),
        check_vma=False,
    )
```

```python
import functools

import jax
import jax.numpy as jnp
from jax import lax
from jax.experimental import pallas as pl
from jax.experimental.pallas import tpu as pltpu
from jax.sharding import PartitionSpec as P

BLK = 128
KB = 4
TILE = 256


def swap(x, axis, size, bit):
    return lax.ppermute(x, axis, [(i, i ^ bit) for i in range(size)])


def swap_both(x, rows_n, cols_n, row_bit, col_bit):
    pairs = []
    for r in range(rows_n):
        for c in range(cols_n):
            pairs.append((r * cols_n + c, (r ^ row_bit) * cols_n + (c ^ col_bit)))
    return lax.ppermute(x, ("row", "col"), pairs)


def add(a, b):
    return (a.astype(jnp.float32) + b.astype(jnp.float32)).astype(jnp.bfloat16)


def place_of(share, me, size):
    apart = share ^ me
    place, bit = 0, 1
    while bit < size:
        place = place * 2 + lax.rem(lax.div(apart, bit), 2)
        bit *= 2
    return place


def forward_kernel(
    cols_n, size_in, blocks_hbm, rhs_hbm, linv_hbm, loff_hbm, usep_hbm,
    forward_ref, keep_ref, send_ref, size_ref, blocks_ref, *rest,
):
    piece_refs, (rhs_v, linv_v, loff_v, total_v, sems) = rest[:-5], rest[-5:]
    width = rhs_v.shape[0]
    tiles = width // TILE
    half = keep_ref.shape[0]
    per_share = 2 * half // cols_n // BLK
    me = lax.axis_index("col")

    step = 2 * TILE
    copies = [pltpu.make_async_copy(rhs_hbm.at[0], rhs_v, sems.at[0])]
    for i in range(tiles):
        rows = pl.ds(i * TILE, TILE)
        live = pl.ds(0, (i + 1) * TILE)
        copies.append(pltpu.make_async_copy(
            linv_hbm.at[0, rows, live], linv_v.at[rows, live], sems.at[len(copies)]))
        if i % 2:
            cols = pl.ds((i - 1) * TILE, step)
            copies.append(pltpu.make_async_copy(
                loff_hbm.at[0, :, cols], loff_v.at[:, cols], sems.at[len(copies)]))
    copies.append(pltpu.make_async_copy(blocks_hbm, blocks_ref, sems.at[len(copies)]))
    late = len(copies)
    block_r = piece_refs[0].shape[1]
    for p, piece_ref in enumerate(piece_refs):
        across = pl.multiple_of((lax.div(me, cols_n // 2) ^ p) * block_r, block_r)
        copies.append(pltpu.make_async_copy(
            usep_hbm.at[:, pl.ds(across, block_r)], piece_ref, sems.at[len(copies)]))
    ahead = 7
    for copy in copies[:ahead]:
        copy.start()

    def arrive(n):
        copies[n].wait()
        if n + ahead < len(copies):
            copies[n + ahead].start()

    def update(s):
        cols = pl.ds(s * step, step)
        return jnp.dot(loff_v[:, cols], forward_ref[cols, :], preferred_element_type=jnp.float32)

    size = size_in[0]
    size_ref[0] = size
    keep_ref[...] = jnp.zeros_like(keep_ref)
    send_ref[...] = jnp.zeros_like(send_ref)
    arrive(0)
    at = lax.broadcasted_iota(jnp.int32, rhs_v.shape, 0)
    rhs_v[...] = jnp.where(at < size, rhs_v[...], jnp.zeros_like(rhs_v))
    for s in range(tiles // 2):
        if s >= 1:
            arrive(3 * s)
        arrive(3 * s + 1)
        arrive(3 * s + 2)
        if s == 1:
            total_v[...] = update(0)
        elif s > 1:
            total_v[...] += update(s - 1)
        for i in (2 * s, 2 * s + 1):
            rows = pl.ds(i * TILE, TILE)
            live = pl.ds(0, (i + 1) * TILE)
            tile = jnp.dot(linv_v[rows, live], rhs_v[live, :], preferred_element_type=jnp.float32)
            at = lax.broadcasted_iota(jnp.int32, tile.shape, 0) + i * TILE
            forward_ref[rows, :] = jnp.where(at < size, tile, 0.0).astype(jnp.bfloat16)
    arrive(3 * (tiles // 2))
    total_v[...] += update(tiles // 2 - 1)

    for n in range(late - 1, len(copies)):
        arrive(n)
    for k in range(KB):
        block = blocks_ref[0, k]
        share = lax.div(block, per_share)
        start = (place_of(share, me, cols_n) * per_share + lax.rem(block, per_share)) * BLK
        part = total_v[pl.ds(k * BLK, BLK), :].astype(jnp.bfloat16)

        @pl.when(start < half)
        def _():
            keep_ref[pl.ds(pl.multiple_of(start, BLK), BLK), :] = part

        @pl.when(start >= half)
        def _():
            send_ref[pl.ds(pl.multiple_of(start - half, BLK), BLK), :] = part


def separator_kernel(rows_n, own_ref, got_ref, near_ref, far_ref, out_ref):
    row = lax.axis_index("row")
    top, low = lax.div(row, rows_n // 2), lax.rem(row, 2)
    straight = top == low
    first = jnp.where(straight, own_ref[...], got_ref[...])
    second = jnp.where(straight, got_ref[...], own_ref[...])
    total = jnp.dot(near_ref[...], first, preferred_element_type=jnp.float32)
    total += jnp.dot(far_ref[...], second, preferred_element_type=jnp.float32)
    out_ref[...] = total.astype(jnp.bfloat16)


def ahead_kernel(tiles_here, size_ref, uoff_ref, forward_ref, uinv_hbm, inner_ref, outer_ref,
                 both_v, uinv_v, sems):
    width, inner = uoff_ref.shape[1:]
    size = size_ref[0]
    copies = []
    for n, i in enumerate(tiles_here):
        copies.append(pltpu.make_async_copy(
            uinv_hbm.at[0, pl.ds(i * TILE, TILE), pl.ds(i * TILE, width - i * TILE)],
            uinv_v.at[pl.ds(n * TILE, TILE), pl.ds(i * TILE, width - i * TILE)],
            sems.at[n]))
        copies[-1].start()
    for j in range(min(tiles_here), width // TILE):
        rows = pl.ds(j * TILE, TILE)
        block = uoff_ref[0, rows, :]
        at = lax.broadcasted_iota(jnp.int32, block.shape, 0) + j * TILE
        both_v[rows, 0:inner] = jnp.where(at < size, block, jnp.zeros_like(block))
        both_v[rows, inner:] = forward_ref[rows, :]
    for n, i in enumerate(tiles_here):
        rows = pl.ds(n * TILE, TILE)
        live = pl.ds(i * TILE, width - i * TILE)
        copies[n].wait()
        out = jnp.dot(uinv_v[rows, live], both_v[live, :], preferred_element_type=jnp.float32)
        inner_ref[rows, :] = out[:, :inner].astype(jnp.bfloat16)
        outer_ref[rows, :] = out[:, inner:]


def backward_kernel(cols_n, groups, size_ref, blocks_ref, own_ref, got_ref, *rest):
    count = len(groups)
    inner_refs, outer_refs = rest[:count], rest[count:2 * count]
    leaf_hbm, rows_hbm, coupled_v, solved_v, rows_v, sems = rest[2 * count:]
    tiles = solved_v.shape[0] // TILE
    half = own_ref.shape[0]
    block_r = rows_hbm.shape[0]
    rows_n = 2 * half // block_r
    size = size_ref[0]
    row, col = lax.axis_index("row"), lax.axis_index("col")

    def solved_at(first, length):
        index = lax.div(first, block_r)
        top, rest = lax.div(index, rows_n // 2), lax.rem(index, rows_n // 2)
        where = lax.rem(rest, 2) * (cols_n // 2) + lax.div(rest, 2)
        place = (top ^ lax.div(row, rows_n // 2)) + 2 * place_of(where, col, cols_n)
        start = place * block_r + lax.rem(first, block_r)
        inside = start < half
        near = pl.multiple_of(jnp.where(inside, start, 0), BLK)
        far = pl.multiple_of(jnp.where(inside, 0, start - half), BLK)
        return jnp.where(inside, own_ref[pl.ds(near, length), :], got_ref[pl.ds(far, length), :])

    for k in range(KB):
        coupled_v[pl.ds(k * BLK, BLK), :] = solved_at(blocks_ref[0, k] * BLK, BLK)
    rows_v[...] = solved_at(row * block_r, block_r)
    copies = [pltpu.make_async_copy(rows_v, rows_hbm, sems.at[tiles])]
    copies[0].start()
    for group, inner_ref, outer_ref in zip(groups, inner_refs, outer_refs):
        term = jnp.dot(inner_ref[...], coupled_v[...], preferred_element_type=jnp.float32)
        for n, i in enumerate(group):
            here = slice(n * TILE, (n + 1) * TILE)
            tile = outer_ref[here, :] - term[here, :]
            at = lax.broadcasted_iota(jnp.int32, tile.shape, 0) + i * TILE
            rows = pl.ds(i * TILE, TILE)
            solved_v[rows, :] = jnp.where(at < size, tile, 0.0).astype(jnp.bfloat16)
            copies.append(pltpu.make_async_copy(
                solved_v.at[rows], leaf_hbm.at[0, rows], sems.at[i]))
            copies[-1].start()
    for copy in copies:
        copy.wait()


def shards(
    rows_n,
    cols_n,
    rhs_leaf,
    rhs_sep,
    leaf_sizes,
    off_blocks,
    linv_leaf,
    uinv_leaf,
    l_off,
    u_off,
    linv_sep,
    uinv_sep,
):
    width, columns = rhs_leaf.shape[1:]
    share = rhs_sep.shape[0]
    sep = share * cols_n
    block_r = sep // rows_n
    assert rows_n == 2 * cols_n and rows_n >= 8
    tiles = width // TILE
    bf16 = jnp.bfloat16
    smem = pl.BlockSpec(memory_space=pltpu.SMEM)
    vmem = pl.BlockSpec(memory_space=pltpu.VMEM)
    any_space = pl.BlockSpec(memory_space=pl.ANY)
    in_vmem = functools.partial(pltpu.with_memory_space_constraint, memory_space=pltpu.VMEM)
    in_smem = functools.partial(pltpu.with_memory_space_constraint, memory_space=pltpu.SMEM)
    in_hbm = functools.partial(pltpu.with_memory_space_constraint, memory_space=pltpu.HBM)

    forward, keep, send, size, blocks, *pieces = pl.pallas_call(
        functools.partial(forward_kernel, cols_n),
        out_shape=[
            pltpu.VMEM((width, columns), bf16),
            pltpu.VMEM((sep // 2, columns), bf16),
            pltpu.VMEM((sep // 2, columns), bf16),
            pltpu.SMEM((1,), jnp.int32),
            pltpu.SMEM((1, KB), jnp.int32),
        ] + [pltpu.VMEM((block_r, block_r), bf16)] * 2,
        in_specs=[smem] + [any_space] * 5,
        out_specs=[vmem, vmem, vmem, smem, smem, vmem, vmem],
        scratch_shapes=[
            pltpu.VMEM((width, columns), bf16),
            pltpu.VMEM((width, width), bf16),
            pltpu.VMEM((KB * BLK, width), bf16),
            pltpu.VMEM((KB * BLK, columns), jnp.float32),
            pltpu.SemaphoreType.DMA((2 * tiles + 2,)),
        ],
        compiler_params=pltpu.CompilerParams(vmem_limit_bytes=24 * 2**20),
        cost_estimate=pl.CostEstimate(
            flops=900_000_000, bytes_accessed=8_000_000, transcendentals=0),
        name="leaf_forward",
    )(
        leaf_sizes, in_hbm(off_blocks), in_hbm(rhs_leaf), in_hbm(linv_leaf),
        in_hbm(l_off), in_hbm(uinv_sep),
    )
    tied = lax.optimization_barrier
    groups = [[0], [1]] + [[2 + j, tiles - 1 - j] for j in range((tiles - 2) // 2)]
    inner, outer, moved = [], [], []

    def move(p):
        wide = cols_n // 2
        pairs = []
        for r in range(rows_n):
            for c in range(cols_n):
                top, zl, y = r // 2 // wide, r // 2 % wide, r % 2
                to_r = (top * wide + c % wide) * 2 + ((c // wide) ^ p)
                pairs.append((r * cols_n + c, to_r * cols_n + y * wide + zl))
        return lax.ppermute(pieces[p], ("row", "col"), pairs)

    due = []

    def send_move(x):
        p = len(moved)
        x, piece = tied((x, pieces[p]))
        pieces[p] = piece
        moved.append(move(p))
        due.append(p)
        return x

    def swap_beside(x, axis, count, bit):
        return beside(x, lambda part: [swap(part, axis, count, bit)])[0]

    def beside(x, exchange):
        if len(inner) == len(groups):
            return exchange(x)
        group = groups[len(inner)]
        x, factor = tied((x, uinv_leaf))
        while due:
            p = due.pop()
            factor, moved[p] = tied((factor, moved[p]))
        got = exchange(x)
        length = len(group) * TILE
        ahead = pl.pallas_call(
            functools.partial(ahead_kernel, group),
            out_shape=[
                pltpu.VMEM((length, u_off.shape[2]), bf16),
                pltpu.VMEM((length, columns), jnp.float32),
            ],
            in_specs=[smem, vmem, vmem, any_space],
            out_specs=[vmem, vmem],
            scratch_shapes=[
                pltpu.VMEM((width, u_off.shape[2] + columns), bf16),
                pltpu.VMEM((length, width), bf16),
                pltpu.SemaphoreType.DMA((len(group),)),
            ],
            compiler_params=pltpu.CompilerParams(vmem_limit_bytes=16 * 2**20),
            cost_estimate=pl.CostEstimate(
                flops=600_000_000, bytes_accessed=1_000_000, transcendentals=0),
            name="leaf_ahead",
        )(in_smem(size), in_vmem(u_off), in_vmem(forward), in_hbm(factor))
        *got, first, second = tied((*got, *ahead))
        inner.append(first)
        outer.append(second)
        return got

    def three(part):
        return [swap(part, "row", rows_n, bits) for bits in (1, 2, 3)]

    def corner(part):
        return [
            swap_both(part, rows_n, cols_n, 0, cols_n // 2),
            swap_both(part, rows_n, cols_n, rows_n // 2, 0),
            swap_both(part, rows_n, cols_n, rows_n // 2, cols_n // 2),
        ]

    def four_sum(x, near, far, both):
        near = x.astype(jnp.float32) + near.astype(jnp.float32)
        return (near + (far.astype(jnp.float32) + both.astype(jnp.float32))).astype(bf16)

    bit = 1
    while bit < cols_n:
        if bit == 2:
            send = send_move(send)
        got = (swap if bit <= 2 else swap_beside)(send, "col", cols_n, bit)
        bit *= 2
        if bit < cols_n:
            part = keep.shape[0] // 2
            send = add(keep[part:], got[part:])
            keep = add(keep[:part], got[:part])
        else:
            keep = add(keep, got)
    keep = four_sum(keep, *beside(keep, lambda part: three(send_move(part))))
    bit = 4
    while bit < rows_n:
        keep = add(keep, swap_beside(keep, "row", rows_n, bit))
        bit *= 2
    sep_rhs = (rhs_sep.astype(jnp.float32) - keep.astype(jnp.float32)).astype(bf16)

    own = jnp.dot(linv_sep, sep_rhs, preferred_element_type=jnp.float32).astype(bf16)
    bit = 1
    while bit < cols_n // 2:
        own = add(own, swap(own, "col", cols_n, bit))
        bit *= 2
    near, far, both = beside(own, corner)
    own, got = add(own, near), add(far, both)
    own = pl.pallas_call(
        functools.partial(separator_kernel, rows_n),
        out_shape=pltpu.VMEM((block_r, columns), bf16),
        in_specs=[vmem] * 4,
        out_specs=vmem,
        compiler_params=pltpu.CompilerParams(vmem_limit_bytes=8 * 2**20),
        name="separator_backward",
    )(in_vmem(own), in_vmem(got), *map(in_vmem, moved))
    own = four_sum(own, *beside(own, three))
    bit = 4
    while bit < rows_n // 2:
        own = add(own, swap(own, "row", rows_n, bit))
        bit *= 2
    near, far, both = beside(own, corner)
    own = jnp.concatenate([own, far, near, both], 0)
    bit = cols_n // 4
    while bit >= 1:
        got = (swap if bit == 1 else swap_beside)(own, "col", cols_n, bit)
        if bit > 1:
            own = jnp.concatenate([own, got], 0)
        bit //= 2

    solved_leaf, solved_rows = pl.pallas_call(
        functools.partial(backward_kernel, cols_n, groups),
        out_shape=[
            jax.ShapeDtypeStruct((1, width, columns), bf16),
            jax.ShapeDtypeStruct((block_r, columns), bf16),
        ],
        in_specs=[smem, smem] + [vmem] * (2 + 2 * len(groups)),
        out_specs=[any_space, any_space],
        scratch_shapes=[
            pltpu.VMEM((KB * BLK, columns), bf16),
            pltpu.VMEM((width, columns), bf16),
            pltpu.VMEM((block_r, columns), bf16),
            pltpu.SemaphoreType.DMA((tiles + 1,)),
        ],
        compiler_params=pltpu.CompilerParams(vmem_limit_bytes=16 * 2**20),
        cost_estimate=pl.CostEstimate(
            flops=270_000_000, bytes_accessed=4_000_000, transcendentals=0),
        name="leaf_backward",
    )(
        in_smem(size), in_smem(blocks), in_vmem(own), in_vmem(got),
        *map(in_vmem, inner), *map(in_vmem, outer),
    )
    return (solved_leaf, solved_rows)


def solution(mesh):
    placed = (
        P(("row", "col"), None, None),
        P("col", None),
        P(("row", "col")),
        P(("row", "col"), None),
        P(("row", "col"), None, None),
        P(("row", "col"), None, None),
        P(("row", "col"), None, None),
        P(("row", "col"), None, None),
        P("row", "col"),
        P("row", "col"),
    )
    return jax.shard_map(
        functools.partial(shards, mesh.shape["row"], mesh.shape["col"]),
        mesh=mesh,
        in_specs=placed,
        out_specs=(P(("row", "col"), None, None), P("row", None)),
        check_vma=False,
    )
```
